128 devices in a mesh: dp: 16 (over y, x), seq: 8 (over z, core).
Axes of the slice: x: 4, y: 4, z: 4, core: 2. Of those that a mesh axis runs over, the one named last changes fastest.
Arguments:
- inputs: bfloat16 [32, 1024, 1024], P('dp', 'seq'), may hold values from -6 to 6
- cotangent: bfloat16 [32, 1024, 1024], P('dp', 'seq'), may hold values from -8 to 8
- norm_gains: float32 [2, 1024], P(None, ('dp', 'seq')), may hold values from 0.5 to 1.5
- conv_taps: float32 [3, 1024], P(None, ('dp', 'seq')), may hold values from -3 to 3
- w_in: float32 [1024, 3072], P(('dp', 'seq')), may hold values from -0.1875 to 0.1875
- w_out: float32 [1024, 1024], P(('dp', 'seq')), may hold values from -0.1875 to 0.1875
- w_gate: float32 [1024, 4608], P(('dp', 'seq')), may hold values from -0.1875 to 0.1875
- w_up: float32 [1024, 4608], P(('dp', 'seq')), may hold values from -0.1875 to 0.1875
- w_down: float32 [4608, 1024], P(('dp', 'seq')), may hold values from -0.09375 to 0.09375
- first_gains: float32 [2, 1024], P(None, ('dp', 'seq')), may hold values from -256 to 256
- first_taps: float32 [3, 1024], P(None, ('dp', 'seq')), may hold values from -128 to 128
- first_in: float32 [1024, 3072], P(('dp', 'seq')), may hold values from -128 to 128
- first_out: float32 [1024, 1024], P(('dp', 'seq')), may hold values from -128 to 128
- first_gate: float32 [1024, 4608], P(('dp', 'seq')), may hold values from -64 to 64
- first_up: float32 [1024, 4608], P(('dp', 'seq')), may hold values from -64 to 64
- first_down: float32 [4608, 1024], P(('dp', 'seq')), may hold values from -64 to 64
- second_gains: float32 [2, 1024], P(None, ('dp', 'seq')), may hold values from 6881.28 to 27525.12
- second_taps: float32 [3, 1024], P(None, ('dp', 'seq')), may hold values from 1723.5968 to 6881.28
- second_in: float32 [1024, 3072], P(('dp', 'seq')), may hold values from 1723.5968 to 6881.28
- second_out: float32 [1024, 1024], P(('dp', 'seq')), may hold values from 1723.5968 to 6881.28
- second_gate: float32 [1024, 4608], P(('dp', 'seq')), may hold values from 432.5376 to 1723.5968
- second_up: float32 [1024, 4608], P(('dp', 'seq')), may hold values from 432.5376 to 1723.5968
- second_down: float32 [4608, 1024], P(('dp', 'seq')), may hold values from 432.5376 to 1723.5968
Outputs:
- output: bfloat16 [32, 1024, 1024], P('dp', 'seq')
- input_grad: float32 [32, 1024, 1024], P('dp', 'seq')
- new_gains: float32 [2, 1024], P(None, ('dp', 'seq'))
- new_taps: float32 [3, 1024], P(None, ('dp', 'seq'))
- new_in: float32 [1024, 3072], P(('dp', 'seq'))
- new_out: float32 [1024, 1024], P(('dp', 'seq'))
- new_gate: float32 [1024, 4608], P(('dp', 'seq'))
- new_up: float32 [1024, 4608], P(('dp', 'seq'))
- new_down: float32 [4608, 1024], P(('dp', 'seq'))
- new_first_gains: float32 [2, 1024], P(None, ('dp', 'seq'))
- new_first_taps: float32 [3, 1024], P(None, ('dp', 'seq'))
- new_first_in: float32 [1024, 3072], P(('dp', 'seq'))
- new_first_out: float32 [1024, 1024], P(('dp', 'seq'))
- new_first_gate: float32 [1024, 4608], P(('dp', 'seq'))
- new_first_up: float32 [1024, 4608], P(('dp', 'seq'))
- new_first_down: float32 [4608, 1024], P(('dp', 'seq'))
- new_second_gains: float32 [2, 1024], P(None, ('dp', 'seq'))
- new_second_taps: float32 [3, 1024], P(None, ('dp', 'seq'))
- new_second_in: float32 [1024, 3072], P(('dp', 'seq'))
- new_second_out: float32 [1024, 1024], P(('dp', 'seq'))
- new_second_gate: float32 [1024, 4608], P(('dp', 'seq'))
- new_second_up: float32 [1024, 4608], P(('dp', 'seq'))
- new_second_down: float32 [4608, 1024], P(('dp', 'seq'))
The draws below stay inside these ranges and needn't reach their ends.
All inputs are finite; a program needn't handle non-finite values.
Results may differ from the reference program's by a relative error of at most 0.019.
Values may be sent and summed in bfloat16 or wider, within the bound.
A program may use at most 256 MiB of HBM per device.

```python
import math
import jax
import jax.numpy as jnp
from jax import lax

D = 1024
FF = 4608
LENGTH = 1024
STEP = 5
SEQS = 32
TOKENS = 32768


def with_spikes(entries, stream_key, source, target, blocks, factor):
    owner, partner = [(jnp.arange(entries.shape[dim]) // (entries.shape[dim] // blocks)).reshape([-1 if axis == dim else 1 for axis in range(entries.ndim)]) for dim in (source, target)]
    chosen = jax.random.permutation(stream_key, blocks)[partner]
    strong = (owner == chosen) | (owner == (partner + blocks // 2) % blocks)
    return jnp.where(strong, factor * entries, entries)


def block_scale(key, shape, shards, least, largest):
    loudness = 1.0
    for axis_at, blocks in shards:
        draws = jax.random.uniform(jax.random.fold_in(jax.random.fold_in(key, 6), axis_at), (blocks,), jnp.float32, least / len(shards), largest / len(shards))
        loudness = loudness * jnp.repeat(jnp.exp(draws), shape[axis_at] // blocks).reshape((-1,) + (1,) * (len(shape) - 1 - axis_at))
    return loudness


def scatter_about(key, dims, spread, limit, cuts=(), held_as=jnp.bfloat16):
    entries = jax.random.normal(key, dims, jnp.float32) * spread
    if len(cuts) > 0:
        entries = block_scale(key, dims, cuts, -0.22, 0.18) * entries
    return jnp.clip(entries, min=-limit, max=limit).astype(held_as)


def gaussian_with(key, dims, width, bound, split, heavy, dtype=jnp.bfloat16):
    drawn = width * jax.random.normal(key, dims, jnp.float32)
    if split:
        drawn = drawn * block_scale(key, dims, split, -0.22, 0.18)
    return jnp.clip(with_spikes(drawn, jax.random.fold_in(key, 3), *heavy), -bound, bound).astype(dtype)


def setup_inputs(seed: int = 0) -> dict:
    keys = jax.random.split(jax.random.key(seed), 24)
    inputs = scatter_about(keys[0], (SEQS, LENGTH, D), 1.0, 6.0, ((0, 16), (1, 8)))
    cotangent = gaussian_with(keys[1], (SEQS, LENGTH, D), 1.0, 8.0, ((0, 16), (1, 8)), (0, 2, 16, 2.0))
    norm_gains = jnp.clip(1.0 + 0.1 * jax.random.normal(keys[2], (2, D), jnp.float32), 0.5, 1.5)
    conv_taps = scatter_about(keys[3], (3, D), 0.6, 3.0, ((1, 128),), jnp.float32)
    w_in = scatter_about(keys[4], (D, 3 * D), D ** -0.5, 0.1875, ((0, 128),), jnp.float32)
    w_out = scatter_about(keys[5], (D, D), D ** -0.5, 0.1875, ((0, 128),), jnp.float32)
    w_gate = scatter_about(keys[6], (D, FF), D ** -0.5, 0.1875, ((0, 128),), jnp.float32)
    w_up = scatter_about(keys[7], (D, FF), D ** -0.5, 0.1875, ((0, 128),), jnp.float32)
    w_down = scatter_about(keys[8], (FF, D), FF ** -0.5, 0.09375, ((0, 128),), jnp.float32)
    first_gains = scatter_about(keys[9], (2, D), (0.222 * TOKENS ** 0.5), 256.0, ((1, 128),), jnp.float32)
    first_taps = scatter_about(keys[10], (3, D), (0.111 * TOKENS ** 0.5), 128.0, ((1, 128),), jnp.float32)
    first_in = scatter_about(keys[11], (D, 3 * D), (0.111 * TOKENS ** 0.5), 128.0, ((0, 128),), jnp.float32)
    first_out = scatter_about(keys[12], (D, D), (0.111 * TOKENS ** 0.5), 128.0, ((0, 128),), jnp.float32)
    first_gate = scatter_about(keys[13], (D, FF), (0.055 * TOKENS ** 0.5), 64.0, ((0, 128),), jnp.float32)
    first_up = scatter_about(keys[14], (D, FF), (0.055 * TOKENS ** 0.5), 64.0, ((0, 128),), jnp.float32)
    first_down = scatter_about(keys[15], (FF, D), (0.055 * TOKENS ** 0.5), 64.0, ((0, 128),), jnp.float32)
    second_gains = jnp.clip(jnp.exp(math.log(27525.12) - 1.3862944 * jax.random.uniform(keys[16], (2, D), jnp.float32) ** block_scale(keys[16], (2, D), ((1, 128),), -0.2, 0.2)), 6881.28, 27525.12)
    second_taps = jnp.clip(jnp.exp(math.log(6881.28) - 1.3843914 * jax.random.uniform(keys[17], (3, D), jnp.float32) ** block_scale(keys[17], (3, D), ((1, 128),), -0.2, 0.2)), 1723.5968, 6881.28)
    second_in = jnp.clip(jnp.exp(math.log(6881.28) - 1.3843914 * jax.random.uniform(keys[18], (D, 3 * D), jnp.float32) ** block_scale(keys[18], (D, 3 * D), ((0, 128),), -0.2, 0.2)), 1723.5968, 6881.28)
    second_out = jnp.clip(jnp.exp(math.log(6881.28) - 1.3843914 * jax.random.uniform(keys[19], (D, D), jnp.float32) ** block_scale(keys[19], (D, D), ((0, 128),), -0.2, 0.2)), 1723.5968, 6881.28)
    second_gate = jnp.clip(jnp.exp(math.log(1723.5968) - 1.3824993 * jax.random.uniform(keys[20], (D, FF), jnp.float32) ** block_scale(keys[20], (D, FF), ((0, 128),), -0.2, 0.2)), 432.5376, 1723.5968)
    second_up = jnp.clip(jnp.exp(math.log(1723.5968) - 1.3824993 * jax.random.uniform(keys[21], (D, FF), jnp.float32) ** block_scale(keys[21], (D, FF), ((0, 128),), -0.2, 0.2)), 432.5376, 1723.5968)
    second_down = jnp.clip(jnp.exp(math.log(1723.5968) - 1.3824993 * jax.random.uniform(keys[22], (FF, D), jnp.float32) ** block_scale(keys[22], (FF, D), ((0, 128),), -0.2, 0.2)), 432.5376, 1723.5968)
    return {"inputs": inputs, "cotangent": cotangent, "norm_gains": norm_gains, "conv_taps": conv_taps, "w_in": w_in, "w_out": w_out, "w_gate": w_gate, "w_up": w_up, "w_down": w_down, "first_gains": first_gains, "first_taps": first_taps, "first_in": first_in, "first_out": first_out, "first_gate": first_gate, "first_up": first_up, "first_down": first_down, "second_gains": second_gains, "second_taps": second_taps, "second_in": second_in, "second_out": second_out, "second_gate": second_gate, "second_up": second_up, "second_down": second_down}


@jax.custom_vjp
def low(v):
    return lax.optimization_barrier(v.astype(jnp.bfloat16)).astype(jnp.float32)

@jax.custom_vjp
def reduced_return(v):
    return v

def low_keep(v):
    return (low(v), None)

def low_pass(kept, grad):
    return (grad,)

def back_keep(v):
    return (v, None)

def back_low(kept, grad):
    return (low(grad),)
low.defvjp(low_keep, low_pass)
reduced_return.defvjp(back_keep, back_low)
epsilon_norm = 1e-05
beta_one = 0.9
beta_two = 0.95
epsilon_adam = 1e-08
rate_matrix = 0.02
rate_small = 0.3
weight_decay = 0.1

def gated_product(form, left, right):
    return jnp.einsum(form, left, right, precision=lax.Precision.HIGHEST)

def normalize(values):
    return values * lax.rsqrt(lax.optimization_barrier(jnp.mean(values * values, axis=-1, keepdims=True)) + epsilon_norm)

def block_forward(inputs, norm_gains, conv_taps, w_in, w_out, w_gate, w_up, w_down):
    gains_low = low(norm_gains)
    taps_low = low(conv_taps)
    input_weight_reduced = low(w_in)
    output_weight_reduced = low(w_out)
    gate_weight_reduced = low(w_gate)
    up_weight_reduced = low(w_up)
    down_weight_reduced = low(w_down)
    group_size = math.gcd(SEQS, max(1, 4096 // LENGTH))

    def group_forward(block_in):
        normalized_input = low(normalize(block_in) * gains_low[0])
        projected_rows = reduced_return(gated_product('hyf,fi->hyi', normalized_input, input_weight_reduced))
        b_part = projected_rows[..., :D]
        c_part = projected_rows[..., D:2 * D]
        x_part = projected_rows[..., 2 * D:]
        gated = b_part * x_part
        padded = jnp.pad(gated, ((0, 0), (2, 0), (0, 0)))
        convolved = taps_low[0] * padded[:, :-2] + taps_low[1] * padded[:, 1:-1] + taps_low[2] * padded[:, 2:]
        mixer_input_rows = low(c_part * convolved)
        mixer_output_rows = reduced_return(gated_product('hyf,fi->hyi', mixer_input_rows, output_weight_reduced))
        hidden_state = block_in + mixer_output_rows
        normalized_second = low(normalize(hidden_state) * gains_low[1])
        gate_projection_value = reduced_return(gated_product('wzj,jg->wzg', normalized_second, gate_weight_reduced))
        up_projection_value = reduced_return(gated_product('wzj,jg->wzg', normalized_second, up_weight_reduced))
        activated_hidden = low(jax.nn.silu(gate_projection_value) * up_projection_value)
        return hidden_state + reduced_return(gated_product('omb,bu->omu', activated_hidden, down_weight_reduced))
    blocks = inputs.reshape(SEQS // group_size, group_size, LENGTH, D)
    return lax.map(jax.checkpoint(group_forward), blocks).reshape(SEQS, LENGTH, D)

def adamw(weight, grad, first, second, rate, decay):
    first_new = beta_one * first + (1.0 - beta_one) * grad
    second_new = beta_two * second + (1.0 - beta_two) * grad * grad
    first_hat = first_new / (1.0 - beta_one ** STEP)
    second_hat = second_new / (1.0 - beta_two ** STEP)
    weight_new = weight - rate * (first_hat / (jnp.sqrt(second_hat) + epsilon_adam) + decay * weight)
    return (weight_new, first_new, second_new)

def reference(inputs, cotangent, norm_gains, conv_taps, w_in, w_out, w_gate, w_up, w_down, first_gains, first_taps, first_in, first_out, first_gate, first_up, first_down, second_gains, second_taps, second_in, second_out, second_gate, second_up, second_down):
    result, pullback = jax.vjp(block_forward, inputs.astype(jnp.float32), norm_gains, conv_taps, w_in, w_out, w_gate, w_up, w_down)
    grad_input, grad_gains, grad_taps, grad_in, grad_out, gate_weight_gradient, up_weight_gradient, down_weight_gradient = pullback(cotangent.astype(jnp.float32))
    new_gains, new_first_gains, new_second_gains = adamw(norm_gains, grad_gains, first_gains, second_gains, rate_small, 0.0)
    new_taps, new_first_taps, new_second_taps = adamw(conv_taps, grad_taps, first_taps, second_taps, rate_small, 0.0)
    new_in, new_first_in, new_second_in = adamw(w_in, grad_in, first_in, second_in, rate_matrix, weight_decay)
    new_out, new_first_out, new_second_out = adamw(w_out, grad_out, first_out, second_out, rate_matrix, weight_decay)
    new_gate, new_first_gate, new_second_gate = adamw(w_gate, gate_weight_gradient, first_gate, second_gate, rate_matrix, weight_decay)
    new_up, new_first_up, new_second_up = adamw(w_up, up_weight_gradient, first_up, second_up, rate_matrix, weight_decay)
    new_down, new_first_down, new_second_down = adamw(w_down, down_weight_gradient, first_down, second_down, rate_matrix, weight_decay)
    return (result.astype(jnp.bfloat16), grad_input, new_gains, new_taps, new_in, new_out, new_gate, new_up, new_down, new_first_gains, new_first_taps, new_first_in, new_first_out, new_first_gate, new_first_up, new_first_down, new_second_gains, new_second_taps, new_second_in, new_second_out, new_second_gate, new_second_up, new_second_down)
```

```python
import functools

import jax
import jax.numpy as jnp
from jax import lax
from jax.experimental import pallas as pl
from jax.experimental.pallas import tpu as pltpu
from jax.sharding import PartitionSpec as P

D = 1024
STEP = 5

epsilon_norm = 1e-05
beta_one = 0.9
beta_two = 0.95
epsilon_adam = 1e-08
rate_matrix = 0.02
rate_small = 0.3
weight_decay = 0.1

MESH = pl.DeviceIdType.MESH
BF = jnp.bfloat16
F32 = jnp.float32
SIDE = 4
PEERS = 8
OWN = 36
PAD = 48
SLICE = 576
WIDE = 512
VMEM_BYTES = 52 * 2**20


def place():
    dp, seq = lax.axis_index("dp"), lax.axis_index("seq")
    return lax.rem(dp, SIDE), lax.div(dp, SIDE), lax.div(seq, 2), lax.rem(seq, 2)


def wrap(value, size=SIDE):
    return lax.rem(value + size, size)


def at(x, y, z, core):
    return (y * SIDE + x, z * 2 + core)


class Copies:
    def __init__(self, send, recv):
        self.send, self.recv, self.started = send, recv, []

    def start(self, source, target, device):
        index = len(self.started)
        copy = pltpu.make_async_remote_copy(
            src_ref=source,
            dst_ref=target,
            send_sem=self.send.at[index],
            recv_sem=self.recv.at[index],
            device_id=device,
            device_id_type=MESH,
        )
        copy.start()
        self.started.append(copy)
        return copy

    def drain(self):
        for copy in self.started:
            copy.wait_send()


def greet(devices):
    barrier = pltpu.get_barrier_semaphore()
    for device in devices:
        pl.semaphore_signal(barrier, inc=1, device_id=device, device_id_type=MESH)
    pl.semaphore_wait(barrier, len(devices))


def seq_peers(x, y, z, core):
    seq = z * 2 + core
    return [(y * SIDE + x, wrap(seq + k, PEERS)) for k in range(1, PEERS)]


class RingGather:
    def __init__(self, copies, me, to, block, low, high):
        self.copies, self.me, self.to = copies, me, to
        self.block, self.low, self.high = block, low, high

    def first(self, source=None):
        source = self.block(self.me) if source is None else source
        self.a = self.copies.start(source, self.block(self.me), self.to(wrap(self.me + 1)))
        self.b = self.copies.start(source, self.block(self.me), self.to(wrap(self.me - 1)))

    def second(self):
        below, above = wrap(self.me - 1), wrap(self.me + 1)
        self.a.wait_recv()
        self.e = self.copies.start(self.low(below), self.low(below), self.to(above))
        self.b.wait_recv()
        self.f = self.copies.start(self.high(above), self.high(above), self.to(below))

    def finish(self):
        self.e.wait_recv()
        self.f.wait_recv()


class RingReduce:
    def __init__(self, copies, me, to, block, low, high, landing):
        self.copies, self.me, self.to = copies, me, to
        self.block, self.low, self.high = block, low, high
        self.low_in, self.high_in, self.plus_in, self.minus_in = landing

    def first(self):
        far, below, above = wrap(self.me + 2), wrap(self.me - 1), wrap(self.me + 1)
        self.e = self.copies.start(self.low(far), self.low_in, self.to(above))
        self.f = self.copies.start(self.high(far), self.high_in, self.to(below))

    def second(self):
        below, above = wrap(self.me - 1), wrap(self.me + 1)
        self.e.wait_recv()
        accumulate(self.low(above), self.low(above), self.low_in)
        self.g = self.copies.start(self.block(above), self.plus_in, self.to(above))
        self.f.wait_recv()
        accumulate(self.high(below), self.high(below), self.high_in)
        self.h = self.copies.start(self.block(below), self.minus_in, self.to(below))

    def finish(self, target=None):
        own = self.block(self.me)
        self.g.wait_recv()
        self.h.wait_recv()
        accumulate(own if target is None else target, own, self.plus_in, self.minus_in)


def accumulate(target, *sources):
    shape = target.shape
    if len(shape) > 2:
        for index in range(shape[0]):
            accumulate(target.at[index], *[source.at[index] for source in sources])
        return
    step = 16

    @pl.loop(0, shape[0] // step)
    def _(i):
        rows = pl.ds(pl.multiple_of(i * step, step), step)
        total = sources[0][rows, :].astype(F32)
        for source in sources[1:]:
            total = total + source[rows, :].astype(F32)
        target[rows, :] = total.astype(target.dtype)


def any_spec():
    return pl.BlockSpec(memory_space=pl.ANY)


def vmem_spec():
    return pl.BlockSpec(memory_space=pltpu.VMEM)


def call(kernel, name, ident, outs, ins, scratch, copies, specs_in, specs_out):
    return pl.pallas_call(
        kernel,
        out_shape=outs,
        in_specs=specs_in,
        out_specs=specs_out,
        scratch_shapes=list(scratch)
        + [pltpu.SemaphoreType.DMA((copies,)), pltpu.SemaphoreType.DMA((copies,))],
        compiler_params=pltpu.CompilerParams(
            collective_id=ident, has_side_effects=True, vmem_limit_bytes=VMEM_BYTES
        ),
        name=name,
    )(*ins)


def columns_of(seq, dp_count=16):
    return [(288 * d + OWN * seq, 36 * d) for d in range(dp_count)]


def gather_kernel(
    w_in, w_out, w_gate, w_up, w_down, small, edge, grad,
    mix, feed, down, small_all, edge_in, grad_all,
    mix_send, feed_send, mix_got, feed_got, small_got, mix_block, feed_block, down_block, down_wide,
    small_send, local_sem, send, recv,
):
    x, y, z, core = place()
    seq = z * 2 + core
    copies = Copies(send, recv)
    peers = seq_peers(x, y, z, core)
    across = [at(wrap(x + k), y, z, core) for k in range(1, SIDE)]
    along = [at(x, wrap(y + k), z, core) for k in range(1, SIDE)]
    greet(peers + across + along)

    partner = at(x, y, z, 1 - core)
    ring = RingGather(
        copies,
        z,
        lambda i: at(x, y, i, core),
        lambda i: grad_all.at[i * 2 + core],
        lambda i: grad_all.at[i * 2 + core, pl.ds(0, 128)],
        lambda i: grad_all.at[i * 2 + core, pl.ds(128, 128)],
    )
    own_grad = pltpu.make_async_copy(grad, grad_all.at[seq], local_sem.at[0])
    own_grad.start()

    small_copies = [
        copies.start(small, small_got.at[seq], peer) for peer in peers
    ]
    edge_copy = copies.start(edge, edge_in, (y * SIDE + x, wrap(seq + 1, PEERS)))
    small_got[seq] = small[...]
    for half in range(2):
        parts = [w_in[:, 1024 * k + 512 * half : 1024 * k + 512 * half + 512] for k in range(3)]
        parts.append(w_out[:, 512 * half : 512 * half + 512])
        upper = jnp.concatenate(parts[:2], axis=1)
        lower = jnp.concatenate(parts[2:], axis=1)
        mix_send[half] = jnp.concatenate([upper, lower], axis=0).astype(BF)
    mix_copies = []
    for k, peer in enumerate(peers):
        other = wrap(seq + k + 1, PEERS)
        mix_copies.append(copies.start(mix_send.at[lax.rem(other, 2)], mix_got.at[seq], peer))
    mix_got[seq] = mix_send[core]
    for s in range(PEERS):
        gate = jnp.concatenate([w_gate[:, a : a + OWN] for a, _ in columns_of(s)], axis=1)
        up = jnp.concatenate([w_up[:, a : a + OWN] for a, _ in columns_of(s)], axis=1)
        tail = jnp.concatenate([gate[:, WIDE:], up[:, WIDE:]], axis=1)
        upper = jnp.concatenate([gate[:, :WIDE], up[:, :128]], axis=1)
        lower = jnp.concatenate([up[:, 128:WIDE], tail, jnp.zeros((8, 128), F32)], axis=1)
        feed_send[s] = jnp.concatenate([upper, lower], axis=0).astype(BF)
    feed_copies = []
    for k, peer in enumerate(peers):
        other = wrap(seq + k + 1, PEERS)
        feed_copies.append(copies.start(feed_send.at[other], feed_got.at[seq], peer))
    feed_got[seq] = feed_send[seq]
    ring.first(grad)
    own_to_partner = copies.start(grad, grad_all.at[seq], partner)
    down_wide[...] = jnp.zeros_like(down_wide)
    down_wide[0:OWN, :] = w_down[...]
    down_block[...] = down_wide[...].astype(BF)

    for copy in small_copies:
        copy.wait_recv()
    small_send[...] = functools.reduce(lambda a, b: a + b, [small_got[s] for s in range(PEERS)])
    small_x = [copies.start(small_send, small_all.at[y, x], device) for device in across]
    own_small = pltpu.make_async_copy(small_send, small_all.at[y, x], local_sem.at[1])
    own_small.start()

    for copy in mix_copies:
        copy.wait_recv()
    for k in range(4):
        a, b = mix_got[2 * k].astype(F32), mix_got[2 * k + 1].astype(F32)
        rows = slice(16 * k, 16 * k + 16)
        mix_block[rows, :1024] = jnp.concatenate([a[:8], b[:8]], axis=0).astype(BF)
        mix_block[rows, 1024:] = jnp.concatenate([a[8:], b[8:]], axis=0).astype(BF)

    def plane(target, halves):
        row_x = RingGather(
            copies, x, lambda i: at(i, y, z, core),
            lambda i: halves(target.at[y, i], 0, None),
            lambda i: halves(target.at[y, i], 0, 0),
            lambda i: halves(target.at[y, i], 0, 1),
        )
        row_y = RingGather(
            copies, y, lambda i: at(x, i, z, core),
            lambda i: halves(target.at[i, x], 1, None),
            lambda i: halves(target.at[i, x], 1, 0),
            lambda i: halves(target.at[i, x], 1, 1),
        )
        all_y = RingGather(
            copies, y, lambda i: at(x, i, z, core),
            lambda i: halves(target.at[i], 0, None),
            lambda i: halves(target.at[i, pl.ds(0, 2)], 0, None),
            lambda i: halves(target.at[i, pl.ds(2, 2)], 0, None),
        )
        all_x = RingGather(
            copies, x, lambda i: at(i, y, z, core),
            lambda i: halves(target.at[:, i], 1, None),
            lambda i: halves(target.at[pl.ds(0, 2), i], 1, None),
            lambda i: halves(target.at[pl.ds(2, 2), i], 1, None),
        )
        return row_x, row_y, all_y, all_x

    def by_rows(ref, which, part):
        start, size = (32 * which, 32) if part is None else (32 * which + 16 * part, 16)
        lead = [slice(None)] * (len(ref.shape) - 2)
        return ref.at[(*lead, pl.ds(start, size), slice(None))]

    def by_columns(ref, which, part):
        start, size = (512 * which, 512) if part is None else (512 * which + 256 * part, 256)
        lead = [slice(None)] * (len(ref.shape) - 2)
        return ref.at[(*lead, slice(None), pl.ds(start, size))]

    plans = []
    for target, block, halves, index in (
        (mix.at[core], mix_block, by_rows, 2),
        (feed, feed_block, by_rows, 3),
        (down, down_block, by_columns, 4),
    ):
        if index == 3:
            for copy in feed_copies:
                copy.wait_recv()
            for k in range(4):
                a, b = feed_got[2 * k].astype(F32), feed_got[2 * k + 1].astype(F32)
                rows = slice(16 * k, 16 * k + 16)
                feed_block[rows, :640] = jnp.concatenate([a[:8], b[:8]], axis=0).astype(BF)
                feed_block[rows, 640:] = jnp.concatenate([a[8:, :512], b[8:, :512]], axis=0).astype(BF)
        own = pltpu.make_async_copy(block, target.at[y, x], local_sem.at[index])
        own.start()
        plan = plane(target, halves)
        plan[0].first(halves(block, 0, None))
        plan[1].first(halves(block, 1, None))
        plans.append((plan, own))
    ring.second()
    to_partner = [copies.start(grad_all.at[wrap(z - 1) * 2 + core], grad_all.at[wrap(z - 1) * 2 + core], partner)]
    to_partner.append(copies.start(grad_all.at[wrap(z + 1) * 2 + core], grad_all.at[wrap(z + 1) * 2 + core], partner))
    for plan, _ in plans:
        plan[0].second()
        plan[1].second()
    for copy in small_x:
        copy.wait_recv()
    own_small.wait()
    small_y = [copies.start(small_all.at[y], small_all.at[y], device) for device in along]
    for plan, own in plans:
        own.wait()
        plan[0].finish()
        plan[2].first()
        plan[1].finish()
        plan[3].first()
    for plan, _ in plans:
        plan[2].second()
        plan[3].second()
    mixed = mix.at[core]
    for index, (plan, _) in enumerate(plans):
        plan[2].finish()
        plan[3].finish()
        if index == 0:
            across_core = copies.start(mixed, mixed, partner)
    ring.finish()
    far = wrap(z + 2) * 2 + core
    to_partner.append(copies.start(grad_all.at[far], grad_all.at[far], partner))
    for copy in small_y + to_partner + [edge_copy, own_to_partner, across_core]:
        copy.wait_recv()
    own_grad.wait()
    copies.drain()


def gather(w_in, w_out, w_gate, w_up, w_down, small, edge, grad):
    outs = (
        jax.ShapeDtypeStruct((2, 4, 4, 64, 2048), BF),
        jax.ShapeDtypeStruct((4, 4, 64, 1152), BF),
        jax.ShapeDtypeStruct((4, 4, PAD, 1024), BF),
        jax.ShapeDtypeStruct((4, 4, 8, 128), F32),
        jax.ShapeDtypeStruct((2, 16, 1024), BF),
        jax.ShapeDtypeStruct((PEERS, 256, 1024), BF),
    )
    scratch = [
        pltpu.VMEM((2, 16, 1024), BF),
        pltpu.VMEM((PEERS, 16, 640), BF),
        pltpu.VMEM((PEERS, 16, 1024), BF),
        pltpu.VMEM((PEERS, 16, 640), BF),
        pltpu.VMEM((PEERS, 8, 128), F32),
        pltpu.VMEM((64, 2048), BF),
        pltpu.VMEM((64, 1152), BF),
        pltpu.VMEM((PAD, 1024), BF),
        pltpu.VMEM((PAD, 1024), F32),
        pltpu.VMEM((8, 128), F32),
        pltpu.SemaphoreType.DMA((5,)),
    ]
    return call(
        gather_kernel, "gather", 0, outs,
        (w_in, w_out, w_gate, w_up, w_down, small, edge, grad), scratch, 96,
        [vmem_spec()] * 6 + [any_spec()] * 2, (any_spec(),) * 6,
    )


def exchange_kernel(own, everyone, local_sem, send, recv):
    x, y, z, core = place()
    seq = z * 2 + core
    copies = Copies(send, recv)
    partner = at(x, y, z, 1 - core)
    greet([partner, at(x, y, wrap(z + 1), core), at(x, y, wrap(z - 1), core)])
    ring = RingGather(
        copies, z, lambda i: at(x, y, i, core),
        lambda i: everyone.at[i * 2 + core],
        lambda i: everyone.at[i * 2 + core, pl.ds(0, 128)],
        lambda i: everyone.at[i * 2 + core, pl.ds(128, 128)],
    )
    mine = pltpu.make_async_copy(own, everyone.at[seq], local_sem)
    mine.start()
    ring.first(own)
    passed = [copies.start(own, everyone.at[seq], partner)]
    ring.second()
    for step in (-1, 1):
        chunk = everyone.at[wrap(z + step) * 2 + core]
        passed.append(copies.start(chunk, chunk, partner))
    ring.finish()
    chunk = everyone.at[wrap(z + 2) * 2 + core]
    passed.append(copies.start(chunk, chunk, partner))
    for copy in passed:
        copy.wait_recv()
    mine.wait()
    copies.drain()


def exchange(own):
    return call(
        exchange_kernel, "exchange", 1,
        jax.ShapeDtypeStruct((PEERS, 256, 1024), BF), (own,),
        [pltpu.SemaphoreType.DMA], 8, [any_spec()], any_spec(),
    )


def combine_kernel(count, parts, sums, held, landing, low_in, high_in, plus_in, minus_in, send, recv):
    x, y, z, core = place()
    copies = Copies(send, recv)
    partner = at(x, y, z, 1 - core)
    greet([partner, at(x, y, wrap(z + 1), core), at(x, y, wrap(z - 1), core)])
    order = [wrap(z + 2), wrap(z + 1), wrap(z - 1), z]
    given = []
    for index in range(count):
        given.append([copies.start(parts.at[index, i * 2 + 1 - core], landing.at[index, i], partner) for i in order])
    rings = []
    for index in range(count):
        ring = RingReduce(
            copies, z, lambda i: at(x, y, i, core),
            lambda i, index=index: held.at[index, i],
            lambda i, index=index: held.at[index, i, pl.ds(0, 128)],
            lambda i, index=index: held.at[index, i, pl.ds(128, 128)],
            (low_in.at[index], high_in.at[index], plus_in.at[index], minus_in.at[index]),
        )
        for k, i in enumerate(order):
            given[index][k].wait_recv()
            accumulate(held.at[index, i], parts.at[index, i * 2 + core], landing.at[index, i])
            if k == 0:
                ring.first()
        rings.append(ring)
    for ring in rings:
        ring.second()
    for index, ring in enumerate(rings):
        ring.finish(sums.at[index])
    copies.drain()


def combine(parts):
    count = parts.shape[0]
    return call(
        functools.partial(combine_kernel, count), "combine", 2,
        jax.ShapeDtypeStruct((count, 256, 1024), F32), (parts,),
        [
            pltpu.VMEM((count, SIDE, 256, 1024), BF),
            pltpu.VMEM((count, SIDE, 256, 1024), BF),
            pltpu.VMEM((count, 128, 1024), BF),
            pltpu.VMEM((count, 128, 1024), BF),
            pltpu.VMEM((count, 256, 1024), BF),
            pltpu.VMEM((count, 256, 1024), BF),
        ],
        8 * count, [vmem_spec()], vmem_spec(),
    )


def shift_kernel(rows, got, send, recv):
    x, y, z, core = place()
    seq = z * 2 + core
    copies = Copies(send, recv)
    before, after = wrap(seq - 1, PEERS), wrap(seq + 1, PEERS)
    greet([(y * SIDE + x, before), (y * SIDE + x, after)])
    copy = copies.start(rows, got, (y * SIDE + x, before))
    copy.wait_recv()
    copies.drain()


def shift_back(rows):
    return call(
        shift_kernel, "shift_back", 3,
        jax.ShapeDtypeStruct(rows.shape, rows.dtype), (rows,), [], 1, [vmem_spec()], vmem_spec(),
    )


def reduce_kernel(
    mix, feed, down, small,
    g_in, g_out, g_gate, g_up, g_down, g_small,
    mix_sum, mix_got, feed_sum, down_sum,
    mix_wide, feed_wide, down_wide, mix_land, feed_land, small_y, small_x, small_z, small_one, small_two,
    m1l, m1h, m1p, m1m, n1l, n1h, n1p, n1m, m2l, m2h, m2p, m2m, n2l, n2h, n2p, n2m,
    f1l, f1h, f1p, f1m, h1l, h1h, h1p, h1m, f2l, f2h, f2p, f2m, h2l, h2h, h2p, h2m,
    d1l, d1h, d1p, d1m, e1l, e1h, e1p, e1m, d2l, d2h, d2p, d2m, e2l, e2h, e2p, e2m,
    local_sem, send, recv,
):
    x, y, z, core = place()
    seq = z * 2 + core
    copies = Copies(send, recv)
    partner = at(x, y, z, 1 - core)
    peers = seq_peers(x, y, z, core)
    across = [at(wrap(x + k), y, z, core) for k in range(1, SIDE)]
    along = [at(x, wrap(y + k), z, core) for k in range(1, SIDE)]
    greet(peers + across + along)

    order = [wrap(y + 2), wrap(y + 1), wrap(y - 1), y]
    given, loads = [], []
    for k, i in enumerate(order):
        given.append(copies.start(mix.at[1 - core, i], mix_got.at[i], partner))
        load = pltpu.make_async_copy(mix.at[core, i], mix_sum.at[i], local_sem.at[k])
        load.start()
        loads.append(load)
    load_feed = pltpu.make_async_copy(feed, feed_sum, local_sem.at[4])
    load_feed.start()
    load_down = pltpu.make_async_copy(down, down_sum, local_sem.at[5])
    load_down.start()

    sent_y = [
        copies.start(small.at[wrap(y + k)], small_y.at[k], device) for k, device in zip(range(1, SIDE), along)
    ]

    def by_rows(ref, which, part):
        start, size = (32 * which, 32) if part is None else (32 * which + 16 * part, 16)
        lead = [slice(None)] * (len(ref.shape) - 2)
        return ref.at[(*lead, pl.ds(start, size), slice(None))]

    def by_columns(ref, which, part):
        start, size = (512 * which, 512) if part is None else (512 * which + 256 * part, 256)
        lead = [slice(None)] * (len(ref.shape) - 2)
        return ref.at[(*lead, slice(None), pl.ds(start, size))]

    def plane(target, halves, landings):
        all_y = RingReduce(
            copies, y, lambda i: at(x, i, z, core),
            lambda i: halves(target.at[i], 0, None),
            lambda i: halves(target.at[i, pl.ds(0, 2)], 0, None),
            lambda i: halves(target.at[i, pl.ds(2, 2)], 0, None),
            landings[0],
        )
        all_x = RingReduce(
            copies, x, lambda i: at(i, y, z, core),
            lambda i: halves(target.at[:, i], 1, None),
            lambda i: halves(target.at[pl.ds(0, 2), i], 1, None),
            lambda i: halves(target.at[pl.ds(2, 2), i], 1, None),
            landings[1],
        )
        row_x = RingReduce(
            copies, x, lambda i: at(i, y, z, core),
            lambda i: halves(target.at[y, i], 0, None),
            lambda i: halves(target.at[y, i], 0, 0),
            lambda i: halves(target.at[y, i], 0, 1),
            landings[2],
        )
        row_y = RingReduce(
            copies, y, lambda i: at(x, i, z, core),
            lambda i: halves(target.at[i, x], 1, None),
            lambda i: halves(target.at[i, x], 1, 0),
            lambda i: halves(target.at[i, x], 1, 1),
            landings[3],
        )
        return all_y, all_x, row_x, row_y

    plan_feed = plane(
        feed_sum, by_rows,
        ((f1l, f1h, f1p, f1m), (h1l, h1h, h1p, h1m), (f2l, f2h, f2p, f2m), (h2l, h2h, h2p, h2m)),
    )
    plan_down = plane(
        down_sum, by_columns,
        ((d1l, d1h, d1p, d1m), (e1l, e1h, e1p, e1m), (d2l, d2h, d2p, d2m), (e2l, e2h, e2p, e2m)),
    )
    plan_mix = plane(
        mix_sum, by_rows,
        ((m1l, m1h, m1p, m1m), (n1l, n1h, n1p, n1m), (m2l, m2h, m2p, m2m), (n2l, n2h, n2p, n2m)),
    )
    load_feed.wait()
    plan_feed[0].first()
    plan_feed[1].first()
    load_down.wait()
    plan_down[0].first()
    plan_down[1].first()
    for k, i in enumerate(order):
        loads[k].wait()
        given[k].wait_recv()
        accumulate(mix_sum.at[i], mix_sum.at[i], mix_got.at[i])
        if k == 0:
            plan_mix[0].first()
    plan_mix[1].first()
    for copy in sent_y:
        copy.wait_recv()
    for i in range(SIDE):
        total = small[y, i]
        for k in range(1, SIDE):
            total = total + small_y[k, i]
        small_one[i] = total
    sent_x = [
        copies.start(small_one.at[wrap(x + k)], small_x.at[k], device) for k, device in zip(range(1, SIDE), across)
    ]
    plans = (plan_feed, plan_down, plan_mix)
    for plan in plans:
        plan[0].second()
        plan[1].second()
    for copy in sent_x:
        copy.wait_recv()
    total = small_one[x]
    for k in range(1, SIDE):
        total = total + small_x[k]
    small_two[...] = total
    sent_z = [copies.start(small_two, small_z.at[seq], peer) for peer in peers]
    small_z[seq] = total
    for plan in plans:
        plan[0].finish()
        plan[2].first()
        plan[1].finish()
        plan[3].first()
    for plan in plans:
        plan[2].second()
        plan[3].second()
    plan_feed[2].finish(by_rows(feed_wide, 0, None))
    plan_feed[3].finish(by_rows(feed_wide, 1, None))
    sent_feed = []
    for k, peer in enumerate(peers):
        rows = pl.ds(pl.multiple_of(wrap(seq + k + 1, PEERS) * 8, 8), 8)
        sent_feed.append(copies.start(feed_wide.at[rows], feed_land.at[seq], peer))
    feed_land[seq] = feed_wide[pl.ds(pl.multiple_of(seq * 8, 8), 8), :]
    plan_down[2].finish(by_columns(down_wide, 0, None))
    plan_down[3].finish(by_columns(down_wide, 1, None))
    g_down[...] = down_wide[0:OWN, :]
    plan_mix[2].finish(by_rows(mix_wide, 0, None))
    plan_mix[3].finish(by_rows(mix_wide, 1, None))
    sent_mix = []
    for k, peer in enumerate(peers):
        rows = pl.ds(pl.multiple_of(wrap(seq + k + 1, PEERS) * 8, 8), 8)
        sent_mix.append(copies.start(mix_wide.at[rows], mix_land.at[seq], peer))
    mix_land[seq] = mix_wide[pl.ds(pl.multiple_of(seq * 8, 8), 8), :]
    for copy in sent_z:
        copy.wait_recv()
    g_small[...] = functools.reduce(lambda a, b: a + b, [small_z[s] for s in range(PEERS)])
    for copy in sent_feed:
        copy.wait_recv()
    for d in range(16):
        gates, ups = [], []
        for s in range(PEERS):
            rows = feed_land[s]
            gate = jnp.concatenate([rows[:, :WIDE], rows[:, 1024:1088]], axis=1)
            up = jnp.concatenate([rows[:, WIDE:1024], rows[:, 1088:1152]], axis=1)
            gates.append(gate[:, OWN * d : OWN * d + OWN])
            ups.append(up[:, OWN * d : OWN * d + OWN])
        g_gate[:, 288 * d : 288 * d + 288] = jnp.concatenate(gates, axis=1)
        g_up[:, 288 * d : 288 * d + 288] = jnp.concatenate(ups, axis=1)
    for copy in sent_mix:
        copy.wait_recv()
    for half in range(2):
        rows = functools.reduce(lambda a, b: a + b, [mix_land[2 * k + half] for k in range(SIDE)])
        for k in range(3):
            g_in[:, 1024 * k + 512 * half : 1024 * k + 512 * half + 512] = rows[:, 512 * k : 512 * k + 512]
        g_out[:, 512 * half : 512 * half + 512] = rows[:, 1536:]
    copies.drain()


def landing_rows(columns):
    def four(low, whole):
        return [pltpu.VMEM(low, BF), pltpu.VMEM(low, BF), pltpu.VMEM(whole, BF), pltpu.VMEM(whole, BF)]

    group = four((2, 32, columns), (4, 32, columns))
    single = four((16, columns), (32, columns))
    return group + group + single + single


def landing_columns():
    def four(low, whole):
        return [pltpu.VMEM(low, BF), pltpu.VMEM(low, BF), pltpu.VMEM(whole, BF), pltpu.VMEM(whole, BF)]

    group = four((2, PAD, 512), (4, PAD, 512))
    single = four((PAD, 256), (PAD, 512))
    return group + group + single + single


def reduce_grads(mix, feed, down, small):
    outs = (
        jax.ShapeDtypeStruct((8, 3072), F32),
        jax.ShapeDtypeStruct((8, 1024), F32),
        jax.ShapeDtypeStruct((8, 4608), F32),
        jax.ShapeDtypeStruct((8, 4608), F32),
        jax.ShapeDtypeStruct((OWN, 1024), F32),
        jax.ShapeDtypeStruct((8, 128), F32),
    )
    scratch = [
        pltpu.VMEM((4, 4, 64, 2048), BF),
        pltpu.VMEM((4, 4, 64, 2048), BF),
        pltpu.VMEM((4, 4, 64, 1152), BF),
        pltpu.VMEM((4, 4, PAD, 1024), BF),
        pltpu.VMEM((64, 2048), F32),
        pltpu.VMEM((64, 1152), F32),
        pltpu.VMEM((PAD, 1024), F32),
        pltpu.VMEM((PEERS, 8, 2048), F32),
        pltpu.VMEM((PEERS, 8, 1152), F32),
        pltpu.VMEM((4, 4, 8, 128), F32),
        pltpu.VMEM((4, 8, 128), F32),
        pltpu.VMEM((PEERS, 8, 128), F32),
        pltpu.VMEM((4, 8, 128), F32),
        pltpu.VMEM((8, 128), F32),
        *landing_rows(2048),
        *landing_rows(1152),
        *landing_columns(),
        pltpu.SemaphoreType.DMA((6,)),
    ]
    return call(
        reduce_kernel, "reduce_grads", 4, outs, (mix, feed, down, small), scratch, 96,
        [any_spec()] * 3 + [vmem_spec()], (vmem_spec(),) * 6,
    )


def adamw(weight, grad, first, second, rate, decay):
    first_new = beta_one * first + (1.0 - beta_one) * grad
    second_new = beta_two * second + (1.0 - beta_two) * grad * grad
    first_hat = first_new / (1.0 - beta_one**STEP)
    second_hat = second_new / (1.0 - beta_two**STEP)
    weight_new = weight - rate * (
        first_hat / (jnp.sqrt(second_hat) + epsilon_adam) + decay * weight
    )
    return (weight_new, first_new, second_new)


def norm_back(upstream, scaled, inverse, gain):
    weighted = upstream * gain
    return inverse * (weighted - scaled * jnp.mean(weighted * scaled, axis=-1, keepdims=True))


def dot(a, b, dims=((1,), (0,))):
    return lax.dot_general(a, b, (dims, ((), ())), preferred_element_type=F32)


NT = ((1,), (1,))
TN = ((0,), (0,))


def shards(
    inputs, cotangent, norm_gains, conv_taps, w_in, w_out, w_gate, w_up, w_down,
    first_gains, first_taps, first_in, first_out, first_gate, first_up, first_down,
    second_gains, second_taps, second_in, second_out, second_gate, second_up, second_down,
):
    seq = lax.axis_index("seq")
    rows = jnp.concatenate([norm_gains, conv_taps], axis=0).astype(BF).astype(F32)
    small = lax.dynamic_update_slice(
        jnp.zeros((8, 128), F32), jnp.pad(rows, ((0, 3), (0, 0))), (0, seq * 8)
    )
    mix, feed, down, small_all, edge, grad_all = gather(
        w_in, w_out, w_gate, w_up, w_down, small, inputs[:, 112:], cotangent.reshape(256, D)
    )
    mix = mix.reshape(2, D, 2048)
    feed = feed.reshape(D, 2 * SLICE)
    down = down.reshape(16, PAD, D)[:, :OWN].reshape(SLICE, D)
    small_rows = small_all.reshape(16, 8, 128)[:, :, :64].transpose(1, 0, 2).reshape(8, D)
    gains_wide, taps_wide = small_rows[:2], small_rows[2:5]

    wide = inputs.astype(F32).reshape(256, D)
    every = jnp.concatenate([wide, edge[:, 14:].astype(F32).reshape(4, D)], axis=0)
    inverse_every = lax.rsqrt(jnp.mean(every * every, axis=-1, keepdims=True) + epsilon_norm)
    scaled_every = every * inverse_every
    normed_every = (scaled_every * gains_wide[0]).astype(BF)
    inverse, scaled, normed = inverse_every[:256], scaled_every[:256], normed_every[:256]
    grad_wide = cotangent.astype(F32).reshape(256, D)
    projected = [dot(normed_every, mix[c, :, :1536]) for c in range(2)]
    b_every, c_every, x_every = (
        jnp.concatenate([projected[c][:, 512 * k : 512 * k + 512] for c in range(2)], axis=1) for k in range(3)
    )
    gated_every = b_every * x_every
    b_part, c_part, x_part = b_every[:256], c_every[:256], x_every[:256]
    earlier = jnp.where(seq > 0, gated_every[256:], 0.0).reshape(2, 2, D)
    gated = gated_every[:256].reshape(2, 128, D)
    extended = jnp.concatenate([earlier, gated], axis=1)
    convolved = (
        taps_wide[0] * extended[:, :-2] + taps_wide[1] * extended[:, 1:-1] + taps_wide[2] * extended[:, 2:]
    ).reshape(256, D)
    mixer_input = (c_part * convolved).astype(BF)
    hidden = wide + jnp.concatenate([dot(mixer_input, mix[c, :, 1536:]) for c in range(2)], axis=1)
    inverse_two = lax.rsqrt(jnp.mean(hidden * hidden, axis=-1, keepdims=True) + epsilon_norm)
    scaled_two = hidden * inverse_two
    normed_two = (scaled_two * gains_wide[1]).astype(BF)

    tokens = exchange(normed_two).reshape(2048, D)
    grads = grad_all.reshape(2048, D)
    value = dot(tokens, feed)
    active, grad_gate, grad_up = [], [], []
    grad_active = dot(grads, down, NT)
    for gate, up, back in (
        (value[:, :WIDE], value[:, WIDE:1024], grad_active[:, :WIDE]),
        (value[:, 1024:1088], value[:, 1088:], grad_active[:, WIDE:]),
    ):
        sigmoid = jax.nn.sigmoid(gate)
        active.append((gate * sigmoid * up).astype(BF))
        grad_up.append((back * (gate * sigmoid)).astype(BF))
        grad_gate.append((back * up * (sigmoid * (1.0 + gate * (1.0 - sigmoid)))).astype(BF))
    active = jnp.concatenate(active, axis=1)
    grad_value = jnp.concatenate([grad_gate[0], grad_up[0], grad_gate[1], grad_up[1]], axis=1)
    part_out = dot(active, down).astype(BF)
    part_back = dot(grad_value, feed, NT).astype(BF)
    grad_feed = dot(tokens, grad_value, TN).astype(BF)
    grad_down = dot(active, grads, TN).astype(BF)
    sums = combine(jnp.stack([part_back, part_out]).reshape(2, PEERS, 256, D))
    output = (hidden + sums[1]).astype(BF)
    grad_normed_two = sums[0]
    grad_gain_two = jnp.sum(grad_normed_two * scaled_two, axis=0)
    grad_hidden = grad_wide + norm_back(grad_normed_two, scaled_two, inverse_two, gains_wide[1])
    narrow = grad_hidden.astype(BF)
    grad_mixer = sum(dot(narrow[:, 512 * c : 512 * c + 512], mix[c, :, 1536:], NT) for c in range(2))
    grad_c = grad_mixer * convolved
    grad_conv = (grad_mixer * c_part).reshape(2, 128, D)
    grad_taps = jnp.stack([jnp.sum(grad_conv * extended[:, k : k + 128], axis=(0, 1)) for k in range(3)])
    later = shift_back(grad_conv[:, :8])
    later = jnp.where(seq < PEERS - 1, later[:, :2], 0.0)
    padded = jnp.concatenate([grad_conv, later], axis=1)
    grad_gated = (
        taps_wide[2] * padded[:, :128] + taps_wide[1] * padded[:, 1:129] + taps_wide[0] * padded[:, 2:]
    ).reshape(256, D)
    grad_parts = [(grad_gated * x_part).astype(BF), grad_c.astype(BF), (grad_gated * b_part).astype(BF)]
    grad_projected = [
        jnp.concatenate([part[:, 512 * c : 512 * c + 512] for part in grad_parts], axis=1) for c in range(2)
    ]
    grad_normed = sum(dot(grad_projected[c], mix[c, :, :1536], NT) for c in range(2))
    grad_mix = jnp.stack(
        [
            jnp.concatenate(
                [
                    dot(normed, grad_projected[c], TN),
                    dot(mixer_input, narrow[:, 512 * c : 512 * c + 512], TN),
                ],
                axis=1,
            ).astype(BF)
            for c in range(2)
        ]
    )
    grad_gain_one = jnp.sum(grad_normed * scaled, axis=0)
    input_grad = grad_hidden + norm_back(grad_normed, scaled, inverse, gains_wide[0])
    small_grads = jnp.concatenate(
        [grad_gain_one[None], grad_gain_two[None], grad_taps, jnp.zeros((3, D), F32)], axis=0
    )
    small_grads = jnp.pad(small_grads.reshape(8, 16, 64).transpose(1, 0, 2), ((0, 0), (0, 0), (0, 64)))
    red_in, red_out, red_gate, red_up, red_down, red_small = reduce_grads(
        grad_mix.reshape(2, 4, 4, 64, 2048),
        grad_feed.reshape(4, 4, 64, 2 * SLICE),
        jnp.pad(grad_down.reshape(16, OWN, D), ((0, 0), (0, PAD - OWN), (0, 0))).reshape(4, 4, PAD, D),
        small_grads.reshape(4, 4, 8, 128),
    )
    red_small = lax.dynamic_slice(red_small, (0, seq * 8), (8, 8))
    red_gains, red_taps = red_small[:2], red_small[2:5]

    new = (
        adamw(norm_gains, red_gains, first_gains, second_gains, rate_small, 0.0),
        adamw(conv_taps, red_taps, first_taps, second_taps, rate_small, 0.0),
        adamw(w_in, red_in, first_in, second_in, rate_matrix, weight_decay),
        adamw(w_out, red_out, first_out, second_out, rate_matrix, weight_decay),
        adamw(w_gate, red_gate, first_gate, second_gate, rate_matrix, weight_decay),
        adamw(w_up, red_up, first_up, second_up, rate_matrix, weight_decay),
        adamw(w_down, red_down, first_down, second_down, rate_matrix, weight_decay),
    )
    return (
        output.reshape(2, 128, D),
        input_grad.reshape(2, 128, D),
        *[group[0] for group in new],
        *[group[1] for group in new],
        *[group[2] for group in new],
    )


def solution(mesh):
    tokens, columns, rows = P("dp", "seq", None), P(None, ("dp", "seq")), P(("dp", "seq"), None)
    weights = (columns, columns, rows, rows, rows, rows, rows)
    return jax.shard_map(
        shards,
        mesh=mesh,
        in_specs=(tokens, tokens) + weights * 3,
        out_specs=(tokens, tokens) + weights * 3,
        check_vma=False,
    )
```

```python
import functools

import jax
import jax.numpy as jnp
from jax import lax
from jax.experimental import pallas as pl
from jax.experimental.pallas import tpu as pltpu
from jax.sharding import PartitionSpec as P

D = 1024
STEP = 5

epsilon_norm = 1e-05
beta_one = 0.9
beta_two = 0.95
epsilon_adam = 1e-08
rate_matrix = 0.02
rate_small = 0.3
weight_decay = 0.1

MESH = pl.DeviceIdType.MESH
BF = jnp.bfloat16
F32 = jnp.float32
SIDE = 4
PEERS = 8
OWN = 36
PAD = 48
SLICE = 576
WIDE = 512
VMEM_BYTES = 58 * 2**20


def place():
    dp, seq = lax.axis_index("dp"), lax.axis_index("seq")
    return lax.rem(dp, SIDE), lax.div(dp, SIDE), lax.div(seq, 2), lax.rem(seq, 2)


def wrap(value, size=SIDE):
    return lax.rem(value + size, size)


def at(x, y, z, core):
    return (y * SIDE + x, z * 2 + core)


class Copies:
    def __init__(self, send, recv):
        self.send, self.recv, self.started, self.sent = send, recv, [], set()

    def plan(self, source, target, device):
        index = len(self.started)
        copy = pltpu.make_async_remote_copy(
            src_ref=source,
            dst_ref=target,
            send_sem=self.send.at[index],
            recv_sem=self.recv.at[index],
            device_id=device,
            device_id_type=MESH,
        )
        self.started.append(copy)
        return copy

    def start(self, source, target, device):
        copy = self.plan(source, target, device)
        copy.start()
        return copy

    def drain(self, some=None):
        for copy in self.started if some is None else some:
            if id(copy) not in self.sent:
                self.sent.add(id(copy))
                copy.wait_send()


def greet(devices):
    barrier = pltpu.get_barrier_semaphore()
    for device in devices:
        pl.semaphore_signal(barrier, inc=1, device_id=device, device_id_type=MESH)
    pl.semaphore_wait(barrier, len(devices))


def seq_peers(x, y, z, core):
    seq = z * 2 + core
    return [(y * SIDE + x, wrap(seq + k, PEERS)) for k in range(1, PEERS)]


class RingGather:
    def __init__(self, copies, me, to, block, low, high):
        self.copies, self.me, self.to = copies, me, to
        self.block, self.low, self.high = block, low, high

    def plan(self, source=None):
        source = self.block(self.me) if source is None else source
        below, above = wrap(self.me - 1), wrap(self.me + 1)
        self.a = self.copies.plan(source, self.block(self.me), self.to(above))
        self.b = self.copies.plan(source, self.block(self.me), self.to(below))
        self.e = self.copies.plan(self.low(below), self.low(below), self.to(above))
        self.f = self.copies.plan(self.high(above), self.high(above), self.to(below))

    def first(self, source=None):
        if not hasattr(self, "a"):
            self.plan(source)
        self.a.start()
        self.b.start()

    def second(self):
        self.a.wait_recv()
        self.e.start()
        self.b.wait_recv()
        self.f.start()

    def finish(self):
        self.e.wait_recv()
        self.f.wait_recv()

    def copies_made(self):
        return [self.a, self.b, self.e, self.f]


class RingReduce:
    def __init__(self, copies, me, to, block, low, high, landing):
        self.copies, self.me, self.to = copies, me, to
        self.block, self.low, self.high = block, low, high
        self.low_in, self.high_in, self.plus_in, self.minus_in = landing

    def plan(self):
        far, below, above = wrap(self.me + 2), wrap(self.me - 1), wrap(self.me + 1)
        self.e = self.copies.plan(self.low(far), self.low_in, self.to(above))
        self.f = self.copies.plan(self.high(far), self.high_in, self.to(below))
        self.g = self.copies.plan(self.block(above), self.plus_in, self.to(above))
        self.h = self.copies.plan(self.block(below), self.minus_in, self.to(below))

    def first(self):
        if not hasattr(self, "e"):
            self.plan()
        self.e.start()
        self.f.start()

    def second(self):
        below, above = wrap(self.me - 1), wrap(self.me + 1)
        self.e.wait_recv()
        accumulate(self.low(above), self.low(above), self.low_in)
        self.g.start()
        self.f.wait_recv()
        accumulate(self.high(below), self.high(below), self.high_in)
        self.h.start()

    def finish(self, target=None):
        own = self.block(self.me)
        self.g.wait_recv()
        self.h.wait_recv()
        accumulate(own if target is None else target, own, self.plus_in, self.minus_in)


def accumulate(target, *sources):
    shape = target.shape
    if len(shape) > 2:
        for index in range(shape[0]):
            accumulate(target.at[index], *[source.at[index] for source in sources])
        return
    step = 16

    @pl.loop(0, shape[0] // step)
    def _(i):
        rows = pl.ds(pl.multiple_of(i * step, step), step)
        total = sources[0][rows, :].astype(F32)
        for source in sources[1:]:
            total = total + source[rows, :].astype(F32)
        target[rows, :] = total.astype(target.dtype)


def any_spec():
    return pl.BlockSpec(memory_space=pl.ANY)


def vmem_spec():
    return pl.BlockSpec(memory_space=pltpu.VMEM)


def call(kernel, name, ident, outs, ins, scratch, copies, specs_in, specs_out):
    return pl.pallas_call(
        kernel,
        out_shape=outs,
        in_specs=specs_in,
        out_specs=specs_out,
        scratch_shapes=list(scratch)
        + [pltpu.SemaphoreType.DMA((copies,)), pltpu.SemaphoreType.DMA((copies,))],
        compiler_params=pltpu.CompilerParams(
            collective_id=ident, has_side_effects=True, vmem_limit_bytes=VMEM_BYTES
        ),
        name=name,
    )(*ins)


def columns_of(seq, dp_count=16):
    return [(288 * d + OWN * seq, 36 * d) for d in range(dp_count)]


def dot(a, b, dims=((1,), (0,))):
    return lax.dot_general(a, b, (dims, ((), ())), preferred_element_type=F32)


NT = ((1,), (1,))
TN = ((0,), (0,))
ROWS = 256
EVERY = 272
HALF = 512


def by_rows(ref, which, part):
    start, size = (32 * which, 32) if part is None else (32 * which + 16 * part, 16)
    lead = [slice(None)] * (len(ref.shape) - 2)
    return ref.at[(*lead, pl.ds(start, size), slice(None))]


def by_columns(ref, which, part):
    start, size = (512 * which, 512) if part is None else (512 * which + 256 * part, 256)
    lead = [slice(None)] * (len(ref.shape) - 2)
    return ref.at[(*lead, slice(None), pl.ds(start, size))]


def visit(z, k):
    return wrap(z + lax.rem(k, 2) * 2 + lax.div(k, 2))


class PlaneGather:
    def __init__(self, copies, spot, view, halves, block):
        x, y, z, core = spot
        to_x, to_y = (lambda i: at(i, y, z, core)), (lambda i: at(x, i, z, core))
        everything = slice(None)
        self.x, self.y, self.view, self.halves = x, y, view, halves
        self.row_x = RingGather(
            copies, x, to_x,
            lambda i: halves(view(y, i), 0, None),
            lambda i: halves(view(y, i), 0, 0),
            lambda i: halves(view(y, i), 0, 1),
        )
        self.row_y = RingGather(
            copies, y, to_y,
            lambda i: halves(view(i, x), 1, None),
            lambda i: halves(view(i, x), 1, 0),
            lambda i: halves(view(i, x), 1, 1),
        )
        self.all_y = RingGather(
            copies, y, to_y,
            lambda i: halves(view(i, everything), 0, None),
            lambda i: halves(view(i, pl.ds(0, 2)), 0, None),
            lambda i: halves(view(i, pl.ds(2, 2)), 0, None),
        )
        self.all_x = RingGather(
            copies, x, to_x,
            lambda i: halves(view(everything, i), 1, None),
            lambda i: halves(view(pl.ds(0, 2), i), 1, None),
            lambda i: halves(view(pl.ds(2, 2), i), 1, None),
        )
        self.row_x.plan(halves(block, 0, None))
        self.row_y.plan(halves(block, 1, None))
        self.all_y.plan()
        self.all_x.plan()

    def one(self):
        self.row_x.first()
        self.row_y.first()

    def two(self):
        self.row_x.second()
        self.row_y.second()

    def three(self):
        self.row_x.finish()
        self.all_y.first()
        self.row_y.finish()
        self.all_x.first()

    def four(self):
        self.all_y.second()
        self.all_x.second()

    def finish(self):
        self.all_y.finish()
        self.all_x.finish()

    def copies(self):
        return [copy for ring in (self.row_x, self.row_y, self.all_y, self.all_x) for copy in ring.copies_made()]

    def group(self, which, step):
        everything = slice(None)
        if which == 0:
            return self.halves(self.view(wrap(self.y + step), everything), 0, None)
        return self.halves(self.view(everything, wrap(self.x + step)), 1, None)


def small_rows(small_all):
    pieces = [small_all[d // 4, d % 4][:, :64] for d in range(16)]
    return jnp.concatenate(pieces, axis=1)


def normalize(rows, gain):
    inverse = lax.rsqrt(jnp.mean(rows * rows, axis=-1, keepdims=True) + epsilon_norm)
    return rows * inverse * gain


def extend(extended, projected, half, sequence):
    first = pl.ds(ROWS + 8 * sequence, 8)
    main = pl.ds(128 * sequence, 128)
    extended[0:8, :] = projected[half, first, :HALF] * projected[half, first, 1024:]
    extended[8:136, :] = projected[half, main, :HALF] * projected[half, main, 1024:]


def convolve(extended, taps):
    return taps[0:1] * extended[6:134, :] + taps[1:2] * extended[7:135, :] + taps[2:3] * extended[8:136, :]


def half_lanes(half):
    return pl.ds(pl.multiple_of(half * HALF, HALF), HALF)


def forward_kernel(
    w_in, w_out, w_gate, w_up, w_down, small, inputs, edge, cotangent,
    back_sum, hidden_out, mix_out, projected_out, normed_out, mixer_out, held_out, grad_feed, grad_down, rows_out,
    mix, feed, down, small_all, edge_in, tokens, grads,
    mix_send, feed_send, mix_got, feed_got, small_got, mix_block, feed_block, down_block, small_send,
    rows, normed, projected, extended, mixer_in, hidden, normed_two,
    down_rows, narrow_wide, value, grad_active, active, grad_value,
    give, give_out, landing, landing_out, held, sum_out, low_in, high_in, plus_in, minus_in, down_part,
    local_sem, send, recv,
):
    spot = x, y, z, core = place()
    seq = z * 2 + core
    copies = Copies(send, recv)
    peers = seq_peers(x, y, z, core)
    across = [at(wrap(x + k), y, z, core) for k in range(1, SIDE)]
    along = [at(x, wrap(y + k), z, core) for k in range(1, SIDE)]
    partner = at(x, y, z, 1 - core)
    greet(peers + across + along)

    def to_z(i):
        return at(x, y, i, core)

    small_copies = [copies.start(small, small_got.at[seq], peer) for peer in peers]
    edge_copy = copies.start(edge, edge_in, (y * SIDE + x, wrap(seq + 1, PEERS)))
    for half in range(2):
        parts = [w_in[:, 1024 * k + 512 * half : 1024 * k + 512 * half + 512] for k in range(3)]
        parts.append(w_out[:, 512 * half : 512 * half + 512])
        upper = jnp.concatenate(parts[:2], axis=1)
        lower = jnp.concatenate(parts[2:], axis=1)
        mix_send[half] = jnp.concatenate([upper, lower], axis=0).astype(BF)
    mix_copies = []
    for k, peer in enumerate(peers):
        other = wrap(seq + k + 1, PEERS)
        mix_copies.append(copies.start(mix_send.at[lax.rem(other, 2)], mix_got.at[seq], peer))
    mix_got[seq] = mix_send[core]
    small_got[seq] = small[...]
    for s in range(PEERS):
        gate = jnp.concatenate([w_gate[:, a : a + OWN] for a, _ in columns_of(s)], axis=1)
        up = jnp.concatenate([w_up[:, a : a + OWN] for a, _ in columns_of(s)], axis=1)
        tail = jnp.concatenate([gate[:, WIDE:], up[:, WIDE:]], axis=1)
        upper = jnp.concatenate([gate[:, :WIDE], up[:, :128]], axis=1)
        lower = jnp.concatenate([up[:, 128:WIDE], tail, jnp.zeros((8, 128), F32)], axis=1)
        feed_send[s] = jnp.concatenate([upper, lower], axis=0).astype(BF)
    feed_copies = []
    for k, peer in enumerate(peers):
        other = wrap(seq + k + 1, PEERS)
        feed_copies.append(copies.start(feed_send.at[other], feed_got.at[seq], peer))
    feed_got[seq] = feed_send[seq]
    narrow_wide[0:PAD, :] = jnp.zeros((PAD, D), F32)
    narrow_wide[0:OWN, :] = w_down[...]
    down_block[...] = narrow_wide[0:PAD, :].astype(BF)

    mixed = PlaneGather(copies, spot, lambda i, j: mix.at[core, :, i, j], by_rows, mix_block)
    fed = PlaneGather(copies, spot, lambda i, j: feed.at[i, j], by_rows, feed_block)
    downs = PlaneGather(copies, spot, lambda i, j: down.at[i, j], by_columns, down_block)

    for copy in small_copies:
        copy.wait_recv()
    small_send[...] = functools.reduce(lambda a, b: a + b, [small_got[s] for s in range(PEERS)])
    small_x = [copies.start(small_send, small_all.at[y, x], device) for device in across]
    small_all[y, x] = small_send[...]
    for copy in mix_copies:
        copy.wait_recv()
    for k in range(4):
        a, b = mix_got[2 * k].astype(F32), mix_got[2 * k + 1].astype(F32)
        line = slice(16 * k, 16 * k + 16)
        mix_block[0, line, :] = jnp.concatenate([a[:8], b[:8]], axis=0).astype(BF)
        mix_block[1, line, :] = jnp.concatenate([a[8:], b[8:]], axis=0).astype(BF)
    mixed.one()
    mix[core, :, y, x] = mix_block[...]
    down[y, x] = down_block[...]
    for copy in small_x:
        copy.wait_recv()
    small_y = [copies.start(small_all.at[y], small_all.at[y], device) for device in along]

    ring = RingGather(
        copies, z, to_z,
        lambda i: grads.at[i, core],
        lambda i: grads.at[i, core, pl.ds(0, 128)],
        lambda i: grads.at[i, core, pl.ds(128, 128)],
    )
    ring.first(cotangent)
    grads_passed = [copies.start(cotangent, grads.at[z, core], partner)]
    grads[z, core] = cotangent[...]

    mixed.two()
    for copy in feed_copies:
        copy.wait_recv()
    for k in range(4):
        a, b = feed_got[2 * k].astype(F32), feed_got[2 * k + 1].astype(F32)
        line = slice(16 * k, 16 * k + 16)
        feed_block[line, :640] = jnp.concatenate([a[:8], b[:8]], axis=0).astype(BF)
        feed_block[line, 640:] = jnp.concatenate([a[8:, :512], b[8:, :512]], axis=0).astype(BF)
    feed[y, x] = feed_block[...]
    mixed.three()
    mix_passed = []
    for which in range(2):
        part = mixed.group(which, 0)
        mix_passed.append(copies.start(part, part, partner))
    fed.one()
    downs.one()
    for copy in small_y:
        copy.wait_recv()
    rows[...] = small_rows(small_all)
    normed[0:ROWS, :] = normalize(inputs[...].astype(F32), rows[0:1, :]).astype(BF)
    edge_copy.wait_recv()
    inside = (seq > 0).astype(F32)
    earlier = [
        normalize(edge_in[q].astype(F32)[8:], rows[0:1, :]) * inside for q in range(2)
    ]
    normed[ROWS:EVERY, :] = jnp.concatenate(earlier, axis=0).astype(BF)
    fed.two()
    downs.two()
    mixed.four()
    for which in range(2):
        for step in (1, 3):
            part = mixed.group(which, step)
            mix_passed.append(copies.start(part, part, partner))
    fed.three()
    downs.three()
    ring.second()
    for step in (1, 3):
        chunk = grads.at[wrap(z + step), core]
        grads_passed.append(copies.start(chunk, chunk, partner))
    mixed.finish()
    for which in range(2):
        part = mixed.group(which, 2)
        mix_passed.append(copies.start(part, part, partner))

    for turn in range(2):
        if turn == 1:
            for copy in mix_passed:
                copy.wait_recv()
        half = core if turn == 0 else 1 - core
        first = mix.at[half, 0].reshape(D, D)
        second = mix.at[half, 1].reshape(D, D)
        projected[half, :, :1024] = dot(normed[...], first[...])
        projected[half, :, 1024:] = dot(normed[...], second[:, :HALF])
        lanes = half_lanes(half)
        for q in range(2):
            main = slice(128 * q, 128 * q + 128)
            extend(extended, projected, half, q)
            convolved = convolve(extended, rows[2:5, lanes])
            mixer_in[main, lanes] = (projected[half, main, HALF:1024] * convolved).astype(BF)
    mix_save = pltpu.make_async_copy(mix, mix_out, local_sem.at[0])
    mix_save.start()
    saves = [mix_save]
    for index, (source, target) in enumerate(
        ((projected, projected_out), (normed, normed_out), (mixer_in, mixer_out), (rows, rows_out))
    ):
        save = pltpu.make_async_copy(source, target, local_sem.at[index + 1])
        save.start()
        saves.append(save)
    for half in range(2):
        lanes = slice(HALF * half, HALF * half + HALF)
        weight = mix.at[half, 1].reshape(D, D)
        hidden[:, lanes] = inputs[:, lanes].astype(F32) + dot(mixer_in[...], weight[:, HALF:])
    normed_two[...] = normalize(hidden[...], rows[1:2, :]).astype(BF)
    hidden_save = pltpu.make_async_copy(hidden, hidden_out, local_sem.at[5])
    hidden_save.start()
    saves.append(hidden_save)

    around = RingGather(
        copies, z, to_z,
        lambda i: tokens.at[i, core],
        lambda i: tokens.at[i, core, pl.ds(0, 128)],
        lambda i: tokens.at[i, core, pl.ds(128, 128)],
    )
    around.plan(normed_two)
    passed = [copies.plan(normed_two, tokens.at[z, core], partner)]
    for step in (2, 1, 3):
        chunk = tokens.at[wrap(z + step), core]
        passed.append(copies.plan(chunk, chunk, partner))
    around.first()
    passed[0].start()
    tokens[z, core] = normed_two[...]
    fed.four()
    downs.four()
    ring.finish()
    chunk = grads.at[wrap(z + 2), core]
    grads_passed.append(copies.start(chunk, chunk, partner))
    gives, gives_out = [], []
    for k in range(SIDE):
        gives.append(copies.plan(give.at[k], landing.at[k], partner))
        gives_out.append(copies.plan(give_out.at[k], landing_out.at[k], partner))
    reduce = RingReduce(
        copies, z, to_z,
        lambda i: held.at[i],
        lambda i: held.at[i, pl.ds(0, 128)],
        lambda i: held.at[i, pl.ds(128, 128)],
        (low_in, high_in, plus_in, minus_in),
    )
    reduce.plan()
    downs.finish()
    for i in range(SIDE):
        for d in range(SIDE):
            narrow_wide[OWN * d : OWN * d + OWN, :] = down[i, d][:OWN].astype(F32)
        down_rows[144 * i : 144 * i + 144, :] = narrow_wide[0:144, :].astype(BF)
    for copy in grads_passed:
        copy.wait_recv()
    fed.finish()
    weights = feed.reshape(D, 2 * SLICE)

    @pl.loop(0, SIDE)
    def _(k):
        @pl.when(k == 0)
        def _():
            passed[0].wait_recv()

        @pl.when(k == 1)
        def _():
            around.second()
            passed[2].start()
            passed[3].start()
            around.finish()
            passed[1].start()
            for copy in passed[1:]:
                copy.wait_recv()

        chip = visit(z, k)
        for turn in range(2):
            half = 1 - core if turn == 0 else core
            value[...] = dot(tokens[chip, half], weights[...])
            grad_active[...] = dot(grads[chip, half], down_rows[...], NT)
            base = (chip * 2 + half) * ROWS

            @pl.loop(0, ROWS // 64)
            def _(r):
                line = pl.ds(pl.multiple_of(r * 64, 64), 64)
                target = pl.ds(pl.multiple_of(base + r * 64, 64), 64)
                tail = value[line, 1024:1152]
                ends = []
                for gate, up, back, where in (
                    (value[line, :WIDE], value[line, WIDE:1024], grad_active[line, :WIDE], slice(0, WIDE)),
                    (tail[:, :64], tail[:, 64:], grad_active[line, WIDE:], slice(WIDE, SLICE)),
                ):
                    sigmoid = jax.nn.sigmoid(gate)
                    soft = gate * sigmoid
                    active[target, where] = (soft * up).astype(BF)
                    grad_up = (back * soft).astype(BF)
                    grad_gate = (back * up * (sigmoid * (1.0 + gate * (1.0 - sigmoid)))).astype(BF)
                    ends.append((grad_gate, grad_up))
                grad_value[target, :WIDE] = ends[0][0]
                grad_value[target, WIDE:1024] = ends[0][1]
                grad_value[target, 1024:1088] = ends[1][0]
                grad_value[target, 1088:1152] = ends[1][1]

            lines = pl.ds(pl.multiple_of(base, ROWS), ROWS)
            result = dot(grad_value[lines, :], weights[...], NT).astype(BF)
            if turn == 0:
                give[k] = result
                for step in range(SIDE):
                    @pl.when(k == step)
                    def _(step=step):
                        gives[step].start()
            else:
                held[chip] = result
            result = dot(active[lines, :], down_rows[...]).astype(BF)
            if turn == 0:
                give_out[k] = result
                for step in range(SIDE):
                    @pl.when(k == step)
                    def _(step=step):
                        gives_out[step].start()
            else:
                sum_out[chip] = result
        for step in range(SIDE):
            @pl.when(k == step)
            def _(step=step):
                gives[step].wait_recv()
                accumulate(held.at[chip], held.at[chip], landing.at[step])
                if step == 1:
                    reduce.first()

    reduce.second()
    copies.drain(fed.copies())

    @pl.loop(0, 8)
    def _(n):
        columns = pl.ds(pl.multiple_of(n * 128, 128), 128)
        wide = tokens.reshape(2048, D)
        weights[columns, :] = dot(wide[:, columns], grad_value[...], TN).astype(BF)

    feed_save = pltpu.make_async_copy(weights, grad_feed, local_sem.at[6])
    feed_save.start()
    saves.append(feed_save)
    for k in range(SIDE):
        gives_out[k].wait_recv()
        accumulate(sum_out.at[visit(z, k)], sum_out.at[visit(z, k)], landing_out.at[k])
    out_save = pltpu.make_async_copy(sum_out, held_out, local_sem.at[7])
    out_save.start()
    saves.append(out_save)
    reduce.finish(back_sum)

    copies.drain(downs.copies())

    @pl.loop(0, 4)
    def _(n):
        columns = pl.ds(pl.multiple_of(n * 256, 256), 256)
        wide = grads.reshape(2048, D)
        down_part[0:SLICE, :] = dot(active[...], wide[:, columns], TN)
        down_part[SLICE:, :] = jnp.zeros((PAD - OWN, 256), F32)
        for d in range(16):
            down[d // 4, d % 4, :, columns] = down_part[OWN * d : OWN * d + PAD, :].astype(BF)

    down_save = pltpu.make_async_copy(down, grad_down, local_sem.at[8])
    down_save.start()
    saves.append(down_save)
    for save in saves:
        save.wait()
    copies.drain()


def forward(w_in, w_out, w_gate, w_up, w_down, small, inputs, edge, cotangent):
    outs = (
        jax.ShapeDtypeStruct((ROWS, D), F32),
        jax.ShapeDtypeStruct((ROWS, D), F32),
        jax.ShapeDtypeStruct((2, 2, 4, 4, 64, D), BF),
        jax.ShapeDtypeStruct((2, EVERY, 1536), F32),
        jax.ShapeDtypeStruct((EVERY, D), BF),
        jax.ShapeDtypeStruct((ROWS, D), BF),
        jax.ShapeDtypeStruct((SIDE, ROWS, D), BF),
        jax.ShapeDtypeStruct((D, 2 * SLICE), BF),
        jax.ShapeDtypeStruct((4, 4, PAD, D), BF),
        jax.ShapeDtypeStruct((8, D), F32),
    )
    scratch = [
        pltpu.VMEM((2, 2, 4, 4, 64, D), BF),
        pltpu.VMEM((4, 4, 64, 2 * SLICE), BF),
        pltpu.VMEM((4, 4, PAD, D), BF),
        pltpu.VMEM((4, 4, 8, 128), F32),
        pltpu.VMEM((2, 16, D), BF),
        pltpu.VMEM((SIDE, 2, ROWS, D), BF),
        pltpu.VMEM((SIDE, 2, ROWS, D), BF),
        pltpu.VMEM((2, 16, D), BF),
        pltpu.VMEM((PEERS, 16, 640), BF),
        pltpu.VMEM((PEERS, 16, D), BF),
        pltpu.VMEM((PEERS, 16, 640), BF),
        pltpu.VMEM((PEERS, 8, 128), F32),
        pltpu.VMEM((2, 64, D), BF),
        pltpu.VMEM((64, 2 * SLICE), BF),
        pltpu.VMEM((PAD, D), BF),
        pltpu.VMEM((8, 128), F32),
        pltpu.VMEM((8, D), F32),
        pltpu.VMEM((EVERY, D), BF),
        pltpu.VMEM((2, EVERY, 1536), F32),
        pltpu.VMEM((136, HALF), F32),
        pltpu.VMEM((ROWS, D), BF),
        pltpu.VMEM((ROWS, D), F32),
        pltpu.VMEM((ROWS, D), BF),
        pltpu.VMEM((SLICE, D), BF),
        pltpu.VMEM((160, D), F32),
        pltpu.VMEM((ROWS, 2 * SLICE), F32),
        pltpu.VMEM((ROWS, SLICE), F32),
        pltpu.VMEM((2048, SLICE), BF),
        pltpu.VMEM((2048, 2 * SLICE), BF),
        *[pltpu.VMEM((SIDE, ROWS, D), BF)] * 6,
        pltpu.VMEM((128, D), BF),
        pltpu.VMEM((128, D), BF),
        pltpu.VMEM((ROWS, D), BF),
        pltpu.VMEM((ROWS, D), BF),
        pltpu.VMEM((SLICE + PAD - OWN, 256), F32),
        pltpu.SemaphoreType.DMA((9,)),
    ]
    return call(
        forward_kernel, "forward", 0, outs,
        (w_in, w_out, w_gate, w_up, w_down, small, inputs, edge, cotangent), scratch, 128,
        [vmem_spec()] * 9, (vmem_spec(),) + (any_spec(),) * 9,
    )


class PlaneReduce:
    def __init__(self, copies, spot, view, halves, landings):
        x, y, z, core = spot
        to_x, to_y = (lambda i: at(i, y, z, core)), (lambda i: at(x, i, z, core))
        everything = slice(None)
        self.all_y = RingReduce(
            copies, y, to_y,
            lambda i: halves(view(i, everything), 0, None),
            lambda i: halves(view(i, pl.ds(0, 2)), 0, None),
            lambda i: halves(view(i, pl.ds(2, 2)), 0, None),
            landings[0:4],
        )
        self.all_x = RingReduce(
            copies, x, to_x,
            lambda i: halves(view(everything, i), 1, None),
            lambda i: halves(view(pl.ds(0, 2), i), 1, None),
            lambda i: halves(view(pl.ds(2, 2), i), 1, None),
            landings[4:8],
        )
        self.row_x = RingReduce(
            copies, x, to_x,
            lambda i: halves(view(y, i), 0, None),
            lambda i: halves(view(y, i), 0, 0),
            lambda i: halves(view(y, i), 0, 1),
            landings[8:12],
        )
        self.row_y = RingReduce(
            copies, y, to_y,
            lambda i: halves(view(i, x), 1, None),
            lambda i: halves(view(i, x), 1, 0),
            lambda i: halves(view(i, x), 1, 1),
            landings[12:16],
        )
        self.halves = halves

    def one(self):
        self.all_y.first()
        self.all_x.first()

    def two(self):
        self.all_y.second()
        self.all_x.second()

    def three(self):
        self.all_y.finish()
        self.row_x.first()
        self.all_x.finish()
        self.row_y.first()

    def four(self):
        self.row_x.second()
        self.row_y.second()

    def finish(self, target):
        self.row_x.finish(self.halves(target, 0, None))
        self.row_y.finish(self.halves(target, 1, None))


def landing_shapes(lead, rows, columns, split_rows):
    if split_rows:
        half, quarter = (rows // 2, columns), (rows // 4, columns)
    else:
        half, quarter = (rows, columns // 2), (rows, columns // 4)
    group = [(*lead, 2, *half)] * 2 + [(*lead, 4, *half)] * 2
    single = [(*lead, *quarter)] * 2 + [(*lead, *half)] * 2
    return [pltpu.VMEM(shape, BF) for shape in group * 2 + single * 2]


def transposed_dot(left, right, target):
    @pl.loop(0, 4)
    def _(n):
        columns = pl.ds(pl.multiple_of(n * 256, 256), 256)
        target[columns, :] = dot(left[:, columns], right[...], TN).astype(target.dtype)


def backward_kernel(
    back_sum, hidden, cotangent, inputs, rows,
    mix_in, projected_in, normed_in, mixer_in, held_in, feed_in, down_in,
    output, input_grad, g_in, g_out, g_gate, g_up, g_down, g_small,
    mix, projected, normed, mixed_in, held, feed_sum, down_sum, mix_sum, mix_give, mix_got,
    grad_hidden, narrow, grad_mixer, grad_conv, extended, grad_projected, edge_send, edge_got, sums,
    mix_wide, feed_wide, down_wide, mix_land, feed_land,
    small, small_y, small_x, small_z, small_one, small_two, low_in, high_in, plus_in, minus_in,
    *rest,
):
    landings, (local_sem, send, recv) = rest[:48], rest[48:]
    spot = x, y, z, core = place()
    seq = z * 2 + core
    copies = Copies(send, recv)
    partner = at(x, y, z, 1 - core)
    peers = seq_peers(x, y, z, core)
    across = [at(wrap(x + k), y, z, core) for k in range(1, SIDE)]
    along = [at(x, wrap(y + k), z, core) for k in range(1, SIDE)]

    loads = []
    for index, (source, target) in enumerate(
        (
            (feed_in, feed_sum), (down_in, down_sum), (held_in, held), (mix_in, mix),
            (projected_in, projected), (normed_in, normed), (mixer_in, mixed_in),
        )
    ):
        load = pltpu.make_async_copy(source, target, local_sem.at[index])
        load.start()
        loads.append(load)
    greet(peers + across + along)

    fed = PlaneReduce(copies, spot, lambda i, j: feed_sum.at[i, j], by_rows, landings[0:16])
    downs = PlaneReduce(copies, spot, lambda i, j: down_sum.at[i, j], by_columns, landings[16:32])
    mixed = PlaneReduce(copies, spot, lambda i, j: mix_sum.at[:, i, j], by_rows, landings[32:48])
    ring = RingReduce(
        copies, z, lambda i: at(x, y, i, core),
        lambda i: held.at[i], lambda i: held.at[i, pl.ds(0, 128)], lambda i: held.at[i, pl.ds(128, 128)],
        (low_in, high_in, plus_in, minus_in),
    )
    loads[0].wait()
    fed.one()
    loads[1].wait()
    downs.one()
    loads[2].wait()
    ring.first()

    sums[...] = jnp.zeros_like(sums)

    @pl.loop(0, 8)
    def _(n):
        line = pl.ds(pl.multiple_of(n * 32, 32), 32)
        tokens = hidden[line, :]
        inverse = lax.rsqrt(jnp.mean(tokens * tokens, axis=-1, keepdims=True) + epsilon_norm)
        scaled = tokens * inverse
        upstream = back_sum[line, :]
        sums[1:2, :] += jnp.sum(upstream * scaled, axis=0, keepdims=True)
        weighted = upstream * rows[1:2, :]
        result = cotangent[line, :].astype(F32) + inverse * (
            weighted - scaled * jnp.mean(weighted * scaled, axis=-1, keepdims=True)
        )
        grad_hidden[line, :] = result
        narrow[line, :] = result.astype(BF)

    loads[3].wait()
    out_weights = [mix.at[half, 1].reshape(D, D) for half in range(2)]
    grad_mixer[...] = dot(narrow[:, :HALF], out_weights[0][:, HALF:], NT) + dot(
        narrow[:, HALF:], out_weights[1][:, HALF:], NT
    )
    for load in loads[4:]:
        load.wait()
    for q in range(2):
        for half in range(2):
            lanes = slice(HALF * half, HALF * half + HALF)
            start = slice(128 * q, 128 * q + 8)
            edge_send[q, :, lanes] = grad_mixer[start, lanes] * projected[half, start, HALF:1024]
    edge_copy = copies.start(edge_send, edge_got, (y * SIDE + x, wrap(seq - 1, PEERS)))
    for half in range(2):
        lanes = slice(HALF * half, HALF * half + HALF)
        for q in range(2):
            main = slice(128 * q, 128 * q + 128)
            extend(extended, projected, half, q)
            upstream = grad_mixer[main, lanes]
            grad_projected[half, main, HALF:1024] = (upstream * convolve(extended, rows[2:5, lanes])).astype(BF)
            back = upstream * projected[half, main, HALF:1024]
            grad_conv[q, 0:128, lanes] = back
            for k in range(3):
                sums[2 + k : 3 + k, lanes] += jnp.sum(back * extended[6 + k : 134 + k, :], axis=0, keepdims=True)
    fed.two()
    downs.two()
    edge_copy.wait_recv()
    inside = (seq < PEERS - 1).astype(F32)
    for q in range(2):
        grad_conv[q, 128:136, :] = edge_got[q] * inside
        main = slice(128 * q, 128 * q + 128)
        for half in range(2):
            lanes = slice(HALF * half, HALF * half + HALF)
            taps = rows[2:5, lanes]
            gated = (
                taps[2:3] * grad_conv[q, 0:128, lanes]
                + taps[1:2] * grad_conv[q, 1:129, lanes]
                + taps[0:1] * grad_conv[q, 2:130, lanes]
            )
            grad_projected[half, main, 0:HALF] = (gated * projected[half, main, 1024:]).astype(BF)
            grad_projected[half, main, 1024:] = (gated * projected[half, main, :HALF]).astype(BF)

    before = normed.at[0:ROWS]
    given = []
    for target, half in ((mix_give, 1 - core), (mix_sum, core)):
        lanes = half_lanes(half)
        first, second = target.at[0].reshape(D, D), target.at[1].reshape(D, D)
        transposed_dot(before, grad_projected.at[half, :, 0:1024], first)
        if target is mix_give:
            given.append(copies.start(mix_give.at[0], mix_got.at[0], partner))
        transposed_dot(before, grad_projected.at[half, :, 1024:1536], second.at[:, 0:HALF])
        transposed_dot(mixed_in, narrow.at[:, lanes], second.at[:, HALF:1024])
        if target is mix_give:
            given.append(copies.start(mix_give.at[1], mix_got.at[1], partner))
    fed.three()
    downs.three()
    for copy in given:
        copy.wait_recv()
    for k, i in enumerate((wrap(y + 2), wrap(y + 1), wrap(y - 1), y)):
        accumulate(mix_sum.at[:, i], mix_sum.at[:, i], mix_got.at[:, i])
        if k == 0:
            mixed.all_y.first()
    mixed.all_x.first()
    fed.four()
    downs.four()

    grad_mixer[...] = dot(grad_projected[0, :, 0:1024], mix.at[0, 0].reshape(D, D)[...], NT)
    grad_mixer[...] += dot(grad_projected[1, :, 0:1024], mix.at[1, 0].reshape(D, D)[...], NT)
    for half in range(2):
        grad_mixer[...] += dot(grad_projected[half, :, 1024:], out_weights[half][:, :HALF], NT)

    @pl.loop(0, 8)
    def _(n):
        line = pl.ds(pl.multiple_of(n * 32, 32), 32)
        tokens = inputs[line, :].astype(F32)
        inverse = lax.rsqrt(jnp.mean(tokens * tokens, axis=-1, keepdims=True) + epsilon_norm)
        scaled = tokens * inverse
        upstream = grad_mixer[line, :]
        sums[0:1, :] += jnp.sum(upstream * scaled, axis=0, keepdims=True)
        weighted = upstream * rows[0:1, :]
        input_grad[line, :] = grad_hidden[line, :] + inverse * (
            weighted - scaled * jnp.mean(weighted * scaled, axis=-1, keepdims=True)
        )

    for d in range(16):
        tile = jnp.concatenate([sums[:, 64 * d : 64 * d + 64], jnp.zeros((8, 64), F32)], axis=1)
        small[d // 4, d % 4] = tile
    sent_y = [
        copies.start(small.at[wrap(y + k)], small_y.at[k], device) for k, device in zip(range(1, SIDE), along)
    ]
    mixed.two()
    for copy in sent_y:
        copy.wait_recv()
    for i in range(SIDE):
        total = small[y, i]
        for k in range(1, SIDE):
            total = total + small_y[k, i]
        small_one[i] = total
    sent_x = [
        copies.start(small_one.at[wrap(x + k)], small_x.at[k], device) for k, device in zip(range(1, SIDE), across)
    ]
    fed.finish(feed_wide)
    sent_feed = []
    for k, peer in enumerate(peers):
        line = pl.ds(pl.multiple_of(wrap(seq + k + 1, PEERS) * 8, 8), 8)
        sent_feed.append(copies.start(feed_wide.at[line], feed_land.at[seq], peer))
    feed_land[seq] = feed_wide[pl.ds(pl.multiple_of(seq * 8, 8), 8), :]
    downs.finish(down_wide)
    g_down[...] = down_wide[0:OWN, :]
    ring.second()
    for copy in sent_x:
        copy.wait_recv()
    total = small_one[x]
    for k in range(1, SIDE):
        total = total + small_x[k]
    small_two[...] = total
    sent_z = [copies.start(small_two, small_z.at[seq], peer) for peer in peers]
    small_z[seq] = total
    for copy in sent_feed:
        copy.wait_recv()
    for d in range(16):
        gates, ups = [], []
        for s in range(PEERS):
            line = feed_land[s]
            gate = jnp.concatenate([line[:, :WIDE], line[:, 1024:1088]], axis=1)
            up = jnp.concatenate([line[:, WIDE:1024], line[:, 1088:1152]], axis=1)
            gates.append(gate[:, OWN * d : OWN * d + OWN])
            ups.append(up[:, OWN * d : OWN * d + OWN])
        g_gate[:, 288 * d : 288 * d + 288] = jnp.concatenate(gates, axis=1)
        g_up[:, 288 * d : 288 * d + 288] = jnp.concatenate(ups, axis=1)
    for copy in sent_z:
        copy.wait_recv()
    g_small[...] = functools.reduce(lambda a, b: a + b, [small_z[s] for s in range(PEERS)])
    mixed.three()
    ring.finish(output)
    mixed.four()
    mixed.finish(mix_wide)
    sent_mix = []
    for k, peer in enumerate(peers):
        line = pl.ds(pl.multiple_of(wrap(seq + k + 1, PEERS) * 8, 8), 8)
        sent_mix.append(copies.start(mix_wide.at[:, line], mix_land.at[seq], peer))
    mix_land[seq] = mix_wide[:, pl.ds(pl.multiple_of(seq * 8, 8), 8), :]
    for copy in sent_mix:
        copy.wait_recv()
    for half in range(2):
        upper, lower = (
            functools.reduce(lambda a, b: a + b, [mix_land[2 * k + half, p] for k in range(SIDE)]) for p in range(2)
        )
        for k, part in enumerate((upper[:, :HALF], upper[:, HALF:], lower[:, :HALF])):
            g_in[:, 1024 * k + 512 * half : 1024 * k + 512 * half + 512] = part
        g_out[:, 512 * half : 512 * half + 512] = lower[:, HALF:]
    copies.drain()


def backward(*operands):
    outs = (
        jax.ShapeDtypeStruct((ROWS, D), F32),
        jax.ShapeDtypeStruct((ROWS, D), F32),
        jax.ShapeDtypeStruct((8, 3072), F32),
        jax.ShapeDtypeStruct((8, 1024), F32),
        jax.ShapeDtypeStruct((8, 4608), F32),
        jax.ShapeDtypeStruct((8, 4608), F32),
        jax.ShapeDtypeStruct((OWN, 1024), F32),
        jax.ShapeDtypeStruct((8, 128), F32),
    )
    scratch = [
        pltpu.VMEM((2, 2, 4, 4, 64, D), BF),
        pltpu.VMEM((2, EVERY, 1536), F32),
        pltpu.VMEM((EVERY, D), BF),
        pltpu.VMEM((ROWS, D), BF),
        pltpu.VMEM((SIDE, ROWS, D), BF),
        pltpu.VMEM((4, 4, 64, 2 * SLICE), BF),
        pltpu.VMEM((4, 4, PAD, D), BF),
        *[pltpu.VMEM((2, 4, 4, 64, D), BF)] * 3,
        pltpu.VMEM((ROWS, D), F32),
        pltpu.VMEM((ROWS, D), BF),
        pltpu.VMEM((ROWS, D), F32),
        pltpu.VMEM((2, 136, D), F32),
        pltpu.VMEM((136, HALF), F32),
        pltpu.VMEM((2, ROWS, 1536), BF),
        pltpu.VMEM((2, 8, D), F32),
        pltpu.VMEM((2, 8, D), F32),
        pltpu.VMEM((8, D), F32),
        pltpu.VMEM((2, 64, D), F32),
        pltpu.VMEM((64, 2 * SLICE), F32),
        pltpu.VMEM((PAD, D), F32),
        pltpu.VMEM((PEERS, 2, 8, D), F32),
        pltpu.VMEM((PEERS, 8, 2 * SLICE), F32),
        pltpu.VMEM((4, 4, 8, 128), F32),
        pltpu.VMEM((4, 4, 8, 128), F32),
        pltpu.VMEM((4, 8, 128), F32),
        pltpu.VMEM((PEERS, 8, 128), F32),
        pltpu.VMEM((4, 8, 128), F32),
        pltpu.VMEM((8, 128), F32),
        pltpu.VMEM((128, D), BF),
        pltpu.VMEM((128, D), BF),
        pltpu.VMEM((ROWS, D), BF),
        pltpu.VMEM((ROWS, D), BF),
        *landing_shapes((), 64, 2 * SLICE, True),
        *landing_shapes((), PAD, D, False),
        *landing_shapes((2,), 64, D, True),
        pltpu.SemaphoreType.DMA((7,)),
    ]
    return call(
        backward_kernel, "backward", 1, outs, operands, scratch, 96,
        [vmem_spec()] * 5 + [any_spec()] * 7, (vmem_spec(),) * 8,
    )


def adamw(weight, grad, first, second, rate, decay):
    first_new = beta_one * first + (1.0 - beta_one) * grad
    second_new = beta_two * second + (1.0 - beta_two) * grad * grad
    first_hat = first_new / (1.0 - beta_one**STEP)
    second_hat = second_new / (1.0 - beta_two**STEP)
    weight_new = weight - rate * (
        first_hat / (jnp.sqrt(second_hat) + epsilon_adam) + decay * weight
    )
    return (weight_new, first_new, second_new)


def shards(
    inputs, cotangent, norm_gains, conv_taps, w_in, w_out, w_gate, w_up, w_down,
    first_gains, first_taps, first_in, first_out, first_gate, first_up, first_down,
    second_gains, second_taps, second_in, second_out, second_gate, second_up, second_down,
):
    seq = lax.axis_index("seq")
    rows = jnp.concatenate([norm_gains, conv_taps], axis=0).astype(BF).astype(F32)
    small = lax.dynamic_update_slice(
        jnp.zeros((8, 128), F32), jnp.pad(rows, ((0, 3), (0, 0))), (0, seq * 8)
    )
    flat = inputs.reshape(ROWS, D)
    upstream = cotangent.reshape(ROWS, D)
    back_sum, hidden, mix, projected, normed, mixer_in, held, grad_feed, grad_down, whole_rows = forward(
        w_in, w_out, w_gate, w_up, w_down, small, flat, inputs[:, 112:], upstream
    )
    out_sum, input_grad, red_in, red_out, red_gate, red_up, red_down, red_small = backward(
        back_sum, hidden, upstream, flat, whole_rows,
        mix, projected, normed, mixer_in, held, grad_feed.reshape(4, 4, 64, 2 * SLICE), grad_down,
    )
    output = (hidden + out_sum).astype(BF)
    red_small = lax.dynamic_slice(red_small, (0, seq * 8), (8, 8))
    red_gains, red_taps = red_small[:2], red_small[2:5]

    new = (
        adamw(norm_gains, red_gains, first_gains, second_gains, rate_small, 0.0),
        adamw(conv_taps, red_taps, first_taps, second_taps, rate_small, 0.0),
        adamw(w_in, red_in, first_in, second_in, rate_matrix, weight_decay),
        adamw(w_out, red_out, first_out, second_out, rate_matrix, weight_decay),
        adamw(w_gate, red_gate, first_gate, second_gate, rate_matrix, weight_decay),
        adamw(w_up, red_up, first_up, second_up, rate_matrix, weight_decay),
        adamw(w_down, red_down, first_down, second_down, rate_matrix, weight_decay),
    )
    return (
        output.reshape(2, 128, D),
        input_grad.reshape(2, 128, D),
        *[group[0] for group in new],
        *[group[1] for group in new],
        *[group[2] for group in new],
    )


def solution(mesh):
    tokens, columns, rows = P("dp", "seq", None), P(None, ("dp", "seq")), P(("dp", "seq"), None)
    weights = (columns, columns, rows, rows, rows, rows, rows)
    return jax.shard_map(
        shards,
        mesh=mesh,
        in_specs=(tokens, tokens) + weights * 3,
        out_specs=(tokens, tokens) + weights * 3,
        check_vma=False,
    )
```

```python
import functools
import types

import jax
import jax.numpy as jnp
from jax import lax
from jax.experimental import pallas as pl
from jax.experimental.pallas import tpu as pltpu
from jax.sharding import PartitionSpec as P

D = 1024
STEP = 5

epsilon_norm = 1e-05
beta_one = 0.9
beta_two = 0.95
epsilon_adam = 1e-08
rate_matrix = 0.02
rate_small = 0.3
weight_decay = 0.1

MESH = pl.DeviceIdType.MESH
BF = jnp.bfloat16
F32 = jnp.float32
SIDE = 4
PEERS = 8
OWN = 36
PACKED = 2304
SLICE = 576
WIDE = 512
VMEM_BYTES = 62 * 2**20


def place():
    dp, seq = lax.axis_index("dp"), lax.axis_index("seq")
    return lax.rem(dp, SIDE), lax.div(dp, SIDE), lax.div(seq, 2), lax.rem(seq, 2)


def wrap(value, size=SIDE):
    return lax.rem(value + size, size)


def at(x, y, z, core):
    return (y * SIDE + x, z * 2 + core)


class Copies:
    def __init__(self, send, recv):
        self.send, self.recv, self.started, self.sent = send, recv, [], set()

    def plan(self, source, target, device):
        index = len(self.started)
        assert index < self.send.shape[0]
        copy = pltpu.make_async_remote_copy(
            src_ref=source,
            dst_ref=target,
            send_sem=self.send.at[index],
            recv_sem=self.recv.at[index],
            device_id=device,
            device_id_type=MESH,
        )
        self.started.append(copy)
        return copy

    def start(self, source, target, device):
        copy = self.plan(source, target, device)
        copy.start()
        return copy

    def drain(self, some=None):
        for copy in self.started if some is None else some:
            if id(copy) not in self.sent:
                self.sent.add(id(copy))
                copy.wait_send()


def seq_peers(x, y, z, core):
    seq = z * 2 + core
    return [(y * SIDE + x, wrap(seq + k, PEERS)) for k in range(1, PEERS)]


def halver(dim, low):
    def split(ref, part):
        size = ref.shape[dim]
        places = [slice(None)] * len(ref.shape)
        places[dim] = pl.ds(0, low) if part == 0 else pl.ds(low, size - low)
        return ref.at[tuple(places)]

    return split


class RingGather:
    def __init__(self, copies, me, to, block, split):
        self.copies, self.me, self.to, self.block, self.split = copies, me, to, block, split

    def plan(self, source=None):
        source = self.block(self.me) if source is None else source
        below, above = wrap(self.me - 1), wrap(self.me + 1)

        def move(start, target, part, place):
            return self.copies.plan(self.split(start, part), self.split(target, part), self.to(place))

        mine, before, after = self.block(self.me), self.block(below), self.block(above)
        self.up = [move(source, mine, part, above) for part in range(2)]
        self.down = [move(source, mine, part, below) for part in range(2)]
        self.pass_up = move(before, before, 0, above)
        self.pass_down = move(after, after, 1, below)

    def first(self, source=None):
        if not hasattr(self, "up"):
            self.plan(source)
        self.up[0].start()
        self.down[1].start()
        self.up[1].start()
        self.down[0].start()

    def second(self):
        self.up[0].wait_recv()
        self.pass_up.start()
        self.down[1].wait_recv()
        self.pass_down.start()

    def wait_below(self):
        self.up[1].wait_recv()

    def wait_above(self):
        self.down[0].wait_recv()

    def wait_far(self):
        self.pass_up.wait_recv()
        self.pass_down.wait_recv()

    def finish(self):
        self.wait_below()
        self.wait_above()
        self.wait_far()

    def copies_made(self):
        return [*self.up, *self.down, self.pass_up, self.pass_down]


class RingReduce:
    def __init__(self, copies, me, to, block, split, landing):
        self.copies, self.me, self.to, self.block, self.split = copies, me, to, block, split
        self.low_in, self.high_in, self.plus_in, self.minus_in = landing

    def plan(self):
        far, below, above = wrap(self.me + 2), wrap(self.me - 1), wrap(self.me + 1)
        plan, split = self.copies.plan, self.split
        self.far_up = plan(split(self.block(far), 0), self.low_in, self.to(above))
        self.far_down = plan(split(self.block(far), 1), self.high_in, self.to(below))
        self.up = [plan(split(self.block(above), k), split(self.plus_in, k), self.to(above)) for k in range(2)]
        self.down = [plan(split(self.block(below), k), split(self.minus_in, k), self.to(below)) for k in range(2)]

    def first_far(self):
        self.far_up.start()
        self.far_down.start()

    def first_above(self):
        self.up[1].start()

    def first_below(self):
        self.down[0].start()

    def first(self):
        if not hasattr(self, "up"):
            self.plan()
        self.first_far()
        self.first_above()
        self.first_below()

    def second(self):
        below, above = self.block(wrap(self.me - 1)), self.block(wrap(self.me + 1))
        self.far_up.wait_recv()
        accumulate(self.split(above, 0), self.split(above, 0), self.low_in)
        self.up[0].start()
        self.far_down.wait_recv()
        accumulate(self.split(below, 1), self.split(below, 1), self.high_in)
        self.down[1].start()

    def copies_made(self):
        return [self.far_up, self.far_down, *self.up, *self.down]

    def finish(self, target=None):
        own = self.block(self.me)
        for copy in (*self.up, *self.down):
            copy.wait_recv()
        accumulate(own if target is None else target, own, self.plus_in, self.minus_in)


def accumulate(target, *sources):
    shape = target.shape
    if len(shape) > 2:
        for index in range(shape[0]):
            accumulate(target.at[index], *[source.at[index] for source in sources])
        return
    step = 16

    @pl.loop(0, shape[0] // step)
    def _(i):
        rows = pl.ds(pl.multiple_of(i * step, step), step)
        total = sources[0][rows, :].astype(F32)
        for source in sources[1:]:
            total = total + source[rows, :].astype(F32)
        target[rows, :] = total.astype(target.dtype)


def columns_of(seq, dp_count=16):
    return [(288 * d + OWN * seq, 36 * d) for d in range(dp_count)]


def dot(a, b, dims=((1,), (0,))):
    return lax.dot_general(a, b, (dims, ((), ())), preferred_element_type=F32)


NT = ((1,), (1,))
TN = ((0,), (0,))
ROWS = 256
PAIR = 512
EVERY = 272
HALF = 512


def by_rows(ref, which, part):
    start, size = (32 * which, 32) if part is None else (32 * which + 16 * part, 16)
    lead = [slice(None)] * (len(ref.shape) - 2)
    return ref.at[(*lead, pl.ds(start, size), slice(None))]


def by_columns(ref, which, part):
    first, size = ((0, 1152), (0, 640), (640, 512))[0 if part is None else part + 1]
    lead = [slice(None)] * (len(ref.shape) - 2)
    return ref.at[(*lead, slice(None), pl.ds(1152 * which + first, size))]


def visit(z, k):
    return wrap(z + k + lax.div(k, 2) * (5 - 2 * k))


def turn_of(z, chip):
    ahead = wrap(chip - z)
    return ahead + lax.div(ahead, 2) * (5 - 2 * ahead)


class PlaneGather:
    def __init__(self, copies, spot, view, halves, block, split):
        x, y, z, core = spot
        to_x, to_y = (lambda i: at(i, y, z, core)), (lambda i: at(x, i, z, core))
        everything, fours = slice(None), halver(0, 2)
        self.x, self.y, self.view, self.halves = x, y, view, halves
        self.row_x = RingGather(copies, x, to_x, lambda i: halves(view(y, i), 0, None), split)
        self.row_y = RingGather(copies, y, to_y, lambda i: halves(view(i, x), 1, None), split)
        self.all_y = RingGather(copies, y, to_y, lambda i: halves(view(i, everything), 0, None), fours)
        self.all_x = RingGather(copies, x, to_x, lambda i: halves(view(everything, i), 1, None), fours)
        self.row_x.plan(halves(block, 0, None))
        self.row_y.plan(halves(block, 1, None))
        self.all_y.plan()
        self.all_x.plan()

    def one(self):
        self.row_x.first()
        self.row_y.first()

    def two(self):
        self.row_x.second()
        self.row_y.second()

    def three(self):
        self.row_x.finish()
        self.all_y.first()
        self.row_y.finish()
        self.all_x.first()

    def four(self):
        self.all_y.second()
        self.all_x.second()

    def finish(self):
        self.all_y.finish()
        self.all_x.finish()

    def copies(self):
        return [copy for ring in (self.row_x, self.row_y, self.all_y, self.all_x) for copy in ring.copies_made()]

    def group(self, which, step):
        everything = slice(None)
        if which == 0:
            return self.halves(self.view(wrap(self.y + step), everything), 0, None)
        return self.halves(self.view(everything, wrap(self.x + step)), 1, None)


ORDERS = (("x", "y", "z"), ("y", "z", "x"), ("z", "x", "y"))


def cube_spots(spot, order):
    x, y, z, core = spot
    own = {"x": x, "y": y, "z": z}
    to = {
        "x": lambda i: at(i, y, z, core),
        "y": lambda i: at(x, i, z, core),
        "z": lambda i: at(x, y, i, core),
    }

    def view(ref, **places):
        return ref.at[tuple(places.get(axis, own[axis]) for axis in ("y", "x", "z"))]

    return [own[axis] for axis in order], [to[axis] for axis in order], view


def cube_rings(spot, order, ref, make):
    (a, b, c), (to_a, to_b, to_c), view = cube_spots(spot, order)
    one, two, three = order
    everything = slice(None)
    place_of = {"y": 0, "x": 1, "z": 2}
    first = make(a, to_a, lambda i: view(ref, **{one: i}), halver(-1, ref.shape[-1] // 2))
    second = make(b, to_b, lambda i: view(ref, **{one: everything, two: i}), halver(0, 2))
    third = make(
        c, to_c,
        lambda i: view(ref, **{one: everything, two: everything, three: i}),
        halver(0 if place_of[two] < place_of[one] else 1, 2),
    )
    return first, second, third


def small_rows(small_all):
    pieces = [small_all[d // 4, d % 4][:, :64] for d in range(16)]
    return jnp.concatenate(pieces, axis=1)


def normalize(rows, gain):
    inverse = lax.rsqrt(jnp.mean(rows * rows, axis=-1, keepdims=True) + epsilon_norm)
    return rows * inverse * gain


def extend(extended, projected, half, sequence):
    first = pl.ds(ROWS + 8 * sequence, 8)
    main = pl.ds(128 * sequence, 128)
    extended[0:8, :] = projected[half, first, :HALF] * projected[half, first, 1024:]
    extended[8:136, :] = projected[half, main, :HALF] * projected[half, main, 1024:]


def convolve(extended, taps):
    return taps[0:1] * extended[6:134, :] + taps[1:2] * extended[7:135, :] + taps[2:3] * extended[8:136, :]


def half_lanes(half):
    return pl.ds(pl.multiple_of(half * HALF, HALF), HALF)


class PlaneReduce:
    def __init__(self, copies, spot, view, halves, split, landings):
        x, y, z, core = spot
        to_x, to_y = (lambda i: at(i, y, z, core)), (lambda i: at(x, i, z, core))
        everything, fours = slice(None), halver(0, 2)
        self.halves = halves
        self.all_y = RingReduce(copies, y, to_y, lambda i: halves(view(i, everything), 0, None), fours, landings[0:4])
        self.all_x = RingReduce(copies, x, to_x, lambda i: halves(view(everything, i), 1, None), fours, landings[4:8])
        self.row_x = RingReduce(copies, x, to_x, lambda i: halves(view(y, i), 0, None), split, landings[8:12])
        self.row_y = RingReduce(copies, y, to_y, lambda i: halves(view(i, x), 1, None), split, landings[12:16])

    def one(self):
        self.all_y.first()
        self.all_x.first()

    def two(self):
        self.all_y.second()
        self.all_x.second()

    def three(self):
        self.all_y.finish()
        self.row_x.first()
        self.all_x.finish()
        self.row_y.first()

    def four(self):
        self.row_x.second()
        self.row_y.second()

    def finish(self, target):
        self.row_x.finish(self.halves(target, 0, None))
        self.row_y.finish(self.halves(target, 1, None))


def plane_landings(ref):
    wide = lambda count, blocks, rows: ref.reshape(count, blocks, rows, 1152)
    single = lambda rows: ref.reshape(2048 // rows, rows, 1152)
    fed, downs = [], []
    for k in range(2):
        fed += [wide(32, 2, 32).at[8 + 2 * k], wide(32, 2, 32).at[9 + 2 * k]]
        fed += [wide(16, 4, 32).at[2 * k], wide(16, 4, 32).at[2 * k + 1]]
        downs += [wide(64, 2, 16).at[38 + 2 * k], wide(64, 2, 16).at[39 + 2 * k]]
        downs += [wide(32, 4, 16).at[15 + 2 * k], wide(32, 4, 16).at[16 + 2 * k]]
    for k in range(2):
        fed += [single(16).at[56 + 2 * k], single(16).at[57 + 2 * k], single(32).at[24 + 2 * k], single(32).at[25 + 2 * k]]
        downs += [single(16).at[88 + 2 * k, :, pl.ds(0, 640)], single(16).at[89 + 2 * k, :, pl.ds(0, 512)]]
        downs += [single(16).at[84 + 2 * k], single(16).at[85 + 2 * k]]
    return fed, downs


def cube_landings(ref, order):
    width = ref.shape[-1]
    place_of = {"y": 0, "x": 1, "z": 2}
    halved = (2, 4) if place_of[order[1]] < place_of[order[0]] else (4, 2)
    single, half = ref.reshape(64, 16, width), pl.ds(0, width // 2)
    first = [single.at[60, :, half], single.at[61, :, half], single.at[62], single.at[63]]
    pairs, fours = ref.reshape(32, 2, 16, width), ref.reshape(16, 4, 16, width)
    second = [pairs.at[24], pairs.at[25], fours.at[13], fours.at[14]]
    lows, wholes = ref.reshape(8, *halved, 16, width), ref.reshape(4, 4, 4, 16, width)
    third = [lows.at[4], lows.at[5], wholes.at[0], wholes.at[1]]
    return first, second, third


def local_copies(semaphores):
    count = iter(range(semaphores.shape[0]))

    def start(source, target):
        copy = pltpu.make_async_copy(source, target, semaphores.at[next(count)])
        copy.start()
        return copy

    return start


OPERANDS = ("w_in", "w_out", "w_gate", "w_up", "w_down", "gains", "taps", "inputs", "cotangent")
RESULTS = {
    "output": ((2, 128, D), BF),
    "input_grad": ((2, 128, D), F32),
    "g_in": ((8, 3072), F32),
    "g_out": ((8, 1024), F32),
    "g_gate": ((8, 4608), F32),
    "g_up": ((8, 4608), F32),
    "g_down": ((OWN, D), F32),
    "g_small": ((8, 128), F32),
}
SCRATCH = {
    "w_in": ((8, 3072), F32),
    "w_out": ((8, 1024), F32),
    "w_gate": ((8, 4608), F32),
    "w_up": ((8, 4608), F32),
    "w_down": ((OWN, D), F32),
    "tile": ((8, 128), F32),
    "inputs": ((2, 128, D), BF),
    "mix": ((2, 4, 4, 64, 2048), BF),
    "feed": ((4, 4, 64, 2 * SLICE), BF),
    "down": ((4, 4, 16, PACKED), BF),
    "small_all": ((4, 4, 8, 128), F32),
    "edge_in": ((2, 16, D), BF),
    "tokens": ((SIDE, 2, ROWS, D), BF),
    "grads": ((SIDE, 2, ROWS, D), BF),
    "mix_send": ((2, 16, D), BF),
    "feed_send": ((PEERS, 16, 640), BF),
    "mix_got": ((PEERS, 16, D), BF),
    "feed_got": ((PEERS, 16, 640), BF),
    "small_got": ((PEERS, 8, 128), F32),
    "mix_block": ((64, 2048), BF),
    "feed_block": ((64, 2 * SLICE), BF),
    "down_block": ((16, PACKED), BF),
    "small_send": ((8, 128), F32),
    "rows": ((8, D), F32),
    "normed": ((EVERY, D), BF),
    "projected": ((2, EVERY, 1536), F32),
    "extended": ((136, HALF), F32),
    "mixer_in": ((ROWS, D), BF),
    "hidden": ((ROWS, D), F32),
    "normed_two": ((ROWS, D), BF),
    "down_rows": ((SLICE, D), BF),
    "narrow_wide": ((160, D), F32),
    "value": ((PAIR, 2 * SLICE), F32),
    "grad_active": ((PAIR, SLICE), F32),
    "active": ((2048, SLICE), BF),
    "grad_value": ((2048, 2 * SLICE), BF),
    "part": ((SIDE, 2, ROWS, D), BF),
    "part_out": ((SIDE, 2, ROWS, D), BF),
    "landing": ((SIDE, ROWS, D), BF),
    "landing_left": ((SIDE, ROWS, HALF), BF),
    "landing_right": ((SIDE, ROWS, HALF), BF),
    "low_in": ((128, D), BF),
    "high_in": ((128, D), BF),
    "plus_in": ((ROWS, D), BF),
    "minus_in": ((ROWS, D), BF),
    "low_out": ((128, D), BF),
    "high_out": ((128, D), BF),
    "plus_out": ((ROWS, D), BF),
    "minus_out": ((ROWS, D), BF),
    "down_part": ((SLICE, 256), F32),
    "down_tail": ((16, 16, 256), F32),
    "grad_conv": ((2, 136, D), F32),
    "grad_x": ((2, ROWS, HALF), BF),
    "edge_send": ((2, 8, D), F32),
    "edge_got": ((2, 8, D), F32),
    "sums": ((8, D), F32),
    "mix_wide": ((16, 2048), F32),
    "feed_wide": ((64, 2 * SLICE), F32),
    "down_wide": ((16, PACKED), F32),
    "mix_land": ((2, 8, 2048), F32),
    "feed_land": ((PEERS, 8, 2 * SLICE), F32),
    "small": ((4, 4, 8, 128), F32),
    "small_y": ((4, 4, 8, 128), F32),
    "small_x": ((4, 8, 128), F32),
    "small_z": ((PEERS, 8, 128), F32),
    "small_one": ((4, 8, 128), F32),
    "small_two": ((8, 128), F32),
    "g_small": ((8, 128), F32),
}
COPIES = 352


def step_kernel(*refs):
    count = len(OPERANDS)
    given = types.SimpleNamespace(**dict(zip(OPERANDS, refs)))
    result = types.SimpleNamespace(**dict(zip(RESULTS, refs[count:])))
    count += len(RESULTS)
    m = types.SimpleNamespace(**dict(zip(SCRATCH, refs[count:])))
    ready, load_sem, save_sem, send, recv = refs[count + len(SCRATCH) :]

    spot = x, y, z, core = place()
    seq = z * 2 + core
    copies = Copies(send, recv)
    peers = seq_peers(x, y, z, core)
    across = [at(wrap(x + k), y, z, core) for k in range(1, SIDE)]
    along = [at(x, wrap(y + k), z, core) for k in range(1, SIDE)]
    partner = at(x, y, z, 1 - core)
    load = local_copies(load_sem)
    loads = {
        "w_in": load(given.w_in, m.w_in),
        "w_out": load(given.w_out, m.w_out),
        "w_gate": load(given.w_gate, m.w_gate),
        "w_up": load(given.w_up, m.w_up),
        "w_down": load(given.w_down, m.w_down),
        "inputs": load(given.inputs, m.inputs),
        "cotangent": load(given.cotangent, m.grads.at[z, core]),
    }
    barrier = pltpu.get_barrier_semaphore()
    for device in peers + across + along:
        pl.semaphore_signal(barrier, inc=1, device_id=device, device_id_type=MESH)

    def to_z(i):
        return at(x, y, i, core)

    loads["w_in"].wait()
    loads["w_out"].wait()
    for half in range(2):
        parts = [m.w_out[:, 512 * half : 512 * half + 512]]
        parts += [m.w_in[:, 1024 * k + 512 * half : 1024 * k + 512 * half + 512] for k in range(3)]
        upper = jnp.concatenate(parts[:2], axis=1)
        lower = jnp.concatenate(parts[2:], axis=1)
        m.mix_send[half] = jnp.concatenate([upper, lower], axis=0).astype(BF)
    pl.semaphore_wait(barrier, len(peers + across + along))
    mix_copies = []
    for k, peer in enumerate(peers):
        other = wrap(seq + k + 1, PEERS)
        mix_copies.append(copies.start(m.mix_send.at[lax.rem(other, 2)], m.mix_got.at[seq], peer))
    m.mix_got[seq] = m.mix_send[core]
    m.tile[...] = jnp.zeros_like(m.tile)
    m.tile[0:2, 0:8] = given.gains[...].astype(BF).astype(F32)
    m.tile[2:5, 0:8] = given.taps[...].astype(BF).astype(F32)
    m.small_got[seq] = pltpu.roll(m.tile[...], seq * 8, 1)
    small_copies = [copies.start(m.small_got.at[seq], m.small_got.at[seq], peer) for peer in peers]
    edge_copy = copies.start(
        given.inputs.at[:, pl.ds(112, 16)], m.edge_in, (y * SIDE + x, wrap(seq + 1, PEERS))
    )
    mixed = PlaneGather(copies, spot, lambda i, j: m.mix.at[core, i, j], by_rows, m.mix_block, halver(-2, 16))
    fed = PlaneGather(copies, spot, lambda i, j: m.feed.at[i, j], by_rows, m.feed_block, halver(-2, 16))
    downs = PlaneGather(copies, spot, lambda i, j: m.down.at[i, j], by_columns, m.down_block, halver(-1, 640))
    ring = RingGather(
        copies, z, to_z,
        lambda i: m.grads.at[i, core],
        halver(0, 128),
    )
    ring.plan(given.cotangent)

    for copy in mix_copies:
        copy.wait_recv()
    for k in range(4):
        a, b = m.mix_got[2 * k].astype(F32), m.mix_got[2 * k + 1].astype(F32)
        line = slice(16 * k, 16 * k + 16)
        m.mix_block[line, :1024] = jnp.concatenate([a[:8], b[:8]], axis=0).astype(BF)
        m.mix_block[line, 1024:] = jnp.concatenate([a[8:], b[8:]], axis=0).astype(BF)
    mixed.one()
    m.mix[core, y, x] = m.mix_block[...]
    ring.first()
    cotangent_ring = ring
    grads_passed = [copies.start(given.cotangent, m.grads.at[z, core], partner)]

    def slices(which):
        for s in which:
            gate = jnp.concatenate([m.w_gate[:, a : a + OWN] for a, _ in columns_of(s)], axis=1)
            up = jnp.concatenate([m.w_up[:, a : a + OWN] for a, _ in columns_of(s)], axis=1)
            tail = jnp.concatenate([gate[:, WIDE:], up[:, WIDE:]], axis=1)
            upper = jnp.concatenate([gate[:, :WIDE], up[:, :128]], axis=1)
            lower = jnp.concatenate([up[:, 128:WIDE], tail, jnp.zeros((8, 128), F32)], axis=1)
            m.feed_send[s] = jnp.concatenate([upper, lower], axis=0).astype(BF)

    loads["w_gate"].wait()
    loads["w_up"].wait()
    slices(range(0, 4))
    mixed.two()
    slices(range(4, 8))
    feed_copies = []
    for k, peer in enumerate(peers):
        other = wrap(seq + k + 1, PEERS)
        feed_copies.append(copies.start(m.feed_send.at[other], m.feed_got.at[seq], peer))
    m.feed_got[seq] = m.feed_send[seq]
    for copy in small_copies:
        copy.wait_recv()
    m.small_send[...] = functools.reduce(lambda a, b: a + b, [m.small_got[s] for s in range(PEERS)])
    small_x = [copies.start(m.small_send, m.small_all.at[y, x], device) for device in across]
    m.small_all[y, x] = m.small_send[...]
    mixed.three()
    mix_passed = []

    def pass_on(step):
        for which in range(2):
            part = mixed.group(which, step)
            mix_passed.append(copies.start(part, part, partner))

    pass_on(0)
    for copy in small_x:
        copy.wait_recv()
    small_y = [copies.start(m.small_all.at[y], m.small_all.at[y], device) for device in along]
    loads["w_down"].wait()
    for i in range(4):
        m.narrow_wide[4 * i : 4 * i + 4, 0:256] = m.w_down[32:36, 256 * i : 256 * i + 256]
    m.down_block[:, 0:1024] = m.w_down[0:16, :].astype(BF)
    m.down_block[:, 1024:2048] = m.w_down[16:32, :].astype(BF)
    m.down_block[:, 2048:PACKED] = m.narrow_wide[0:16, 0:256].astype(BF)
    m.down[y, x] = m.down_block[...]
    for copy in feed_copies:
        copy.wait_recv()
    for k in range(4):
        a, b = m.feed_got[2 * k].astype(F32), m.feed_got[2 * k + 1].astype(F32)
        line = slice(16 * k, 16 * k + 16)
        m.feed_block[line, :640] = jnp.concatenate([a[:8], b[:8]], axis=0).astype(BF)
        m.feed_block[line, 640:] = jnp.concatenate([a[8:, :512], b[8:, :512]], axis=0).astype(BF)
    m.feed[y, x] = m.feed_block[...]
    for copy in small_y:
        copy.wait_recv()
    m.rows[...] = small_rows(m.small_all)
    loads["inputs"].wait()
    for q in range(2):
        m.normed[128 * q : 128 * q + 128, :] = normalize(m.inputs[q].astype(F32), m.rows[0:1, :]).astype(BF)
    edge_copy.wait_recv()
    inside = (seq > 0).astype(F32)
    earlier = [normalize(m.edge_in[q].astype(F32)[8:], m.rows[0:1, :]) * inside for q in range(2)]
    m.normed[ROWS:EVERY, :] = jnp.concatenate(earlier, axis=0).astype(BF)
    ring.second()
    mixed.four()
    downs.one()
    fed.one()
    mixed.all_y.wait_below()
    mixed.all_x.wait_below()
    pass_on(-1)
    mixed.all_y.wait_above()
    mixed.all_x.wait_above()
    pass_on(1)
    downs.two()
    fed.two()
    downs.three()
    fed.three()
    mixed.all_y.wait_far()
    mixed.all_x.wait_far()
    pass_on(2)
    ring.finish()
    for step in (1, 3, 2):
        chunk = m.grads.at[wrap(z + step), core]
        grads_passed.append(copies.start(chunk, chunk, partner))

    for turn in range(2):
        if turn == 1:
            for copy in mix_passed:
                copy.wait_recv()
        half = core if turn == 0 else 1 - core
        m.projected[half] = dot(m.normed[...], m.mix.at[half].reshape(D, 2048)[:, HALF:])
        lanes = half_lanes(half)
        for q in range(2):
            main = slice(128 * q, 128 * q + 128)
            extend(m.extended, m.projected, half, q)
            convolved = convolve(m.extended, m.rows[2:5, lanes])
            m.mixer_in[main, lanes] = (m.projected[half, main, HALF:1024] * convolved).astype(BF)
    weights = [m.mix.at[half].reshape(D, 2048) for half in range(2)]
    for half in range(2):
        lanes = slice(HALF * half, HALF * half + HALF)
        mixed_out = dot(m.mixer_in[...], weights[half][:, :HALF])
        for q in range(2):
            main = slice(128 * q, 128 * q + 128)
            m.hidden[main, lanes] = m.inputs[q, :, lanes].astype(F32) + mixed_out[main]
    m.normed_two[...] = normalize(m.hidden[...], m.rows[1:2, :]).astype(BF)

    around = RingGather(
        copies, z, to_z,
        lambda i: m.tokens.at[i, core],
        halver(0, 128),
    )
    around.plan(m.normed_two)
    passed = [copies.plan(m.normed_two, m.tokens.at[z, core], partner)]
    for step in (1, 3, 2):
        chunk = m.tokens.at[wrap(z + step), core]
        passed.append(copies.plan(chunk, chunk, partner))
    around.first()
    passed[0].start()
    m.tokens[z, core] = m.normed_two[...]
    downs.four()
    fed.four()
    gives, gives_left, gives_right = [], [], []
    for k in range(SIDE):
        theirs = m.part_out.at[k, 1 - core]
        gives.append(copies.plan(m.part.at[k, 1 - core], m.landing.at[k], partner))
        gives_left.append(copies.plan(theirs.at[:, 0:HALF], m.landing_left.at[k], partner))
        gives_right.append(copies.plan(theirs.at[:, HALF:D], m.landing_right.at[k], partner))
    reduce = RingReduce(
        copies, z, to_z,
        lambda i: m.part.at[turn_of(z, i), core],
        halver(0, 128),
        (m.low_in, m.high_in, m.plus_in, m.minus_in),
    )
    reduce.plan()
    downs.finish()
    for i in range(SIDE):
        for d in range(SIDE):
            packed = m.down[i, d].astype(F32)
            m.narrow_wide[OWN * d : OWN * d + 16, :] = packed[:, 0:1024]
            m.narrow_wide[OWN * d + 16 : OWN * d + 32, :] = packed[:, 1024:2048]
            for k in range(4):
                m.narrow_wide[OWN * d + 32 : OWN * d + 36, 256 * k : 256 * k + 256] = packed[4 * k : 4 * k + 4, 2048:]
        m.down_rows[144 * i : 144 * i + 144, :] = m.narrow_wide[0:144, :].astype(BF)
    for copy in grads_passed:
        copy.wait_recv()
    loads["cotangent"].wait()
    fed.finish()
    feed = m.feed.reshape(D, 2 * SLICE)
    around.second()
    around.wait_above()
    passed[1].start()
    around.wait_below()
    passed[2].start()

    @pl.loop(0, SIDE)
    def _(k):
        @pl.when(k == 0)
        def _():
            passed[0].wait_recv()

        @pl.when(k == 1)
        def _():
            passed[1].wait_recv()

        @pl.when(k == 2)
        def _():
            passed[2].wait_recv()
            around.wait_far()
            passed[3].start()

        @pl.when(k == 3)
        def _():
            passed[3].wait_recv()

        chip = visit(z, k)
        m.value[...] = dot(m.tokens.at[chip].reshape(PAIR, D)[...], feed[...])
        m.grad_active[...] = dot(m.grads.at[chip].reshape(PAIR, D)[...], m.down_rows[...], NT)
        base = chip * PAIR

        @pl.loop(0, PAIR // 64)
        def _(r):
            line = pl.ds(pl.multiple_of(r * 64, 64), 64)
            target = pl.ds(pl.multiple_of(base + r * 64, 64), 64)
            tail = m.value[line, 1024:1152]
            ends = []
            for gate, up, back, where in (
                (m.value[line, :WIDE], m.value[line, WIDE:1024], m.grad_active[line, :WIDE], slice(0, WIDE)),
                (tail[:, :64], tail[:, 64:], m.grad_active[line, WIDE:], slice(WIDE, SLICE)),
            ):
                sigmoid = jax.nn.sigmoid(gate)
                soft = gate * sigmoid
                m.active[target, where] = (soft * up).astype(BF)
                grad_up = (back * soft).astype(BF)
                grad_gate = (back * up * (sigmoid * (1.0 + gate * (1.0 - sigmoid)))).astype(BF)
                ends.append((grad_gate, grad_up))
            m.grad_value[target, :WIDE] = ends[0][0]
            m.grad_value[target, WIDE:1024] = ends[0][1]
            m.grad_value[target, 1024:1088] = ends[1][0]
            m.grad_value[target, 1088:1152] = ends[1][1]

        lines = pl.ds(pl.multiple_of(base, PAIR), PAIR)
        m.part.at[k].reshape(PAIR, D)[...] = dot(m.grad_value[lines, :], feed[...], NT).astype(BF)
        for step in range(SIDE):
            @pl.when(k == step)
            def _(step=step):
                gives[step].start()
        m.part_out.at[k].reshape(PAIR, D)[...] = dot(m.active[lines, :], m.down_rows[...]).astype(BF)
        for step in range(SIDE):
            @pl.when(k == step)
            def _(step=step):
                gives_left[step].start()
                gives_right[step].start()
                gives[step].wait_recv()
                accumulate(m.part.at[step, core], m.part.at[step, core], m.landing.at[step])
                if step == 1:
                    reduce.first_above()
                if step == 2:
                    reduce.first_below()
                if step == 3:
                    reduce.first_far()

    copies.drain(fed.copies())
    copies.drain(downs.copies())
    every_grad, every_token = m.grads.reshape(2048, D), m.tokens.reshape(2048, D)

    @pl.loop(0, 4)
    def _(n):
        columns = pl.ds(pl.multiple_of(n * 256, 256), 256)
        feed[columns, :] = dot(every_token[:, columns], m.grad_value[...], TN).astype(BF)

    plane_neighbours = [at(wrap(x + 1), y, z, core), at(wrap(x - 1), y, z, core)]
    plane_neighbours += [at(x, wrap(y + 1), z, core), at(x, wrap(y - 1), z, core)]
    for device in plane_neighbours:
        pl.semaphore_signal(ready.at[0], inc=1, device_id=device, device_id_type=MESH)
    reduce.second()

    def down_columns(n):
        columns = slice(256 * n, 256 * n + 256)
        m.down_part[...] = dot(m.active[...], every_grad[:, columns], TN)
        for d in range(16):
            block = m.down.at[d // 4, d % 4]
            block[:, columns] = m.down_part[OWN * d : OWN * d + 16, :].astype(BF)
            block[:, 1024 + 256 * n : 1280 + 256 * n] = m.down_part[OWN * d + 16 : OWN * d + 32, :].astype(BF)
            m.down_tail[d, 4 * n : 4 * n + 4, :] = m.down_part[OWN * d + 32 : OWN * d + 36, :]

    fed_landings, down_landings = plane_landings(m.grad_value)
    fed = PlaneReduce(copies, spot, lambda i, j: m.feed.at[i, j], by_rows, halver(-2, 16), fed_landings)
    downs = PlaneReduce(copies, spot, lambda i, j: m.down.at[i, j], by_columns, halver(-1, 640), down_landings)
    down_columns(0)
    pl.semaphore_wait(ready.at[0], len(plane_neighbours))
    fed.one()
    for n in range(1, 4):
        down_columns(n)
    for d in range(16):
        m.down[d // 4, d % 4, :, 2048:PACKED] = m.down_tail[d].astype(BF)
    downs.one()
    for k in range(SIDE):
        gives_left[k].wait_recv()
        gives_right[k].wait_recv()
        ours = m.part_out.at[k, core]
        accumulate(ours.at[:, 0:HALF], ours.at[:, 0:HALF], m.landing_left.at[k])
        accumulate(ours.at[:, HALF:D], ours.at[:, HALF:D], m.landing_right.at[k])
    ring = RingReduce(
        copies, z, to_z,
        lambda i: m.part_out.at[turn_of(z, i), core],
        halver(0, 128),
        (m.low_out, m.high_out, m.plus_out, m.minus_out),
    )
    ring.first()
    grad_hidden = m.value.at[0:ROWS, 0:D]
    grad_mixer = m.value.at[ROWS : 2 * ROWS, 0:D]
    reduce.finish(grad_hidden)

    copies.drain(gives + gives_left + gives_right + reduce.copies_made() + around.copies_made() + passed)
    copies.drain(grads_passed)
    copies.drain(cotangent_ring.copies_made())
    neighbours = plane_neighbours + [at(x, y, wrap(z + 1), core), at(x, y, wrap(z - 1), core), partner]
    for device in neighbours:
        pl.semaphore_signal(ready.at[1], inc=1, device_id=device, device_id_type=MESH)

    sum_blocks = m.grads.reshape(2, 4, 4, 4, 16, D)
    sum_views = [sum_blocks.at[0]] + [sum_blocks.at[1, :, :, :, :, pl.ds(HALF * k, HALF)] for k in range(2)]

    def flat_views(ref):
        flat = ref.reshape(2, D, D)
        return [flat.at[0], flat.at[1, :, pl.ds(0, HALF)], flat.at[1, :, pl.ds(HALF, HALF)]]

    sum_flat, give_flat, got_flat = flat_views(m.grads), flat_views(m.tokens), flat_views(m.part)
    cubes = []
    for ref, buffer, order in zip(sum_views, (m.landing, m.landing_left, m.landing_right), ORDERS):
        lands = iter(cube_landings(buffer, order))

        def make(me, to, block, split, lands=lands):
            return RingReduce(copies, me, to, block, split, next(lands))

        cubes.append(cube_rings(spot, order, ref, make))
    save = local_copies(save_sem)
    saves = []

    m.sums[...] = jnp.zeros_like(m.sums)
    narrow = m.normed_two

    @pl.loop(0, 8)
    def _(n):
        line = pl.ds(pl.multiple_of(n * 32, 32), 32)
        tokens = m.hidden[line, :]
        inverse = lax.rsqrt(jnp.mean(tokens * tokens, axis=-1, keepdims=True) + epsilon_norm)
        scaled = tokens * inverse
        upstream = grad_hidden[line, :]
        m.sums[1:2, :] += jnp.sum(upstream * scaled, axis=0, keepdims=True)
        weighted = upstream * m.rows[1:2, :]
        total = m.grads[z, core, line, :].astype(F32) + inverse * (
            weighted - scaled * jnp.mean(weighted * scaled, axis=-1, keepdims=True)
        )
        grad_hidden[line, :] = total
        narrow[line, :] = total.astype(BF)

    grad_mixer[...] = dot(narrow[:, :HALF], weights[0][:, :HALF], NT) + dot(narrow[:, HALF:], weights[1][:, :HALF], NT)
    for q in range(2):
        for half in range(2):
            lanes = slice(HALF * half, HALF * half + HALF)
            start = slice(128 * q, 128 * q + 8)
            m.edge_send[q, :, lanes] = grad_mixer[start, lanes] * m.projected[half, start, HALF:1024]
    edge_copy = copies.start(m.edge_send, m.edge_got, (y * SIDE + x, wrap(seq - 1, PEERS)))
    fed.two()
    grad_bc = m.grad_value.reshape(8, ROWS, 2 * SLICE)
    for half in range(2):
        lanes = slice(HALF * half, HALF * half + HALF)
        for q in range(2):
            main = slice(128 * q, 128 * q + 128)
            extend(m.extended, m.projected, half, q)
            upstream = grad_mixer[main, lanes]
            grad_bc[6 + half, main, HALF:D] = (upstream * convolve(m.extended, m.rows[2:5, lanes])).astype(BF)
            back = upstream * m.projected[half, main, HALF:1024]
            m.grad_conv[q, 0:128, lanes] = back
            for k in range(3):
                m.sums[2 + k : 3 + k, lanes] += jnp.sum(back * m.extended[6 + k : 134 + k, :], axis=0, keepdims=True)
    ring.second()
    edge_copy.wait_recv()
    inside = (seq < PEERS - 1).astype(F32)
    for q in range(2):
        m.grad_conv[q, 128:136, :] = m.edge_got[q] * inside
        main = slice(128 * q, 128 * q + 128)
        for half in range(2):
            lanes = slice(HALF * half, HALF * half + HALF)
            taps = m.rows[2:5, lanes]
            gated = (
                taps[2:3] * m.grad_conv[q, 0:128, lanes]
                + taps[1:2] * m.grad_conv[q, 1:129, lanes]
                + taps[0:1] * m.grad_conv[q, 2:130, lanes]
            )
            grad_bc[6 + half, main, 0:HALF] = (gated * m.projected[half, main, 1024:]).astype(BF)
            m.grad_x[half, main, :] = (gated * m.projected[half, main, :HALF]).astype(BF)
    downs.two()

    before = m.normed.at[0:ROWS]
    given_parts = []
    for targets, half in ((give_flat, 1 - core), (sum_flat, core)):
        back, back_x, back_out = grad_bc.at[6 + half], m.grad_x.at[half], narrow.at[:, half_lanes(half)]

        @pl.loop(0, 4)
        def _(n, targets=targets, back=back, back_x=back_x, back_out=back_out):
            columns = pl.ds(pl.multiple_of(n * 256, 256), 256)
            left = before[:, columns]
            first = dot(left, back[:, 0:D], TN).astype(BF)
            targets[0][columns, HALF:D] = first[:, :HALF]
            targets[1][columns, :] = first[:, HALF:]
            targets[2][columns, :] = dot(left, back_x[...], TN).astype(BF)
            targets[0][columns, 0:HALF] = dot(m.mixer_in[:, columns], back_out[...], TN).astype(BF)

        if targets is give_flat:
            pl.semaphore_wait(ready.at[1], len(neighbours))
            for part in range(3):
                given_parts.append(copies.start(give_flat[part], got_flat[part], partner))
    for part in range(3):
        given_parts[part].wait_recv()
        accumulate(sum_flat[part], sum_flat[part], got_flat[part])
        cubes[part][2].first()
    fed.three()
    downs.three()

    grad_mixer[...] = dot(grad_bc[6, :, 0:D], weights[0][:, HALF:1536], NT)
    grad_mixer[...] += dot(grad_bc[7, :, 0:D], weights[1][:, HALF:1536], NT)
    grad_mixer[...] += dot(m.grad_x[0], weights[0][:, 1536:], NT) + dot(m.grad_x[1], weights[1][:, 1536:], NT)

    @pl.loop(0, 8)
    def _(n):
        line = pl.ds(pl.multiple_of(n * 32, 32), 32)
        tokens = m.inputs.reshape(ROWS, D)[line, :].astype(F32)
        inverse = lax.rsqrt(jnp.mean(tokens * tokens, axis=-1, keepdims=True) + epsilon_norm)
        scaled = tokens * inverse
        upstream = grad_mixer[line, :]
        m.sums[0:1, :] += jnp.sum(upstream * scaled, axis=0, keepdims=True)
        weighted = upstream * m.rows[0:1, :]
        grad_mixer[line, :] = grad_hidden[line, :] + inverse * (
            weighted - scaled * jnp.mean(weighted * scaled, axis=-1, keepdims=True)
        )

    for q in range(2):
        saves.append(save(grad_mixer.at[128 * q : 128 * q + 128], result.input_grad.at[q]))

    for part in range(3):
        cubes[part][2].second()
    fed.four()
    downs.four()

    for d in range(16):
        tile = jnp.concatenate([m.sums[:, 64 * d : 64 * d + 64], jnp.zeros((8, 64), F32)], axis=1)
        m.small[d // 4, d % 4] = tile
    sent_y = [
        copies.start(m.small.at[wrap(y + k)], m.small_y.at[k], device) for k, device in zip(range(1, SIDE), along)
    ]
    for copy in sent_y:
        copy.wait_recv()
    for i in range(SIDE):
        total = m.small[y, i]
        for k in range(1, SIDE):
            total = total + m.small_y[k, i]
        m.small_one[i] = total
    sent_x = [
        copies.start(m.small_one.at[wrap(x + k)], m.small_x.at[k], device)
        for k, device in zip(range(1, SIDE), across)
    ]
    for part in (1, 2, 0):
        cubes[part][2].finish()
        cubes[part][1].first()
    fed.finish(m.feed_wide)
    sent_feed = []
    for k, peer in enumerate(peers):
        line = pl.ds(pl.multiple_of(wrap(seq + k + 1, PEERS) * 8, 8), 8)
        sent_feed.append(copies.start(m.feed_wide.at[line], m.feed_land.at[seq], peer))
    m.feed_land[seq] = m.feed_wide[pl.ds(pl.multiple_of(seq * 8, 8), 8), :]
    downs.finish(m.down_wide)
    m.w_down[0:16, :] = m.down_wide[:, 0:1024]
    m.w_down[16:32, :] = m.down_wide[:, 1024:2048]
    for i in range(4):
        m.w_down[32:36, 256 * i : 256 * i + 256] = m.down_wide[4 * i : 4 * i + 4, 2048:PACKED]
    saves.append(save(m.w_down, result.g_down))
    for copy in sent_x:
        copy.wait_recv()
    total = m.small_one[x]
    for k in range(1, SIDE):
        total = total + m.small_x[k]
    m.small_two[...] = total
    sent_z = [copies.start(m.small_two, m.small_z.at[seq], peer) for peer in peers]
    m.small_z[seq] = total
    for part in (1, 2, 0):
        cubes[part][1].second()
    ring.finish(grad_hidden)
    m.mixer_in[...] = (m.hidden[...] + grad_hidden[...]).astype(BF)
    for q in range(2):
        saves.append(save(m.mixer_in.at[128 * q : 128 * q + 128], result.output.at[q]))
    for copy in sent_feed:
        copy.wait_recv()
    for d in range(16):
        gates, ups = [], []
        for s in range(PEERS):
            line = m.feed_land[s]
            gate = jnp.concatenate([line[:, :WIDE], line[:, 1024:1088]], axis=1)
            up = jnp.concatenate([line[:, WIDE:1024], line[:, 1088:1152]], axis=1)
            gates.append(gate[:, OWN * d : OWN * d + OWN])
            ups.append(up[:, OWN * d : OWN * d + OWN])
        m.w_gate[:, 288 * d : 288 * d + 288] = jnp.concatenate(gates, axis=1)
        m.w_up[:, 288 * d : 288 * d + 288] = jnp.concatenate(ups, axis=1)
    saves.append(save(m.w_gate, result.g_gate))
    saves.append(save(m.w_up, result.g_up))
    for copy in sent_z:
        copy.wait_recv()
    m.g_small[...] = functools.reduce(lambda a, b: a + b, [m.small_z[s] for s in range(PEERS)])
    saves.append(save(m.g_small, result.g_small))
    for part in (1, 2, 0):
        cubes[part][1].finish()
        cubes[part][0].first()
    for part in range(3):
        cubes[part][0].second()
    for part, (start, size) in enumerate(((0, D), (D, HALF), (D + HALF, HALF))):
        cubes[part][0].finish(m.mix_wide.at[:, pl.ds(start, size)])
    theirs = pl.ds(pl.multiple_of((1 - core) * 8, 8), 8)
    mix_copy = copies.start(m.mix_wide.at[theirs], m.mix_land.at[core], partner)
    m.mix_land[core] = m.mix_wide[pl.ds(pl.multiple_of(core * 8, 8), 8), :]
    mix_copy.wait_recv()
    for half in range(2):
        for k in range(3):
            m.w_in[:, 1024 * k + 512 * half : 1024 * k + 512 * half + 512] = m.mix_land[
                half, :, 512 * k + 512 : 512 * k + 1024
            ]
        m.w_out[:, 512 * half : 512 * half + 512] = m.mix_land[half, :, 0:512]
    saves.append(save(m.w_in, result.g_in))
    saves.append(save(m.w_out, result.g_out))
    for copy in saves:
        copy.wait()
    copies.drain()


def step(*operands):
    hbm, vmem = pl.BlockSpec(memory_space=pl.ANY), pl.BlockSpec(memory_space=pltpu.VMEM)
    return pl.pallas_call(
        step_kernel,
        out_shape=tuple(jax.ShapeDtypeStruct(*shape) for shape in RESULTS.values()),
        in_specs=[vmem if name in ("gains", "taps") else hbm for name in OPERANDS],
        out_specs=(hbm,) * len(RESULTS),
        scratch_shapes=[pltpu.VMEM(*shape) for shape in SCRATCH.values()]
        + [
            pltpu.SemaphoreType.REGULAR((2,)),
            pltpu.SemaphoreType.DMA((7,)),
            pltpu.SemaphoreType.DMA((10,)),
            pltpu.SemaphoreType.DMA((COPIES,)),
            pltpu.SemaphoreType.DMA((COPIES,)),
        ],
        compiler_params=pltpu.CompilerParams(
            collective_id=0, has_side_effects=True, vmem_limit_bytes=VMEM_BYTES
        ),
        name="step",
    )(*operands)


def adamw(weight, grad, first, second, rate, decay):
    first_new = beta_one * first + (1.0 - beta_one) * grad
    second_new = beta_two * second + (1.0 - beta_two) * grad * grad
    first_hat = first_new / (1.0 - beta_one**STEP)
    second_hat = second_new / (1.0 - beta_two**STEP)
    weight_new = weight - rate * (
        first_hat / (jnp.sqrt(second_hat) + epsilon_adam) + decay * weight
    )
    return (weight_new, first_new, second_new)


def shards(
    inputs, cotangent, norm_gains, conv_taps, w_in, w_out, w_gate, w_up, w_down,
    first_gains, first_taps, first_in, first_out, first_gate, first_up, first_down,
    second_gains, second_taps, second_in, second_out, second_gate, second_up, second_down,
):
    seq = lax.axis_index("seq")
    output, input_grad, red_in, red_out, red_gate, red_up, red_down, red_small = step(
        w_in, w_out, w_gate, w_up, w_down, norm_gains, conv_taps, inputs, cotangent.reshape(ROWS, D)
    )
    red_small = lax.dynamic_slice(red_small, (0, seq * 8), (8, 8))
    red_gains, red_taps = red_small[:2], red_small[2:5]

    new = (
        adamw(norm_gains, red_gains, first_gains, second_gains, rate_small, 0.0),
        adamw(conv_taps, red_taps, first_taps, second_taps, rate_small, 0.0),
        adamw(w_in, red_in, first_in, second_in, rate_matrix, weight_decay),
        adamw(w_out, red_out, first_out, second_out, rate_matrix, weight_decay),
        adamw(w_gate, red_gate, first_gate, second_gate, rate_matrix, weight_decay),
        adamw(w_up, red_up, first_up, second_up, rate_matrix, weight_decay),
        adamw(w_down, red_down, first_down, second_down, rate_matrix, weight_decay),
    )
    return (
        output,
        input_grad,
        *[group[0] for group in new],
        *[group[1] for group in new],
        *[group[2] for group in new],
    )


def solution(mesh):
    tokens, columns, rows = P("dp", "seq", None), P(None, ("dp", "seq")), P(("dp", "seq"), None)
    weights = (columns, columns, rows, rows, rows, rows, rows)
    return jax.shard_map(
        shards,
        mesh=mesh,
        in_specs=(tokens, tokens) + weights * 3,
        out_specs=(tokens, tokens) + weights * 3,
        check_vma=False,
    )
```

```python
import functools
import types

import jax
import jax.numpy as jnp
from jax import lax
from jax.experimental import pallas as pl
from jax.experimental.pallas import tpu as pltpu
from jax.sharding import PartitionSpec as P

D = 1024
STEP = 5

epsilon_norm = 1e-05
beta_one = 0.9
beta_two = 0.95
epsilon_adam = 1e-08
rate_matrix = 0.02
rate_small = 0.3
weight_decay = 0.1

MESH = pl.DeviceIdType.MESH
BF = jnp.bfloat16
F32 = jnp.float32
SIDE = 4
PEERS = 8
OWN = 36
PACKED = 2304
SLICE = 576
WIDE = 512
VMEM_BYTES = 62 * 2**20


def place():
    dp, seq = lax.axis_index("dp"), lax.axis_index("seq")
    return lax.rem(dp, SIDE), lax.div(dp, SIDE), lax.div(seq, 2), lax.rem(seq, 2)


def wrap(value, size=SIDE):
    return lax.rem(value + size, size)


def at(x, y, z, core):
    return (y * SIDE + x, z * 2 + core)


class Copies:
    def __init__(self, send, recv):
        self.send, self.recv, self.started, self.sent = send, recv, [], set()

    def plan(self, source, target, device):
        index = len(self.started)
        assert index < self.send.shape[0]
        copy = pltpu.make_async_remote_copy(
            src_ref=source,
            dst_ref=target,
            send_sem=self.send.at[index],
            recv_sem=self.recv.at[index],
            device_id=device,
            device_id_type=MESH,
        )
        self.started.append(copy)
        return copy

    def start(self, source, target, device):
        copy = self.plan(source, target, device)
        copy.start()
        return copy

    def drain(self, some=None):
        for copy in self.started if some is None else some:
            if id(copy) not in self.sent:
                self.sent.add(id(copy))
                copy.wait_send()


def seq_peers(x, y, z, core):
    seq = z * 2 + core
    return [(y * SIDE + x, wrap(seq + k, PEERS)) for k in range(1, PEERS)]


def halver(dim, low):
    def split(ref, part):
        size = ref.shape[dim]
        places = [slice(None)] * len(ref.shape)
        places[dim] = pl.ds(0, low) if part == 0 else pl.ds(low, size - low)
        return ref.at[tuple(places)]

    return split


class RingGather:
    def __init__(self, copies, me, to, block, split):
        self.copies, self.me, self.to, self.block, self.split = copies, me, to, block, split

    def plan(self, source=None):
        source = self.block(self.me) if source is None else source
        below, above = wrap(self.me - 1), wrap(self.me + 1)

        def move(start, target, part, place):
            return self.copies.plan(self.split(start, part), self.split(target, part), self.to(place))

        mine, before, after = self.block(self.me), self.block(below), self.block(above)
        self.up = [move(source, mine, part, above) for part in range(2)]
        self.down = [move(source, mine, part, below) for part in range(2)]
        self.pass_up = move(before, before, 0, above)
        self.pass_down = move(after, after, 1, below)

    def first(self, source=None):
        if not hasattr(self, "up"):
            self.plan(source)
        self.up[0].start()
        self.down[1].start()
        self.up[1].start()
        self.down[0].start()

    def second(self):
        self.up[0].wait_recv()
        self.pass_up.start()
        self.down[1].wait_recv()
        self.pass_down.start()

    def wait_below(self):
        self.up[1].wait_recv()

    def wait_above(self):
        self.down[0].wait_recv()

    def wait_far(self):
        self.pass_up.wait_recv()
        self.pass_down.wait_recv()

    def finish(self):
        self.wait_below()
        self.wait_above()
        self.wait_far()

    def copies_made(self):
        return [*self.up, *self.down, self.pass_up, self.pass_down]


class RingReduce:
    def __init__(self, copies, me, to, block, split, landing):
        self.copies, self.me, self.to, self.block, self.split = copies, me, to, block, split
        self.low_in, self.high_in, self.plus_in, self.minus_in = landing

    def plan(self):
        far, below, above = wrap(self.me + 2), wrap(self.me - 1), wrap(self.me + 1)
        plan, split = self.copies.plan, self.split
        self.far_up = plan(split(self.block(far), 0), self.low_in, self.to(above))
        self.far_down = plan(split(self.block(far), 1), self.high_in, self.to(below))
        self.up = [plan(split(self.block(above), k), split(self.plus_in, k), self.to(above)) for k in range(2)]
        self.down = [plan(split(self.block(below), k), split(self.minus_in, k), self.to(below)) for k in range(2)]

    def first_far(self):
        self.far_up.start()
        self.far_down.start()

    def first_above(self):
        self.up[1].start()

    def first_below(self):
        self.down[0].start()

    def first(self):
        if not hasattr(self, "up"):
            self.plan()
        self.first_far()
        self.first_above()
        self.first_below()

    def second(self):
        below, above = self.block(wrap(self.me - 1)), self.block(wrap(self.me + 1))
        self.far_up.wait_recv()
        accumulate(self.split(above, 0), self.split(above, 0), self.low_in)
        self.up[0].start()
        self.far_down.wait_recv()
        accumulate(self.split(below, 1), self.split(below, 1), self.high_in)
        self.down[1].start()

    def copies_made(self):
        return [self.far_up, self.far_down, *self.up, *self.down]

    def finish(self, target=None):
        own = self.block(self.me)
        for copy in (*self.up, *self.down):
            copy.wait_recv()
        accumulate(own if target is None else target, own, self.plus_in, self.minus_in)


def accumulate(target, *sources):
    shape = target.shape
    if len(shape) > 2:
        for index in range(shape[0]):
            accumulate(target.at[index], *[source.at[index] for source in sources])
        return
    step = 16

    @pl.loop(0, shape[0] // step)
    def _(i):
        rows = pl.ds(pl.multiple_of(i * step, step), step)
        total = sources[0][rows, :].astype(F32)
        for source in sources[1:]:
            total = total + source[rows, :].astype(F32)
        target[rows, :] = total.astype(target.dtype)


def columns_of(seq, dp_count=16):
    return [(288 * d + OWN * seq, 36 * d) for d in range(dp_count)]


def dot(a, b, dims=((1,), (0,))):
    return lax.dot_general(a, b, (dims, ((), ())), preferred_element_type=F32)


NT = ((1,), (1,))
TN = ((0,), (0,))
ROWS = 256
PAIR = 512
EVERY = 272
HALF = 512


def by_rows(ref, which, part):
    start, size = (32 * which, 32) if part is None else (32 * which + 16 * part, 16)
    lead = [slice(None)] * (len(ref.shape) - 2)
    return ref.at[(*lead, pl.ds(start, size), slice(None))]


def rows_of(lanes):
    def halves(ref, which, part):
        rows = by_rows(ref, which, part)
        return rows.at[(*[slice(None)] * (len(rows.shape) - 1), lanes)]

    return halves


def by_columns(ref, which, part):
    first, size = ((0, 1152), (0, 640), (640, 512))[0 if part is None else part + 1]
    lead = [slice(None)] * (len(ref.shape) - 2)
    return ref.at[(*lead, slice(None), pl.ds(1152 * which + first, size))]


def visit(z, k):
    return wrap(z + k + lax.div(k, 2) * (5 - 2 * k))


def turn_of(z, chip):
    ahead = wrap(chip - z)
    return ahead + lax.div(ahead, 2) * (5 - 2 * ahead)


class PlaneGather:
    def __init__(self, copies, spot, view, halves, block, split):
        x, y, z, core = spot
        to_x, to_y = (lambda i: at(i, y, z, core)), (lambda i: at(x, i, z, core))
        everything, fours = slice(None), halver(0, 2)
        self.x, self.y, self.view, self.halves = x, y, view, halves
        self.row_x = RingGather(copies, x, to_x, lambda i: halves(view(y, i), 0, None), split)
        self.row_y = RingGather(copies, y, to_y, lambda i: halves(view(i, x), 1, None), split)
        self.all_y = RingGather(copies, y, to_y, lambda i: halves(view(i, everything), 0, None), fours)
        self.all_x = RingGather(copies, x, to_x, lambda i: halves(view(everything, i), 1, None), fours)
        self.row_x.plan(halves(block, 0, None))
        self.row_y.plan(halves(block, 1, None))
        self.all_y.plan()
        self.all_x.plan()

    def one(self):
        self.row_x.first()
        self.row_y.first()

    def two(self):
        self.row_x.second()
        self.row_y.second()

    def three(self):
        self.row_x.finish()
        self.all_y.first()
        self.row_y.finish()
        self.all_x.first()

    def four(self):
        self.all_y.second()
        self.all_x.second()

    def finish(self):
        self.all_y.finish()
        self.all_x.finish()

    def wait_near(self, then):
        self.all_y.wait_below()
        self.all_x.wait_below()
        then(self, -1)
        self.all_y.wait_above()
        self.all_x.wait_above()
        then(self, 1)

    def copies(self):
        return [copy for ring in (self.row_x, self.row_y, self.all_y, self.all_x) for copy in ring.copies_made()]

    def group(self, which, step):
        everything = slice(None)
        if which == 0:
            return self.halves(self.view(wrap(self.y + step), everything), 0, None)
        return self.halves(self.view(everything, wrap(self.x + step)), 1, None)


PARTS = (
    (0, pl.ds(0, 512), 0, ("y", "z", "x")),
    (0, pl.ds(512, 512), 512, ("x", "y", "z")),
    (1, pl.ds(0, 512), 1024, ("z", "x", "y")),
    (1, pl.ds(512, 512), 1536, ("y", "z", "x")),
)


def first_half(width):
    return (width + 255) // 256 * 128


def cube_spots(spot, order):
    x, y, z, core = spot
    own = {"x": x, "y": y, "z": z}
    to = {
        "x": lambda i: at(i, y, z, core),
        "y": lambda i: at(x, i, z, core),
        "z": lambda i: at(x, y, i, core),
    }

    def view(ref, **places):
        return ref.at[tuple(places.get(axis, own[axis]) for axis in ("y", "x", "z"))]

    return [own[axis] for axis in order], [to[axis] for axis in order], view


def cube_rings(spot, order, ref, make):
    (a, b, c), (to_a, to_b, to_c), view = cube_spots(spot, order)
    one, two, three = order
    everything = slice(None)
    place_of = {"y": 0, "x": 1, "z": 2}
    first = make(a, to_a, lambda i: view(ref, **{one: i}), halver(-1, first_half(ref.shape[-1])))
    second = make(b, to_b, lambda i: view(ref, **{one: everything, two: i}), halver(0, 2))
    third = make(
        c, to_c,
        lambda i: view(ref, **{one: everything, two: everything, three: i}),
        halver(0 if place_of[two] < place_of[one] else 1, 2),
    )
    return first, second, third


def small_rows(small_all):
    pieces = [small_all[d // 4, d % 4][:, :64] for d in range(16)]
    return jnp.concatenate(pieces, axis=1)


def normalize(rows, gain):
    inverse = lax.rsqrt(jnp.mean(rows * rows, axis=-1, keepdims=True) + epsilon_norm)
    return rows * inverse * gain


def extend(extended, projected, half, sequence):
    first = pl.ds(ROWS + 8 * sequence, 8)
    main = pl.ds(128 * sequence, 128)
    extended[0:8, :] = projected[half, first, :HALF] * projected[half, first, 1024:]
    extended[8:136, :] = projected[half, main, :HALF] * projected[half, main, 1024:]


def convolve(extended, taps):
    return taps[0:1] * extended[6:134, :] + taps[1:2] * extended[7:135, :] + taps[2:3] * extended[8:136, :]


def half_lanes(half):
    return pl.ds(pl.multiple_of(half * HALF, HALF), HALF)


class PlaneReduce:
    def __init__(self, copies, spot, view, halves, split, landings):
        x, y, z, core = spot
        to_x, to_y = (lambda i: at(i, y, z, core)), (lambda i: at(x, i, z, core))
        everything, fours = slice(None), halver(0, 2)
        self.halves = halves
        self.all_y = RingReduce(copies, y, to_y, lambda i: halves(view(i, everything), 0, None), fours, landings[0:4])
        self.all_x = RingReduce(copies, x, to_x, lambda i: halves(view(everything, i), 1, None), fours, landings[4:8])
        self.row_x = RingReduce(copies, x, to_x, lambda i: halves(view(y, i), 0, None), split, landings[8:12])
        self.row_y = RingReduce(copies, y, to_y, lambda i: halves(view(i, x), 1, None), split, landings[12:16])

    def one(self):
        self.all_y.first()
        self.all_x.first()

    def two(self):
        self.all_y.second()
        self.all_x.second()

    def three(self):
        self.all_y.finish()
        self.row_x.first()
        self.all_x.finish()
        self.row_y.first()

    def four(self):
        self.row_x.second()
        self.row_y.second()

    def finish(self, target):
        self.row_x.finish(self.halves(target, 0, None))
        self.row_y.finish(self.halves(target, 1, None))


def plane_landings(ref):
    wide = lambda count, blocks, rows: ref.reshape(count, blocks, rows, 1152)
    single = lambda rows: ref.reshape(2048 // rows, rows, 1152)
    fed, downs = [], []
    for k in range(2):
        fed += [wide(32, 2, 32).at[8 + 2 * k], wide(32, 2, 32).at[9 + 2 * k]]
        fed += [wide(16, 4, 32).at[2 * k], wide(16, 4, 32).at[2 * k + 1]]
        downs += [wide(64, 2, 16).at[38 + 2 * k], wide(64, 2, 16).at[39 + 2 * k]]
        downs += [wide(32, 4, 16).at[15 + 2 * k], wide(32, 4, 16).at[16 + 2 * k]]
    for k in range(2):
        fed += [single(16).at[56 + 2 * k], single(16).at[57 + 2 * k], single(32).at[24 + 2 * k], single(32).at[25 + 2 * k]]
        downs += [single(16).at[88 + 2 * k, :, pl.ds(0, 640)], single(16).at[89 + 2 * k, :, pl.ds(0, 512)]]
        downs += [single(16).at[84 + 2 * k], single(16).at[85 + 2 * k]]
    return fed, downs


def cube_landings(ref, lanes, order):
    width, total = lanes.size, ref.shape[-1]
    place_of = {"y": 0, "x": 1, "z": 2}
    halved = (2, 4) if place_of[order[1]] < place_of[order[0]] else (4, 2)

    def take(count, lead, index, part=None):
        window = lanes
        if part is not None:
            low = first_half(width)
            window = pl.ds(lanes.start, low) if part == 0 else pl.ds(lanes.start, width - low)
        places = (slice(None),) * (len(lead) + 1)
        return ref.reshape(count, *lead, 16, total).at[(index, *places, window)]

    first = [take(64, (), 60, 0), take(64, (), 61, 1), take(64, (), 62), take(64, (), 63)]
    second = [take(32, (2,), 24), take(32, (2,), 25), take(16, (4,), 13), take(16, (4,), 14)]
    third = [take(8, halved, 4), take(8, halved, 5), take(4, (4, 4), 0), take(4, (4, 4), 1)]
    return first, second, third


def local_copies(semaphores):
    count = iter(range(semaphores.shape[0]))

    def start(source, target):
        copy = pltpu.make_async_copy(source, target, semaphores.at[next(count)])
        copy.start()
        return copy

    return start


OPERANDS = ("w_in", "w_out", "w_gate", "w_up", "w_down", "gains", "taps", "inputs", "cotangent")
RESULTS = {
    "output": ((2, 128, D), BF),
    "input_grad": ((2, 128, D), F32),
    "g_in": ((8, 3072), F32),
    "g_out": ((8, 1024), F32),
    "g_gate": ((8, 4608), F32),
    "g_up": ((8, 4608), F32),
    "g_down": ((OWN, D), F32),
    "g_small": ((8, 128), F32),
}
SCRATCH = {
    "w_in": ((8, 3072), F32),
    "w_out": ((8, 1024), F32),
    "w_gate": ((8, 4608), F32),
    "w_up": ((8, 4608), F32),
    "w_down": ((OWN, D), F32),
    "tile": ((8, 128), F32),
    "inputs": ((2, 128, D), BF),
    "mix": ((2, 4, 4, 64, 2048), BF),
    "feed": ((4, 4, 64, 2 * SLICE), BF),
    "down": ((4, 4, 16, PACKED), BF),
    "small_all": ((4, 4, 8, 128), F32),
    "edge_in": ((2, 16, D), BF),
    "tokens": ((SIDE, 2, ROWS, D), BF),
    "grads": ((SIDE, 2, ROWS, D), BF),
    "mix_send": ((2, 16, D), BF),
    "feed_send": ((PEERS, 16, 640), BF),
    "mix_got": ((PEERS, 16, D), BF),
    "feed_got": ((PEERS, 16, 640), BF),
    "small_got": ((PEERS, 8, 128), F32),
    "mix_block": ((64, 2048), BF),
    "feed_block": ((64, 2 * SLICE), BF),
    "down_block": ((16, PACKED), BF),
    "small_send": ((8, 128), F32),
    "rows": ((8, D), F32),
    "normed": ((EVERY, D), BF),
    "projected": ((2, EVERY, 1536), F32),
    "extended": ((136, HALF), F32),
    "mixer_in": ((ROWS, D), BF),
    "hidden": ((ROWS, D), F32),
    "normed_two": ((ROWS, D), BF),
    "down_rows": ((SLICE, D), BF),
    "narrow_wide": ((160, D), F32),
    "value": ((PAIR, 2 * SLICE), F32),
    "grad_active": ((PAIR, SLICE), F32),
    "active": ((2048, SLICE), BF),
    "grad_value": ((2048, 2 * SLICE), BF),
    "part": ((SIDE, 2, ROWS, D), BF),
    "part_out": ((SIDE, 2, ROWS, D), BF),
    "landing": ((SIDE, ROWS, D), BF),
    "landing_left": ((SIDE, ROWS, HALF), BF),
    "landing_right": ((SIDE, ROWS, HALF), BF),
    "low_in": ((128, D), BF),
    "high_in": ((128, D), BF),
    "plus_in": ((ROWS, D), BF),
    "minus_in": ((ROWS, D), BF),
    "low_out": ((128, D), BF),
    "high_out": ((128, D), BF),
    "plus_out": ((ROWS, D), BF),
    "minus_out": ((ROWS, D), BF),
    "down_part": ((SLICE, 256), F32),
    "down_tail": ((16, 16, 256), F32),
    "grad_conv": ((2, 136, D), F32),
    "grad_x": ((2, ROWS, HALF), BF),
    "edge_send": ((2, 8, D), F32),
    "edge_got": ((2, 8, D), F32),
    "sums": ((8, D), F32),
    "mix_wide": ((16, 2048), F32),
    "feed_wide": ((64, 2 * SLICE), F32),
    "down_wide": ((16, PACKED), F32),
    "mix_land": ((2, 8, 2048), F32),
    "feed_land": ((PEERS, 8, 2 * SLICE), F32),
    "small": ((4, 4, 8, 128), F32),
    "small_y": ((4, 4, 8, 128), F32),
    "small_x": ((4, 8, 128), F32),
    "small_z": ((PEERS, 8, 128), F32),
    "small_one": ((4, 8, 128), F32),
    "small_two": ((8, 128), F32),
    "g_small": ((8, 128), F32),
}
COPIES = 448


def step_kernel(*refs):
    count = len(OPERANDS)
    given = types.SimpleNamespace(**dict(zip(OPERANDS, refs)))
    result = types.SimpleNamespace(**dict(zip(RESULTS, refs[count:])))
    count += len(RESULTS)
    m = types.SimpleNamespace(**dict(zip(SCRATCH, refs[count:])))
    ready, load_sem, save_sem, send, recv = refs[count + len(SCRATCH) :]

    spot = x, y, z, core = place()
    seq = z * 2 + core
    copies = Copies(send, recv)
    peers = seq_peers(x, y, z, core)
    across = [at(wrap(x + k), y, z, core) for k in range(1, SIDE)]
    along = [at(x, wrap(y + k), z, core) for k in range(1, SIDE)]
    partner = at(x, y, z, 1 - core)
    load = local_copies(load_sem)
    loads = {
        "w_in": load(given.w_in, m.w_in),
        "w_out": load(given.w_out, m.w_out),
        "w_gate": load(given.w_gate, m.w_gate),
        "w_up": load(given.w_up, m.w_up),
        "w_down": load(given.w_down, m.w_down),
        "inputs": load(given.inputs, m.inputs),
        "cotangent": load(given.cotangent, m.grads.at[z, core]),
    }
    barrier = pltpu.get_barrier_semaphore()
    for device in peers + across + along:
        pl.semaphore_signal(barrier, inc=1, device_id=device, device_id_type=MESH)

    def to_z(i):
        return at(x, y, i, core)

    loads["w_in"].wait()
    loads["w_out"].wait()
    for half in range(2):
        parts = [m.w_out[:, 512 * half : 512 * half + 512]]
        parts += [m.w_in[:, 1024 * k + 512 * half : 1024 * k + 512 * half + 512] for k in range(3)]
        upper = jnp.concatenate(parts[:2], axis=1)
        lower = jnp.concatenate(parts[2:], axis=1)
        m.mix_send[half] = jnp.concatenate([upper, lower], axis=0).astype(BF)
    pl.semaphore_wait(barrier, len(peers + across + along))
    mix_copies = []
    for k, peer in enumerate(peers):
        other = wrap(seq + k + 1, PEERS)
        mix_copies.append(copies.start(m.mix_send.at[lax.rem(other, 2)], m.mix_got.at[seq], peer))
    m.mix_got[seq] = m.mix_send[core]
    mixed, mixed_out = (
        PlaneGather(copies, spot, lambda i, j: m.mix.at[core, i, j], rows_of(lanes), m.mix_block, halver(-2, 16))
        for lanes in (pl.ds(HALF, 1536), pl.ds(0, HALF))
    )
    fed = PlaneGather(copies, spot, lambda i, j: m.feed.at[i, j], by_rows, m.feed_block, halver(-2, 16))
    downs = PlaneGather(copies, spot, lambda i, j: m.down.at[i, j], by_columns, m.down_block, halver(-1, 640))
    loads["w_down"].wait()
    for i in range(4):
        m.narrow_wide[4 * i : 4 * i + 4, 0:256] = m.w_down[32:36, 256 * i : 256 * i + 256]
    m.down_block[:, 0:1024] = m.w_down[0:16, :].astype(BF)
    m.down_block[:, 1024:2048] = m.w_down[16:32, :].astype(BF)
    m.down_block[:, 2048:PACKED] = m.narrow_wide[0:16, 0:256].astype(BF)
    m.down[y, x] = m.down_block[...]
    downs.one()
    m.tile[...] = jnp.zeros_like(m.tile)
    m.tile[0:2, 0:8] = given.gains[...].astype(BF).astype(F32)
    m.tile[2:5, 0:8] = given.taps[...].astype(BF).astype(F32)
    m.small_got[seq] = pltpu.roll(m.tile[...], seq * 8, 1)
    small_copies = [copies.start(m.small_got.at[seq], m.small_got.at[seq], peer) for peer in peers]
    edge_copy = copies.start(
        given.inputs.at[:, pl.ds(112, 16)], m.edge_in, (y * SIDE + x, wrap(seq + 1, PEERS))
    )
    ring = RingGather(
        copies, z, to_z,
        lambda i: m.grads.at[i, core],
        halver(0, 128),
    )
    ring.plan(given.cotangent)

    def slices(which):
        for s in which:
            gate = jnp.concatenate([m.w_gate[:, a : a + OWN] for a, _ in columns_of(s)], axis=1)
            up = jnp.concatenate([m.w_up[:, a : a + OWN] for a, _ in columns_of(s)], axis=1)
            tail = jnp.concatenate([gate[:, WIDE:], up[:, WIDE:]], axis=1)
            upper = jnp.concatenate([gate[:, :WIDE], up[:, :128]], axis=1)
            lower = jnp.concatenate([up[:, 128:WIDE], tail, jnp.zeros((8, 128), F32)], axis=1)
            m.feed_send[s] = jnp.concatenate([upper, lower], axis=0).astype(BF)

    loads["w_gate"].wait()
    loads["w_up"].wait()
    slices(range(PEERS))
    feed_copies = []
    for k, peer in enumerate(peers):
        other = wrap(seq + k + 1, PEERS)
        feed_copies.append(copies.start(m.feed_send.at[other], m.feed_got.at[seq], peer))
    m.feed_got[seq] = m.feed_send[seq]
    downs.two()
    for copy in mix_copies:
        copy.wait_recv()
    for k in range(4):
        a, b = m.mix_got[2 * k].astype(F32), m.mix_got[2 * k + 1].astype(F32)
        line = slice(16 * k, 16 * k + 16)
        m.mix_block[line, :1024] = jnp.concatenate([a[:8], b[:8]], axis=0).astype(BF)
        m.mix_block[line, 1024:] = jnp.concatenate([a[8:], b[8:]], axis=0).astype(BF)
    mixed.one()
    mixed_out.one()
    downs.three()
    m.mix[core, y, x] = m.mix_block[...]

    for copy in feed_copies:
        copy.wait_recv()
    for k in range(4):
        a, b = m.feed_got[2 * k].astype(F32), m.feed_got[2 * k + 1].astype(F32)
        line = slice(16 * k, 16 * k + 16)
        m.feed_block[line, :640] = jnp.concatenate([a[:8], b[:8]], axis=0).astype(BF)
        m.feed_block[line, 640:] = jnp.concatenate([a[8:, :512], b[8:, :512]], axis=0).astype(BF)
    m.feed[y, x] = m.feed_block[...]
    fed.one()
    ring.first()
    cotangent_ring = ring
    grads_passed = [copies.start(given.cotangent, m.grads.at[z, core], partner)]
    mixed.two()
    mixed_out.two()
    for copy in small_copies:
        copy.wait_recv()
    m.small_send[...] = functools.reduce(lambda a, b: a + b, [m.small_got[s] for s in range(PEERS)])
    small_x = [copies.start(m.small_send, m.small_all.at[y, x], device) for device in across]
    m.small_all[y, x] = m.small_send[...]
    mixed.three()
    mix_passed = []

    def pass_on(gather, step):
        for which in range(2):
            part = gather.group(which, step)
            mix_passed.append(copies.start(part, part, partner))

    pass_on(mixed, 0)
    fed.two()
    downs.four()
    for copy in small_x:
        copy.wait_recv()
    small_y = [copies.start(m.small_all.at[y], m.small_all.at[y], device) for device in along]
    for copy in small_y:
        copy.wait_recv()
    m.rows[...] = small_rows(m.small_all)
    loads["inputs"].wait()
    for q in range(2):
        m.normed[128 * q : 128 * q + 128, :] = normalize(m.inputs[q].astype(F32), m.rows[0:1, :]).astype(BF)
    edge_copy.wait_recv()
    inside = (seq > 0).astype(F32)
    earlier = [normalize(m.edge_in[q].astype(F32)[8:], m.rows[0:1, :]) * inside for q in range(2)]
    m.normed[ROWS:EVERY, :] = jnp.concatenate(earlier, axis=0).astype(BF)
    ring.second()
    mixed.four()
    mixed_out.three()
    mixed.wait_near(pass_on)
    mixed.all_y.wait_far()
    mixed.all_x.wait_far()
    pass_on(mixed, 2)
    mixed_out.four()
    fed.three()
    for turn in range(2):
        if turn == 1:
            for copy in mix_passed[:8]:
                copy.wait_recv()
        half = core if turn == 0 else 1 - core
        m.projected[half] = dot(m.normed[...], m.mix.at[half].reshape(D, 2048)[:, HALF:])
        lanes = half_lanes(half)
        for q in range(2):
            main = slice(128 * q, 128 * q + 128)
            extend(m.extended, m.projected, half, q)
            convolved = convolve(m.extended, m.rows[2:5, lanes])
            m.mixer_in[main, lanes] = (m.projected[half, main, HALF:1024] * convolved).astype(BF)
    pass_on(mixed_out, 0)
    mixed_out.wait_near(pass_on)
    mixed_out.all_y.wait_far()
    mixed_out.all_x.wait_far()
    pass_on(mixed_out, 2)
    for copy in mix_passed[8:]:
        copy.wait_recv()
    weights = [m.mix.at[half].reshape(D, 2048) for half in range(2)]
    for half in range(2):
        lanes = slice(HALF * half, HALF * half + HALF)
        mixed_out = dot(m.mixer_in[...], weights[half][:, :HALF])
        for q in range(2):
            main = slice(128 * q, 128 * q + 128)
            m.hidden[main, lanes] = m.inputs[q, :, lanes].astype(F32) + mixed_out[main]
    m.normed_two[...] = normalize(m.hidden[...], m.rows[1:2, :]).astype(BF)

    around = RingGather(
        copies, z, to_z,
        lambda i: m.tokens.at[i, core],
        halver(0, 128),
    )
    around.plan(m.normed_two)
    passed = [copies.plan(m.normed_two, m.tokens.at[z, core], partner)]
    for step in (1, 3, 2):
        chunk = m.tokens.at[wrap(z + step), core]
        passed.append(copies.plan(chunk, chunk, partner))
    around.first()
    passed[0].start()
    m.tokens[z, core] = m.normed_two[...]
    fed.four()
    ring.finish()
    for step in (1, 3, 2):
        chunk = m.grads.at[wrap(z + step), core]
        grads_passed.append(copies.start(chunk, chunk, partner))
    gives, gives_left, gives_right = [], [], []
    for k in range(SIDE):
        theirs = m.part_out.at[k, 1 - core]
        gives.append(copies.plan(m.part.at[k, 1 - core], m.landing.at[k], partner))
        gives_left.append(copies.plan(theirs.at[:, 0:HALF], m.landing_left.at[k], partner))
        gives_right.append(copies.plan(theirs.at[:, HALF:D], m.landing_right.at[k], partner))
    reduce = RingReduce(
        copies, z, to_z,
        lambda i: m.part.at[turn_of(z, i), core],
        halver(0, 128),
        (m.low_in, m.high_in, m.plus_in, m.minus_in),
    )
    reduce.plan()
    downs.finish()
    for i in range(SIDE):
        for d in range(SIDE):
            packed = m.down[i, d].astype(F32)
            m.narrow_wide[OWN * d : OWN * d + 16, :] = packed[:, 0:1024]
            m.narrow_wide[OWN * d + 16 : OWN * d + 32, :] = packed[:, 1024:2048]
            for k in range(4):
                m.narrow_wide[OWN * d + 32 : OWN * d + 36, 256 * k : 256 * k + 256] = packed[4 * k : 4 * k + 4, 2048:]
        m.down_rows[144 * i : 144 * i + 144, :] = m.narrow_wide[0:144, :].astype(BF)
    for copy in grads_passed:
        copy.wait_recv()
    loads["cotangent"].wait()
    fed.finish()
    feed = m.feed.reshape(D, 2 * SLICE)
    @pl.loop(0, SIDE)
    def _(k):
        @pl.when(k == 0)
        def _():
            passed[0].wait_recv()

        @pl.when(k == 1)
        def _():
            around.second()
            around.wait_above()
            passed[1].start()
            around.wait_below()
            passed[2].start()
            passed[1].wait_recv()

        @pl.when(k == 2)
        def _():
            passed[2].wait_recv()
            around.wait_far()
            passed[3].start()

        @pl.when(k == 3)
        def _():
            passed[3].wait_recv()

        chip = visit(z, k)
        m.value[...] = dot(m.tokens.at[chip].reshape(PAIR, D)[...], feed[...])
        m.grad_active[...] = dot(m.grads.at[chip].reshape(PAIR, D)[...], m.down_rows[...], NT)
        base = chip * PAIR

        @pl.loop(0, PAIR // 64)
        def _(r):
            line = pl.ds(pl.multiple_of(r * 64, 64), 64)
            target = pl.ds(pl.multiple_of(base + r * 64, 64), 64)
            tail = m.value[line, 1024:1152]
            ends = []
            for gate, up, back, where in (
                (m.value[line, :WIDE], m.value[line, WIDE:1024], m.grad_active[line, :WIDE], slice(0, WIDE)),
                (tail[:, :64], tail[:, 64:], m.grad_active[line, WIDE:], slice(WIDE, SLICE)),
            ):
                sigmoid = jax.nn.sigmoid(gate)
                soft = gate * sigmoid
                m.active[target, where] = (soft * up).astype(BF)
                grad_up = (back * soft).astype(BF)
                grad_gate = (back * up * (sigmoid * (1.0 + gate * (1.0 - sigmoid)))).astype(BF)
                ends.append((grad_gate, grad_up))
            m.grad_value[target, :WIDE] = ends[0][0]
            m.grad_value[target, WIDE:1024] = ends[0][1]
            m.grad_value[target, 1024:1088] = ends[1][0]
            m.grad_value[target, 1088:1152] = ends[1][1]

        lines = pl.ds(pl.multiple_of(base, PAIR), PAIR)
        m.part.at[k].reshape(PAIR, D)[...] = dot(m.grad_value[lines, :], feed[...], NT).astype(BF)
        for step in range(SIDE):
            @pl.when(k == step)
            def _(step=step):
                gives[step].start()
        m.part_out.at[k].reshape(PAIR, D)[...] = dot(m.active[lines, :], m.down_rows[...]).astype(BF)
        for step in range(SIDE):
            @pl.when(k == step)
            def _(step=step):
                gives_left[step].start()
                gives_right[step].start()
                gives[step].wait_recv()
                accumulate(m.part.at[step, core], m.part.at[step, core], m.landing.at[step])
                if step == 1:
                    reduce.first_above()
                if step == 2:
                    reduce.first_below()
                if step == 3:
                    reduce.first_far()

    copies.drain(fed.copies())
    copies.drain(downs.copies())
    every_grad, every_token = m.grads.reshape(2048, D), m.tokens.reshape(2048, D)

    @pl.loop(0, 4)
    def _(n):
        columns = pl.ds(pl.multiple_of(n * 256, 256), 256)
        feed[columns, :] = dot(every_token[:, columns], m.grad_value[...], TN).astype(BF)

    plane_neighbours = [at(wrap(x + 1), y, z, core), at(wrap(x - 1), y, z, core)]
    plane_neighbours += [at(x, wrap(y + 1), z, core), at(x, wrap(y - 1), z, core)]
    for device in plane_neighbours:
        pl.semaphore_signal(ready.at[0], inc=1, device_id=device, device_id_type=MESH)
    reduce.second()

    def down_columns(n):
        columns = slice(256 * n, 256 * n + 256)
        m.down_part[...] = dot(m.active[...], every_grad[:, columns], TN)
        for d in range(16):
            block = m.down.at[d // 4, d % 4]
            block[:, columns] = m.down_part[OWN * d : OWN * d + 16, :].astype(BF)
            block[:, 1024 + 256 * n : 1280 + 256 * n] = m.down_part[OWN * d + 16 : OWN * d + 32, :].astype(BF)
            m.down_tail[d, 4 * n : 4 * n + 4, :] = m.down_part[OWN * d + 32 : OWN * d + 36, :]

    fed_landings, down_landings = plane_landings(m.grad_value)
    fed = PlaneReduce(copies, spot, lambda i, j: m.feed.at[i, j], by_rows, halver(-2, 16), fed_landings)
    downs = PlaneReduce(copies, spot, lambda i, j: m.down.at[i, j], by_columns, halver(-1, 640), down_landings)
    down_columns(0)
    pl.semaphore_wait(ready.at[0], len(plane_neighbours))
    fed.one()
    for n in range(1, 4):
        down_columns(n)
    for d in range(16):
        m.down[d // 4, d % 4, :, 2048:PACKED] = m.down_tail[d].astype(BF)
    downs.one()
    for k in range(SIDE):
        gives_left[k].wait_recv()
        gives_right[k].wait_recv()
        ours = m.part_out.at[k, core]
        accumulate(ours.at[:, 0:HALF], ours.at[:, 0:HALF], m.landing_left.at[k])
        accumulate(ours.at[:, HALF:D], ours.at[:, HALF:D], m.landing_right.at[k])
    ring = RingReduce(
        copies, z, to_z,
        lambda i: m.part_out.at[turn_of(z, i), core],
        halver(0, 128),
        (m.low_out, m.high_out, m.plus_out, m.minus_out),
    )
    ring.first()
    grad_hidden = m.value.at[0:ROWS, 0:D]
    grad_mixer = m.value.at[ROWS : 2 * ROWS, 0:D]
    reduce.finish(grad_hidden)

    copies.drain(gives + gives_left + gives_right + reduce.copies_made() + around.copies_made() + passed)
    copies.drain(grads_passed)
    copies.drain(cotangent_ring.copies_made())
    neighbours = plane_neighbours + [at(x, y, wrap(z + 1), core), at(x, y, wrap(z - 1), core), partner]
    for device in neighbours:
        pl.semaphore_signal(ready.at[1], inc=1, device_id=device, device_id_type=MESH)

    sum_blocks = m.grads.reshape(2, 4, 4, 4, 16, D)

    def flat_views(ref):
        return [ref.reshape(2, D, D).at[group, :, lanes] for group, lanes, _, _ in PARTS]

    sum_flat, give_flat, got_flat = flat_views(m.grads), flat_views(m.tokens), flat_views(m.part)
    cubes = []
    buffers = (m.landing, m.landing, m.landing_left, m.landing_right)
    for (group, lanes, _, order), buffer in zip(PARTS, buffers):
        room = lanes if buffer is m.landing else pl.ds(0, lanes.size)
        lands = iter(cube_landings(buffer, room, order))

        def make(me, to, block, split, lands=lands):
            return RingReduce(copies, me, to, block, split, next(lands))

        cubes.append(cube_rings(spot, order, sum_blocks.at[group, :, :, :, :, lanes], make))
    save = local_copies(save_sem)
    saves = []

    m.sums[...] = jnp.zeros_like(m.sums)
    narrow = m.normed_two

    @pl.loop(0, 8)
    def _(n):
        line = pl.ds(pl.multiple_of(n * 32, 32), 32)
        tokens = m.hidden[line, :]
        inverse = lax.rsqrt(jnp.mean(tokens * tokens, axis=-1, keepdims=True) + epsilon_norm)
        scaled = tokens * inverse
        upstream = grad_hidden[line, :]
        m.sums[1:2, :] += jnp.sum(upstream * scaled, axis=0, keepdims=True)
        weighted = upstream * m.rows[1:2, :]
        total = m.grads[z, core, line, :].astype(F32) + inverse * (
            weighted - scaled * jnp.mean(weighted * scaled, axis=-1, keepdims=True)
        )
        grad_hidden[line, :] = total
        narrow[line, :] = total.astype(BF)

    before = m.normed.at[0:ROWS]
    grad_bc = m.grad_value.reshape(8, ROWS, 2 * SLICE)
    given_parts = {}

    def gradient(part, give):
        half = 1 - core if give else core
        target = (give_flat if give else sum_flat)[part]
        left = m.mixer_in if part == 0 else before
        right = (
            lambda: narrow[:, half_lanes(half)],
            lambda: grad_bc[6 + half, :, 0:HALF],
            lambda: grad_bc[6 + half, :, HALF:D],
            lambda: m.grad_x[half],
        )[part]

        @pl.loop(0, 4)
        def _(n):
            columns = pl.ds(pl.multiple_of(n * 256, 256), 256)
            target[columns, :] = dot(left[:, columns], right(), TN).astype(BF)

        if give:
            given_parts[part] = copies.start(target, got_flat[part], partner)

    def pass_to_cube(part):
        given_parts[part].wait_recv()
        accumulate(sum_flat[part], sum_flat[part], got_flat[part])
        cubes[part][2].first()

    pl.semaphore_wait(ready.at[1], len(neighbours))
    gradient(0, True)
    grad_mixer[...] = dot(narrow[:, :HALF], weights[0][:, :HALF], NT) + dot(narrow[:, HALF:], weights[1][:, :HALF], NT)
    for q in range(2):
        for half in range(2):
            lanes = slice(HALF * half, HALF * half + HALF)
            start = slice(128 * q, 128 * q + 8)
            m.edge_send[q, :, lanes] = grad_mixer[start, lanes] * m.projected[half, start, HALF:1024]
    edge_copy = copies.start(m.edge_send, m.edge_got, (y * SIDE + x, wrap(seq - 1, PEERS)))
    gradient(0, False)
    fed.two()
    for half in range(2):
        lanes = slice(HALF * half, HALF * half + HALF)
        for q in range(2):
            main = slice(128 * q, 128 * q + 128)
            extend(m.extended, m.projected, half, q)
            upstream = grad_mixer[main, lanes]
            grad_bc[6 + half, main, HALF:D] = (upstream * convolve(m.extended, m.rows[2:5, lanes])).astype(BF)
            m.grad_conv[q, 0:128, lanes] = upstream * m.projected[half, main, HALF:1024]
    gradient(2, True)
    pass_to_cube(0)
    edge_copy.wait_recv()
    inside = (seq < PEERS - 1).astype(F32)
    for q in range(2):
        m.grad_conv[q, 128:136, :] = m.edge_got[q] * inside
        main = slice(128 * q, 128 * q + 128)
        for half in range(2):
            lanes = slice(HALF * half, HALF * half + HALF)
            taps = m.rows[2:5, lanes]
            gated = (
                taps[2:3] * m.grad_conv[q, 0:128, lanes]
                + taps[1:2] * m.grad_conv[q, 1:129, lanes]
                + taps[0:1] * m.grad_conv[q, 2:130, lanes]
            )
            grad_bc[6 + half, main, 0:HALF] = (gated * m.projected[half, main, 1024:]).astype(BF)
            m.grad_x[half, main, :] = (gated * m.projected[half, main, :HALF]).astype(BF)
    gradient(1, True)
    gradient(3, True)
    gradient(2, False)
    pass_to_cube(2)
    downs.two()
    ring.second()
    gradient(1, False)
    pass_to_cube(1)
    gradient(3, False)
    pass_to_cube(3)
    for half in range(2):
        lanes = slice(HALF * half, HALF * half + HALF)
        for q in range(2):
            extend(m.extended, m.projected, half, q)
            back = m.grad_conv[q, 0:128, lanes]
            for k in range(3):
                m.sums[2 + k : 3 + k, lanes] += jnp.sum(back * m.extended[6 + k : 134 + k, :], axis=0, keepdims=True)
    fed.three()
    downs.three()

    grad_mixer[...] = dot(grad_bc[6, :, 0:D], weights[0][:, HALF:1536], NT)
    grad_mixer[...] += dot(grad_bc[7, :, 0:D], weights[1][:, HALF:1536], NT)
    grad_mixer[...] += dot(m.grad_x[0], weights[0][:, 1536:], NT) + dot(m.grad_x[1], weights[1][:, 1536:], NT)

    @pl.loop(0, 8)
    def _(n):
        line = pl.ds(pl.multiple_of(n * 32, 32), 32)
        tokens = m.inputs.reshape(ROWS, D)[line, :].astype(F32)
        inverse = lax.rsqrt(jnp.mean(tokens * tokens, axis=-1, keepdims=True) + epsilon_norm)
        scaled = tokens * inverse
        upstream = grad_mixer[line, :]
        m.sums[0:1, :] += jnp.sum(upstream * scaled, axis=0, keepdims=True)
        weighted = upstream * m.rows[0:1, :]
        grad_mixer[line, :] = grad_hidden[line, :] + inverse * (
            weighted - scaled * jnp.mean(weighted * scaled, axis=-1, keepdims=True)
        )

    for q in range(2):
        saves.append(save(grad_mixer.at[128 * q : 128 * q + 128], result.input_grad.at[q]))

    for part in (0, 2, 1, 3):
        cubes[part][2].second()
    fed.four()
    downs.four()

    for d in range(16):
        tile = jnp.concatenate([m.sums[:, 64 * d : 64 * d + 64], jnp.zeros((8, 64), F32)], axis=1)
        m.small[d // 4, d % 4] = tile
    sent_y = [
        copies.start(m.small.at[wrap(y + k)], m.small_y.at[k], device) for k, device in zip(range(1, SIDE), along)
    ]
    for copy in sent_y:
        copy.wait_recv()
    for i in range(SIDE):
        total = m.small[y, i]
        for k in range(1, SIDE):
            total = total + m.small_y[k, i]
        m.small_one[i] = total
    sent_x = [
        copies.start(m.small_one.at[wrap(x + k)], m.small_x.at[k], device)
        for k, device in zip(range(1, SIDE), across)
    ]
    for part in (0, 2, 1, 3):
        cubes[part][2].finish()
        cubes[part][1].first()
    fed.finish(m.feed_wide)
    sent_feed = []
    for k, peer in enumerate(peers):
        line = pl.ds(pl.multiple_of(wrap(seq + k + 1, PEERS) * 8, 8), 8)
        sent_feed.append(copies.start(m.feed_wide.at[line], m.feed_land.at[seq], peer))
    m.feed_land[seq] = m.feed_wide[pl.ds(pl.multiple_of(seq * 8, 8), 8), :]
    downs.finish(m.down_wide)
    m.w_down[0:16, :] = m.down_wide[:, 0:1024]
    m.w_down[16:32, :] = m.down_wide[:, 1024:2048]
    for i in range(4):
        m.w_down[32:36, 256 * i : 256 * i + 256] = m.down_wide[4 * i : 4 * i + 4, 2048:PACKED]
    saves.append(save(m.w_down, result.g_down))
    for copy in sent_x:
        copy.wait_recv()
    total = m.small_one[x]
    for k in range(1, SIDE):
        total = total + m.small_x[k]
    m.small_two[...] = total
    sent_z = [copies.start(m.small_two, m.small_z.at[seq], peer) for peer in peers]
    m.small_z[seq] = total
    for part in (0, 2, 1, 3):
        cubes[part][1].second()
    for copy in sent_z:
        copy.wait_recv()
    m.g_small[...] = functools.reduce(lambda a, b: a + b, [m.small_z[s] for s in range(PEERS)])
    saves.append(save(m.g_small, result.g_small))
    for copy in sent_feed:
        copy.wait_recv()
    def spread(main, tail, target, output):
        for d in range(16):
            pieces = []
            for s in range(PEERS):
                line = m.feed_land[s]
                whole = jnp.concatenate([line[:, main : main + WIDE], line[:, tail : tail + 64]], axis=1)
                pieces.append(whole[:, OWN * d : OWN * d + OWN])
            target[:, 288 * d : 288 * d + 288] = jnp.concatenate(pieces, axis=1)
        saves.append(save(target, output))

    for part in (0, 2, 1, 3):
        cubes[part][1].finish()
        cubes[part][0].first()
    spread(0, 1024, m.w_gate, result.g_gate)
    for part in (0, 2, 1, 3):
        cubes[part][0].second()
    spread(WIDE, 1088, m.w_up, result.g_up)
    for part, (_, lanes, start, _) in enumerate(PARTS):
        cubes[part][0].finish(m.mix_wide.at[:, pl.ds(start, lanes.size)])
    theirs = pl.ds(pl.multiple_of((1 - core) * 8, 8), 8)
    mix_copy = copies.start(m.mix_wide.at[theirs], m.mix_land.at[core], partner)
    m.mix_land[core] = m.mix_wide[pl.ds(pl.multiple_of(core * 8, 8), 8), :]
    ring.finish(grad_hidden)
    m.mixer_in[...] = (m.hidden[...] + grad_hidden[...]).astype(BF)
    for q in range(2):
        saves.append(save(m.mixer_in.at[128 * q : 128 * q + 128], result.output.at[q]))
    mix_copy.wait_recv()
    for half in range(2):
        for k in range(3):
            m.w_in[:, 1024 * k + 512 * half : 1024 * k + 512 * half + 512] = m.mix_land[
                half, :, 512 * k + 512 : 512 * k + 1024
            ]
        m.w_out[:, 512 * half : 512 * half + 512] = m.mix_land[half, :, 0:512]
    saves.append(save(m.w_in, result.g_in))
    saves.append(save(m.w_out, result.g_out))
    for copy in saves:
        copy.wait()
    copies.drain()


def step(*operands):
    hbm, vmem = pl.BlockSpec(memory_space=pl.ANY), pl.BlockSpec(memory_space=pltpu.VMEM)
    return pl.pallas_call(
        step_kernel,
        out_shape=tuple(jax.ShapeDtypeStruct(*shape) for shape in RESULTS.values()),
        in_specs=[vmem if name in ("gains", "taps") else hbm for name in OPERANDS],
        out_specs=(hbm,) * len(RESULTS),
        scratch_shapes=[pltpu.VMEM(*shape) for shape in SCRATCH.values()]
        + [
            pltpu.SemaphoreType.REGULAR((2,)),
            pltpu.SemaphoreType.DMA((7,)),
            pltpu.SemaphoreType.DMA((10,)),
            pltpu.SemaphoreType.DMA((COPIES,)),
            pltpu.SemaphoreType.DMA((COPIES,)),
        ],
        compiler_params=pltpu.CompilerParams(
            collective_id=0, has_side_effects=True, vmem_limit_bytes=VMEM_BYTES
        ),
        name="step",
    )(*operands)


SHAPES = ((2, 8), (3, 8), (8, 3072), (8, 1024), (8, 4608), (8, 4608), (OWN, D))
RATES = ((rate_small, 0.0),) * 2 + ((rate_matrix, weight_decay),) * 5
TILED = 5


def adamw(weight, grad, first, second, rate, decay):
    first_new = beta_one * first + (1.0 - beta_one) * grad
    second_new = beta_two * second + (1.0 - beta_two) * grad * grad
    first_hat = first_new / (1.0 - beta_one**STEP)
    second_hat = second_new / (1.0 - beta_two**STEP)
    weight_new = weight - rate * (
        first_hat / (jnp.sqrt(second_hat) + epsilon_adam) + decay * weight
    )
    return (weight_new, first_new, second_new)


def adamw_kernel(*refs):
    weights, firsts, seconds, refs = refs[:7], refs[7:14], refs[14:21], refs[21:]
    small_grad, grads, finished, refs = refs[0], refs[1:6], refs[6:8], refs[8:]
    outs, final, refs = (refs[:7], refs[7:14], refs[14:21]), refs[21:23], refs[23:]
    held = [refs[5 * k : 5 * k + 5] for k in range(4)]
    through, (load_sem, save_sem) = refs[20:22], refs[22:]
    load, save = local_copies(load_sem), local_copies(save_sem)
    passing = [load(source, kept) for source, kept in zip(finished, through)]
    loads = []
    for index in range(TILED):
        sources = (grads[index], weights[index + 2], firsts[index + 2], seconds[index + 2])
        loads.append([load(source, kept[index]) for source, kept in zip(sources, held)])
    seq = lax.axis_index("seq")
    tile = pltpu.roll(small_grad[...], lax.rem(128 - seq * 8, 128), 1)
    for index, (start, count) in enumerate(((0, 2), (2, 3))):
        grad = tile[start : start + count, 0:8]
        new = adamw(weights[index][...], grad, firsts[index][...], seconds[index][...], *RATES[index])
        for out, value in zip(outs, new):
            out[index][...] = value
    saves = []
    for copy, kept, target in zip(passing, through, final):
        copy.wait()
        saves.append(save(kept, target))
    for index in range(TILED):
        for copy in loads[index]:
            copy.wait()
        grad, weight, first, second = (kept[index] for kept in held)
        rows, columns = weight.shape
        for start in range(0, columns, 512):
            lanes = slice(start, min(start + 512, columns))
            new = adamw(weight[:, lanes], grad[:, lanes], first[:, lanes], second[:, lanes], *RATES[index + 2])
            weight[:, lanes], first[:, lanes], second[:, lanes] = new
        for out, kept in zip(outs, (weight, first, second)):
            saves.append(save(kept, out[index + 2]))
    for copy in saves:
        copy.wait()


def adamw_all(weights, firsts, seconds, small_grad, grads, finished):
    hbm, vmem = pl.BlockSpec(memory_space=pl.ANY), pl.BlockSpec(memory_space=pltpu.VMEM)
    group = [vmem] * 2 + [hbm] * TILED
    return pl.pallas_call(
        adamw_kernel,
        out_shape=[jax.ShapeDtypeStruct(shape, F32) for shape in SHAPES] * 3
        + [jax.ShapeDtypeStruct(array.shape, array.dtype) for array in finished],
        in_specs=group * 3 + [vmem] + [hbm] * (TILED + 2),
        out_specs=group * 3 + [hbm] * 2,
        scratch_shapes=[pltpu.VMEM(shape, F32) for shape in SHAPES[2:]] * 4
        + [pltpu.VMEM(array.shape, array.dtype) for array in finished]
        + [pltpu.SemaphoreType.DMA((4 * TILED + 2,)), pltpu.SemaphoreType.DMA((3 * TILED + 2,))],
        compiler_params=pltpu.CompilerParams(vmem_limit_bytes=VMEM_BYTES),
        name="adamw",
    )(*weights, *firsts, *seconds, small_grad, *grads, *finished)


def shards(
    inputs, cotangent, norm_gains, conv_taps, w_in, w_out, w_gate, w_up, w_down,
    first_gains, first_taps, first_in, first_out, first_gate, first_up, first_down,
    second_gains, second_taps, second_in, second_out, second_gate, second_up, second_down,
):
    output, input_grad, red_in, red_out, red_gate, red_up, red_down, red_small = step(
        w_in, w_out, w_gate, w_up, w_down, norm_gains, conv_taps, inputs, cotangent.reshape(ROWS, D)
    )
    *new, output, input_grad = adamw_all(
        (norm_gains, conv_taps, w_in, w_out, w_gate, w_up, w_down),
        (first_gains, first_taps, first_in, first_out, first_gate, first_up, first_down),
        (second_gains, second_taps, second_in, second_out, second_gate, second_up, second_down),
        red_small,
        (red_in, red_out, red_gate, red_up, red_down),
        (output, input_grad),
    )
    return (output, input_grad, *new)


def solution(mesh):
    tokens, columns, rows = P("dp", "seq", None), P(None, ("dp", "seq")), P(("dp", "seq"), None)
    weights = (columns, columns, rows, rows, rows, rows, rows)
    return jax.shard_map(
        shards,
        mesh=mesh,
        in_specs=(tokens, tokens) + weights * 3,
        out_specs=(tokens, tokens) + weights * 3,
        check_vma=False,
    )
```

```python
import functools
import types

import jax
import jax.numpy as jnp
from jax import lax
from jax.experimental import pallas as pl
from jax.experimental.pallas import tpu as pltpu
from jax.sharding import PartitionSpec as P

D = 1024
STEP = 5

epsilon_norm = 1e-05
beta_one = 0.9
beta_two = 0.95
epsilon_adam = 1e-08
rate_matrix = 0.02
rate_small = 0.3
weight_decay = 0.1

MESH = pl.DeviceIdType.MESH
BF = jnp.bfloat16
F32 = jnp.float32
SIDE = 4
PEERS = 8
OWN = 36
PACKED = 2304
SLICE = 576
WIDE = 512
VMEM_BYTES = 62 * 2**20


def place():
    dp, seq = lax.axis_index("dp"), lax.axis_index("seq")
    return lax.rem(dp, SIDE), lax.div(dp, SIDE), lax.div(seq, 2), lax.rem(seq, 2)


def wrap(value, size=SIDE):
    return lax.rem(value + size, size)


def at(x, y, z, core):
    return (y * SIDE + x, z * 2 + core)


class Copies:
    def __init__(self, send, recv):
        self.send, self.recv, self.started, self.sent = send, recv, [], set()

    def plan(self, source, target, device):
        index = len(self.started)
        assert index < self.send.shape[0]
        copy = pltpu.make_async_remote_copy(
            src_ref=source,
            dst_ref=target,
            send_sem=self.send.at[index],
            recv_sem=self.recv.at[index],
            device_id=device,
            device_id_type=MESH,
        )
        self.started.append(copy)
        return copy

    def start(self, source, target, device):
        copy = self.plan(source, target, device)
        copy.start()
        return copy

    def drain(self, some=None):
        for copy in self.started if some is None else some:
            if id(copy) not in self.sent:
                self.sent.add(id(copy))
                copy.wait_send()


def seq_peers(x, y, z, core):
    seq = z * 2 + core
    return [(y * SIDE + x, wrap(seq + k, PEERS)) for k in range(1, PEERS)]


def halver(dim, low):
    def split(ref, part):
        size = ref.shape[dim]
        places = [slice(None)] * len(ref.shape)
        places[dim] = pl.ds(0, low) if part == 0 else pl.ds(low, size - low)
        return ref.at[tuple(places)]

    return split


class RingGather:
    def __init__(self, copies, me, to, block, split, fine=True):
        self.copies, self.me, self.to, self.block, self.split, self.fine = copies, me, to, block, split, fine

    def plan(self, source=None):
        source = self.block(self.me) if source is None else source
        below, above = wrap(self.me - 1), wrap(self.me + 1)

        def move(start, target, part, place):
            return self.copies.plan(self.split(start, part), self.split(target, part), self.to(place))

        mine, before, after = self.block(self.me), self.block(below), self.block(above)
        if self.fine:
            self.up = [move(source, mine, part, above) for part in range(2)]
            self.down = [move(source, mine, part, below) for part in range(2)]
        else:
            self.up = [self.copies.plan(source, mine, self.to(above))]
            self.down = [self.copies.plan(source, mine, self.to(below))]
        self.pass_up = move(before, before, 0, above)
        self.pass_down = move(after, after, 1, below)

    def first(self, source=None):
        if not hasattr(self, "up"):
            self.plan(source)
        self.up[0].start()
        self.down[-1].start()
        if self.fine:
            self.up[1].start()
            self.down[0].start()

    def second(self):
        self.up[0].wait_recv()
        self.pass_up.start()
        self.down[-1].wait_recv()
        self.pass_down.start()

    def wait_below(self):
        if self.fine:
            self.up[1].wait_recv()

    def wait_above(self):
        if self.fine:
            self.down[0].wait_recv()

    def wait_far(self):
        self.pass_up.wait_recv()
        self.pass_down.wait_recv()

    def finish(self):
        self.wait_below()
        self.wait_above()
        self.wait_far()

    def copies_made(self):
        return [*self.up, *self.down, self.pass_up, self.pass_down]


class RingReduce:
    def __init__(self, copies, me, to, block, split, landing, fine=True):
        self.copies, self.me, self.to, self.block, self.split, self.fine = copies, me, to, block, split, fine
        self.low_in, self.high_in, self.plus_in, self.minus_in = landing

    def plan(self):
        far, below, above = wrap(self.me + 2), wrap(self.me - 1), wrap(self.me + 1)
        plan, split = self.copies.plan, self.split
        self.far_up = plan(split(self.block(far), 0), self.low_in, self.to(above))
        self.far_down = plan(split(self.block(far), 1), self.high_in, self.to(below))
        if self.fine:
            self.up = [plan(split(self.block(above), k), split(self.plus_in, k), self.to(above)) for k in range(2)]
            self.down = [plan(split(self.block(below), k), split(self.minus_in, k), self.to(below)) for k in range(2)]
        else:
            self.up = [plan(self.block(above), self.plus_in, self.to(above))]
            self.down = [plan(self.block(below), self.minus_in, self.to(below))]

    def first_far(self):
        self.far_up.start()
        self.far_down.start()

    def first_above(self):
        self.up[1].start()

    def first_below(self):
        self.down[0].start()

    def first(self):
        if not hasattr(self, "up"):
            self.plan()
        self.first_far()
        if self.fine:
            self.first_above()
            self.first_below()

    def second(self):
        below, above = self.block(wrap(self.me - 1)), self.block(wrap(self.me + 1))
        self.far_up.wait_recv()
        accumulate(self.split(above, 0), self.split(above, 0), self.low_in)
        self.up[0].start()
        self.far_down.wait_recv()
        accumulate(self.split(below, 1), self.split(below, 1), self.high_in)
        self.down[-1].start()

    def copies_made(self):
        return [self.far_up, self.far_down, *self.up, *self.down]

    def finish(self, target=None):
        own = self.block(self.me)
        for copy in (*self.up, *self.down):
            copy.wait_recv()
        accumulate(own if target is None else target, own, self.plus_in, self.minus_in)


def accumulate(target, *sources):
    shape = target.shape
    if len(shape) > 2:
        for index in range(shape[0]):
            accumulate(target.at[index], *[source.at[index] for source in sources])
        return
    step = 16

    @pl.loop(0, shape[0] // step)
    def _(i):
        rows = pl.ds(pl.multiple_of(i * step, step), step)
        total = sources[0][rows, :].astype(F32)
        for source in sources[1:]:
            total = total + source[rows, :].astype(F32)
        target[rows, :] = total.astype(target.dtype)


def columns_of(seq, dp_count=16):
    return [(288 * d + OWN * seq, 36 * d) for d in range(dp_count)]


def dot(a, b, dims=((1,), (0,))):
    return lax.dot_general(a, b, (dims, ((), ())), preferred_element_type=F32)


NT = ((1,), (1,))
TN = ((0,), (0,))
ROWS = 256
PAIR = 512
EVERY = 272
HALF = 512


def by_rows(ref, which, part):
    start, size = (32 * which, 32) if part is None else (32 * which + 16 * part, 16)
    lead = [slice(None)] * (len(ref.shape) - 2)
    return ref.at[(*lead, pl.ds(start, size), slice(None))]


def rows_of(lanes):
    def halves(ref, which, part):
        rows = by_rows(ref, which, part)
        return rows.at[(*[slice(None)] * (len(rows.shape) - 1), lanes)]

    return halves


def by_columns(ref, which, part):
    first, size = ((0, 1152), (0, 640), (640, 512))[0 if part is None else part + 1]
    lead = [slice(None)] * (len(ref.shape) - 2)
    return ref.at[(*lead, slice(None), pl.ds(1152 * which + first, size))]


def visit(z, k):
    return wrap(z + k + lax.div(k, 2) * (5 - 2 * k))


def turn_of(z, chip):
    ahead = wrap(chip - z)
    return ahead + lax.div(ahead, 2) * (5 - 2 * ahead)


class PlaneGather:
    def __init__(self, copies, spot, view, halves, block, split, fine=True):
        x, y, z, core = spot
        to_x, to_y = (lambda i: at(i, y, z, core)), (lambda i: at(x, i, z, core))
        everything, fours = slice(None), halver(0, 2)
        self.x, self.y, self.view, self.halves = x, y, view, halves
        self.row_x = RingGather(copies, x, to_x, lambda i: halves(view(y, i), 0, None), split, False)
        self.row_y = RingGather(copies, y, to_y, lambda i: halves(view(i, x), 1, None), split, False)
        self.all_y = RingGather(copies, y, to_y, lambda i: halves(view(i, everything), 0, None), fours, fine)
        self.all_x = RingGather(copies, x, to_x, lambda i: halves(view(everything, i), 1, None), fours, fine)
        self.row_x.plan(halves(block, 0, None))
        self.row_y.plan(halves(block, 1, None))
        self.all_y.plan()
        self.all_x.plan()

    def one(self):
        self.row_x.first()
        self.row_y.first()

    def two(self):
        self.row_x.second()
        self.row_y.second()

    def three(self):
        self.row_x.finish()
        self.all_y.first()
        self.row_y.finish()
        self.all_x.first()

    def four(self):
        self.all_y.second()
        self.all_x.second()

    def finish(self):
        self.all_y.finish()
        self.all_x.finish()

    def wait_near(self, then):
        self.all_y.wait_below()
        self.all_x.wait_below()
        then(self, -1)
        self.all_y.wait_above()
        self.all_x.wait_above()
        then(self, 1)

    def copies(self):
        return [copy for ring in (self.row_x, self.row_y, self.all_y, self.all_x) for copy in ring.copies_made()]

    def group(self, which, step):
        everything = slice(None)
        if which == 0:
            return self.halves(self.view(wrap(self.y + step), everything), 0, None)
        return self.halves(self.view(everything, wrap(self.x + step)), 1, None)


PARTS = (
    (0, pl.ds(0, 512), 0, ("y", "z", "x")),
    (0, pl.ds(512, 512), 512, ("x", "y", "z")),
    (1, pl.ds(0, 512), 1024, ("z", "x", "y")),
    (1, pl.ds(512, 512), 1536, ("y", "z", "x")),
)


def first_half(width):
    return (width + 255) // 256 * 128


def cube_spots(spot, order):
    x, y, z, core = spot
    own = {"x": x, "y": y, "z": z}
    to = {
        "x": lambda i: at(i, y, z, core),
        "y": lambda i: at(x, i, z, core),
        "z": lambda i: at(x, y, i, core),
    }

    def view(ref, **places):
        return ref.at[tuple(places.get(axis, own[axis]) for axis in ("y", "x", "z"))]

    return [own[axis] for axis in order], [to[axis] for axis in order], view


def cube_rings(spot, order, ref, make):
    (a, b, c), (to_a, to_b, to_c), view = cube_spots(spot, order)
    one, two, three = order
    everything = slice(None)
    place_of = {"y": 0, "x": 1, "z": 2}
    first = make(a, to_a, lambda i: view(ref, **{one: i}), halver(-1, first_half(ref.shape[-1])), False)
    second = make(b, to_b, lambda i: view(ref, **{one: everything, two: i}), halver(0, 2), False)
    third = make(
        c, to_c,
        lambda i: view(ref, **{one: everything, two: everything, three: i}),
        halver(0 if place_of[two] < place_of[one] else 1, 2),
        True,
    )
    return first, second, third


def small_rows(small_all):
    pieces = [small_all[d // 4, d % 4][:, :64] for d in range(16)]
    return jnp.concatenate(pieces, axis=1)


def normalize(rows, gain):
    inverse = lax.rsqrt(jnp.mean(rows * rows, axis=-1, keepdims=True) + epsilon_norm)
    return rows * inverse * gain


def extend(extended, projected, half, sequence):
    first = pl.ds(ROWS + 8 * sequence, 8)
    main = pl.ds(128 * sequence, 128)
    extended[0:8, :] = projected[half, first, :HALF] * projected[half, first, 1024:]
    extended[8:136, :] = projected[half, main, :HALF] * projected[half, main, 1024:]


def convolve(extended, taps):
    return taps[0:1] * extended[6:134, :] + taps[1:2] * extended[7:135, :] + taps[2:3] * extended[8:136, :]


def half_lanes(half):
    return pl.ds(pl.multiple_of(half * HALF, HALF), HALF)


class PlaneReduce:
    def __init__(self, copies, spot, view, halves, split, landings):
        x, y, z, core = spot
        to_x, to_y = (lambda i: at(i, y, z, core)), (lambda i: at(x, i, z, core))
        everything, fours = slice(None), halver(0, 2)
        self.halves = halves
        self.all_y = RingReduce(copies, y, to_y, lambda i: halves(view(i, everything), 0, None), fours, landings[0:4])
        self.all_x = RingReduce(copies, x, to_x, lambda i: halves(view(everything, i), 1, None), fours, landings[4:8])
        self.row_x = RingReduce(copies, x, to_x, lambda i: halves(view(y, i), 0, None), split, landings[8:12], False)
        self.row_y = RingReduce(copies, y, to_y, lambda i: halves(view(i, x), 1, None), split, landings[12:16], False)

    def one(self):
        self.all_y.first()
        self.all_x.first()

    def two(self):
        self.all_y.second()
        self.all_x.second()

    def three(self):
        self.all_y.finish()
        self.row_x.first()
        self.all_x.finish()
        self.row_y.first()

    def four(self):
        self.row_x.second()
        self.row_y.second()

    def finish(self, target):
        self.row_x.finish(self.halves(target, 0, None))
        self.row_y.finish(self.halves(target, 1, None))


def plane_landings(ref):
    wide = lambda count, blocks, rows: ref.reshape(count, blocks, rows, 1152)
    single = lambda rows: ref.reshape(2048 // rows, rows, 1152)
    fed, downs = [], []
    for k in range(2):
        fed += [wide(32, 2, 32).at[8 + 2 * k], wide(32, 2, 32).at[9 + 2 * k]]
        fed += [wide(16, 4, 32).at[2 * k], wide(16, 4, 32).at[2 * k + 1]]
        downs += [wide(64, 2, 16).at[38 + 2 * k], wide(64, 2, 16).at[39 + 2 * k]]
        downs += [wide(32, 4, 16).at[15 + 2 * k], wide(32, 4, 16).at[16 + 2 * k]]
    for k in range(2):
        fed += [single(16).at[56 + 2 * k], single(16).at[57 + 2 * k], single(32).at[24 + 2 * k], single(32).at[25 + 2 * k]]
        downs += [single(16).at[88 + 2 * k, :, pl.ds(0, 640)], single(16).at[89 + 2 * k, :, pl.ds(0, 512)]]
        downs += [single(16).at[84 + 2 * k], single(16).at[85 + 2 * k]]
    return fed, downs


def cube_landings(ref, lanes, order):
    width, total = lanes.size, ref.shape[-1]
    place_of = {"y": 0, "x": 1, "z": 2}
    halved = (2, 4) if place_of[order[1]] < place_of[order[0]] else (4, 2)

    def take(count, lead, index, part=None):
        window = lanes
        if part is not None:
            low = first_half(width)
            window = pl.ds(lanes.start, low) if part == 0 else pl.ds(lanes.start, width - low)
        places = (slice(None),) * (len(lead) + 1)
        return ref.reshape(count, *lead, 16, total).at[(index, *places, window)]

    first = [take(64, (), 60, 0), take(64, (), 61, 1), take(64, (), 62), take(64, (), 63)]
    second = [take(32, (2,), 24), take(32, (2,), 25), take(16, (4,), 13), take(16, (4,), 14)]
    third = [take(8, halved, 4), take(8, halved, 5), take(4, (4, 4), 0), take(4, (4, 4), 1)]
    return first, second, third


def local_copies(semaphores):
    count = iter(range(semaphores.shape[0]))

    def start(source, target):
        copy = pltpu.make_async_copy(source, target, semaphores.at[next(count)])
        copy.start()
        return copy

    return start


OPERANDS = ("w_in", "w_out", "w_gate", "w_up", "w_down", "gains", "taps", "inputs", "cotangent")
RESULTS = {
    "output": ((2, 128, D), BF),
    "input_grad": ((2, 128, D), F32),
    "g_in": ((8, 3072), F32),
    "g_out": ((8, 1024), F32),
    "g_gate": ((8, 4608), F32),
    "g_up": ((8, 4608), F32),
    "g_down": ((OWN, D), F32),
    "g_small": ((8, 128), F32),
}
SCRATCH = {
    "w_in": ((8, 3072), F32),
    "w_out": ((8, 1024), F32),
    "w_gate": ((8, 4608), F32),
    "w_up": ((8, 4608), F32),
    "w_down": ((OWN, D), F32),
    "tile": ((8, 128), F32),
    "inputs": ((2, 128, D), BF),
    "mix": ((2, 4, 4, 64, 2048), BF),
    "feed": ((4, 4, 64, 2 * SLICE), BF),
    "down": ((4, 4, 16, PACKED), BF),
    "small_all": ((4, 4, 8, 128), F32),
    "edge_in": ((2, 16, D), BF),
    "tokens": ((SIDE, 2, ROWS, D), BF),
    "grads": ((SIDE, 2, ROWS, D), BF),
    "mix_send": ((2, 16, D), BF),
    "feed_send": ((PEERS, 16, 640), BF),
    "mix_got": ((PEERS, 16, D), BF),
    "feed_got": ((PEERS, 16, 640), BF),
    "small_got": ((PEERS, 8, 128), F32),
    "mix_block": ((64, 2048), BF),
    "feed_block": ((64, 2 * SLICE), BF),
    "down_block": ((16, PACKED), BF),
    "small_send": ((8, 128), F32),
    "rows": ((8, D), F32),
    "normed": ((EVERY, D), BF),
    "projected": ((2, EVERY, 1536), F32),
    "extended": ((136, HALF), F32),
    "mixer_in": ((ROWS, D), BF),
    "hidden": ((ROWS, D), F32),
    "normed_two": ((ROWS, D), BF),
    "down_rows": ((SLICE, D), BF),
    "narrow_wide": ((160, D), F32),
    "value": ((PAIR, 2 * SLICE), F32),
    "grad_active": ((PAIR, SLICE), F32),
    "active": ((2048, SLICE), BF),
    "grad_value": ((2048, 2 * SLICE), BF),
    "part": ((SIDE, 2, ROWS, D), BF),
    "part_out": ((SIDE, 2, ROWS, D), BF),
    "landing": ((SIDE, ROWS, D), BF),
    "landing_left": ((SIDE, ROWS, HALF), BF),
    "landing_right": ((SIDE, ROWS, HALF), BF),
    "low_in": ((128, D), BF),
    "high_in": ((128, D), BF),
    "plus_in": ((ROWS, D), BF),
    "minus_in": ((ROWS, D), BF),
    "low_out": ((128, D), BF),
    "high_out": ((128, D), BF),
    "plus_out": ((ROWS, D), BF),
    "minus_out": ((ROWS, D), BF),
    "down_part": ((SLICE, 256), F32),
    "down_tail": ((16, 16, 256), F32),
    "grad_conv": ((2, 136, D), F32),
    "grad_x": ((2, ROWS, HALF), BF),
    "edge_send": ((2, 8, D), F32),
    "edge_got": ((2, 8, D), F32),
    "sums": ((8, D), F32),
    "mix_wide": ((16, 2048), F32),
    "feed_wide": ((64, 2 * SLICE), F32),
    "down_wide": ((16, PACKED), F32),
    "mix_land": ((2, 8, 2048), F32),
    "feed_land": ((PEERS, 8, 2 * SLICE), F32),
    "small": ((4, 4, 8, 128), F32),
    "small_y": ((4, 4, 8, 128), F32),
    "small_x": ((4, 8, 128), F32),
    "small_z": ((PEERS, 8, 128), F32),
    "small_one": ((4, 8, 128), F32),
    "small_two": ((8, 128), F32),
    "g_small": ((8, 128), F32),
}
COPIES = 448


def step_kernel(*refs):
    count = len(OPERANDS)
    given = types.SimpleNamespace(**dict(zip(OPERANDS, refs)))
    result = types.SimpleNamespace(**dict(zip(RESULTS, refs[count:])))
    count += len(RESULTS)
    m = types.SimpleNamespace(**dict(zip(SCRATCH, refs[count:])))
    ready, load_sem, save_sem, send, recv = refs[count + len(SCRATCH) :]

    spot = x, y, z, core = place()
    seq = z * 2 + core
    copies = Copies(send, recv)
    peers = seq_peers(x, y, z, core)
    across = [at(wrap(x + k), y, z, core) for k in range(1, SIDE)]
    along = [at(x, wrap(y + k), z, core) for k in range(1, SIDE)]
    partner = at(x, y, z, 1 - core)
    load = local_copies(load_sem)
    loads = {
        "w_in": load(given.w_in, m.w_in),
        "w_out": load(given.w_out, m.w_out),
        "w_gate": load(given.w_gate, m.w_gate),
        "w_up": load(given.w_up, m.w_up),
        "w_down": load(given.w_down, m.w_down),
        "inputs": load(given.inputs, m.inputs),
        "cotangent": load(given.cotangent, m.grads.at[z, core]),
    }
    barrier = pltpu.get_barrier_semaphore()
    for device in peers + across + along:
        pl.semaphore_signal(barrier, inc=1, device_id=device, device_id_type=MESH)

    def to_z(i):
        return at(x, y, i, core)

    loads["w_in"].wait()
    loads["w_out"].wait()
    for half in range(2):
        parts = [m.w_out[:, 512 * half : 512 * half + 512]]
        parts += [m.w_in[:, 1024 * k + 512 * half : 1024 * k + 512 * half + 512] for k in range(3)]
        upper = jnp.concatenate(parts[:2], axis=1)
        lower = jnp.concatenate(parts[2:], axis=1)
        m.mix_send[half] = jnp.concatenate([upper, lower], axis=0).astype(BF)
    pl.semaphore_wait(barrier, len(peers + across + along))
    mix_copies = []
    for k, peer in enumerate(peers):
        other = wrap(seq + k + 1, PEERS)
        mix_copies.append(copies.start(m.mix_send.at[lax.rem(other, 2)], m.mix_got.at[seq], peer))
    m.mix_got[seq] = m.mix_send[core]
    mixed, mixed_out = (
        PlaneGather(copies, spot, lambda i, j: m.mix.at[core, i, j], rows_of(lanes), m.mix_block, halver(-2, 16))
        for lanes in (pl.ds(HALF, 1536), pl.ds(0, HALF))
    )
    fed = PlaneGather(copies, spot, lambda i, j: m.feed.at[i, j], by_rows, m.feed_block, halver(-2, 16))
    downs = PlaneGather(copies, spot, lambda i, j: m.down.at[i, j], by_columns, m.down_block, halver(-1, 640), False)
    loads["w_down"].wait()
    for i in range(4):
        m.narrow_wide[4 * i : 4 * i + 4, 0:256] = m.w_down[32:36, 256 * i : 256 * i + 256]
    m.down_block[:, 0:1024] = m.w_down[0:16, :].astype(BF)
    m.down_block[:, 1024:2048] = m.w_down[16:32, :].astype(BF)
    m.down_block[:, 2048:PACKED] = m.narrow_wide[0:16, 0:256].astype(BF)
    m.down[y, x] = m.down_block[...]
    downs.one()
    m.tile[...] = jnp.zeros_like(m.tile)
    m.tile[0:2, 0:8] = given.gains[...].astype(BF).astype(F32)
    m.tile[2:5, 0:8] = given.taps[...].astype(BF).astype(F32)
    m.small_got[seq] = pltpu.roll(m.tile[...], seq * 8, 1)
    small_copies = [copies.start(m.small_got.at[seq], m.small_got.at[seq], peer) for peer in peers]
    edge_copy = copies.start(
        given.inputs.at[:, pl.ds(112, 16)], m.edge_in, (y * SIDE + x, wrap(seq + 1, PEERS))
    )
    ring = RingGather(
        copies, z, to_z,
        lambda i: m.grads.at[i, core],
        halver(0, 128),
    )
    ring.plan(given.cotangent)

    def slices(which):
        for s in which:
            gate = jnp.concatenate([m.w_gate[:, a : a + OWN] for a, _ in columns_of(s)], axis=1)
            up = jnp.concatenate([m.w_up[:, a : a + OWN] for a, _ in columns_of(s)], axis=1)
            tail = jnp.concatenate([gate[:, WIDE:], up[:, WIDE:]], axis=1)
            upper = jnp.concatenate([gate[:, :WIDE], up[:, :128]], axis=1)
            lower = jnp.concatenate([up[:, 128:WIDE], tail, jnp.zeros((8, 128), F32)], axis=1)
            m.feed_send[s] = jnp.concatenate([upper, lower], axis=0).astype(BF)

    loads["w_gate"].wait()
    loads["w_up"].wait()
    slices(range(PEERS))
    feed_copies = []
    for k, peer in enumerate(peers):
        other = wrap(seq + k + 1, PEERS)
        feed_copies.append(copies.start(m.feed_send.at[other], m.feed_got.at[seq], peer))
    m.feed_got[seq] = m.feed_send[seq]
    downs.two()
    for copy in mix_copies:
        copy.wait_recv()
    for k in range(4):
        a, b = m.mix_got[2 * k].astype(F32), m.mix_got[2 * k + 1].astype(F32)
        line = slice(16 * k, 16 * k + 16)
        m.mix_block[line, :1024] = jnp.concatenate([a[:8], b[:8]], axis=0).astype(BF)
        m.mix_block[line, 1024:] = jnp.concatenate([a[8:], b[8:]], axis=0).astype(BF)
    mixed.one()
    mixed_out.one()
    downs.three()
    m.mix[core, y, x] = m.mix_block[...]

    for copy in feed_copies:
        copy.wait_recv()
    for k in range(4):
        a, b = m.feed_got[2 * k].astype(F32), m.feed_got[2 * k + 1].astype(F32)
        line = slice(16 * k, 16 * k + 16)
        m.feed_block[line, :640] = jnp.concatenate([a[:8], b[:8]], axis=0).astype(BF)
        m.feed_block[line, 640:] = jnp.concatenate([a[8:, :512], b[8:, :512]], axis=0).astype(BF)
    m.feed[y, x] = m.feed_block[...]
    fed.one()
    ring.first()
    cotangent_ring = ring
    grads_passed = [copies.start(given.cotangent, m.grads.at[z, core], partner)]
    mixed.two()
    mixed_out.two()
    for copy in small_copies:
        copy.wait_recv()
    m.small_send[...] = functools.reduce(lambda a, b: a + b, [m.small_got[s] for s in range(PEERS)])
    small_x = [copies.start(m.small_send, m.small_all.at[y, x], device) for device in across]
    m.small_all[y, x] = m.small_send[...]
    mixed.three()
    mix_passed = []

    def pass_on(gather, step):
        for which in range(2):
            part = gather.group(which, step)
            mix_passed.append(copies.start(part, part, partner))

    pass_on(mixed, 0)
    fed.two()
    downs.four()
    for copy in small_x:
        copy.wait_recv()
    small_y = [copies.start(m.small_all.at[y], m.small_all.at[y], device) for device in along]
    for copy in small_y:
        copy.wait_recv()
    m.rows[...] = small_rows(m.small_all)
    loads["inputs"].wait()
    for q in range(2):
        m.normed[128 * q : 128 * q + 128, :] = normalize(m.inputs[q].astype(F32), m.rows[0:1, :]).astype(BF)
    edge_copy.wait_recv()
    inside = (seq > 0).astype(F32)
    earlier = [normalize(m.edge_in[q].astype(F32)[8:], m.rows[0:1, :]) * inside for q in range(2)]
    m.normed[ROWS:EVERY, :] = jnp.concatenate(earlier, axis=0).astype(BF)
    ring.second()
    mixed.four()
    mixed_out.three()
    mixed.wait_near(pass_on)
    mixed.all_y.wait_far()
    mixed.all_x.wait_far()
    pass_on(mixed, 2)
    mixed_out.four()
    fed.three()
    for turn in range(2):
        if turn == 1:
            for copy in mix_passed[:8]:
                copy.wait_recv()
        half = core if turn == 0 else 1 - core
        m.projected[half] = dot(m.normed[...], m.mix.at[half].reshape(D, 2048)[:, HALF:])
        lanes = half_lanes(half)
        for q in range(2):
            main = slice(128 * q, 128 * q + 128)
            extend(m.extended, m.projected, half, q)
            convolved = convolve(m.extended, m.rows[2:5, lanes])
            m.mixer_in[main, lanes] = (m.projected[half, main, HALF:1024] * convolved).astype(BF)
    pass_on(mixed_out, 0)
    mixed_out.wait_near(pass_on)
    mixed_out.all_y.wait_far()
    mixed_out.all_x.wait_far()
    pass_on(mixed_out, 2)
    for copy in mix_passed[8:]:
        copy.wait_recv()
    weights = [m.mix.at[half].reshape(D, 2048) for half in range(2)]
    for half in range(2):
        lanes = slice(HALF * half, HALF * half + HALF)
        mixed_out = dot(m.mixer_in[...], weights[half][:, :HALF])
        for q in range(2):
            main = slice(128 * q, 128 * q + 128)
            m.hidden[main, lanes] = m.inputs[q, :, lanes].astype(F32) + mixed_out[main]
    m.normed_two[...] = normalize(m.hidden[...], m.rows[1:2, :]).astype(BF)

    around = RingGather(
        copies, z, to_z,
        lambda i: m.tokens.at[i, core],
        halver(0, 128),
    )
    around.plan(m.normed_two)
    passed = [copies.plan(m.normed_two, m.tokens.at[z, core], partner)]
    for step in (1, 3, 2):
        chunk = m.tokens.at[wrap(z + step), core]
        passed.append(copies.plan(chunk, chunk, partner))
    around.first()
    passed[0].start()
    m.tokens[z, core] = m.normed_two[...]
    fed.four()
    ring.finish()
    for step in (1, 3, 2):
        chunk = m.grads.at[wrap(z + step), core]
        grads_passed.append(copies.start(chunk, chunk, partner))
    gives, gives_left, gives_right = [], [], []
    for k in range(SIDE):
        theirs = m.part_out.at[k, 1 - core]
        gives.append(copies.plan(m.part.at[k, 1 - core], m.landing.at[k], partner))
        gives_left.append(copies.plan(theirs.at[:, 0:HALF], m.landing_left.at[k], partner))
        gives_right.append(copies.plan(theirs.at[:, HALF:D], m.landing_right.at[k], partner))
    reduce = RingReduce(
        copies, z, to_z,
        lambda i: m.part.at[turn_of(z, i), core],
        halver(0, 128),
        (m.low_in, m.high_in, m.plus_in, m.minus_in),
    )
    reduce.plan()
    downs.finish()
    for i in range(SIDE):
        for d in range(SIDE):
            packed = m.down[i, d].astype(F32)
            m.narrow_wide[OWN * d : OWN * d + 16, :] = packed[:, 0:1024]
            m.narrow_wide[OWN * d + 16 : OWN * d + 32, :] = packed[:, 1024:2048]
            for k in range(4):
                m.narrow_wide[OWN * d + 32 : OWN * d + 36, 256 * k : 256 * k + 256] = packed[4 * k : 4 * k + 4, 2048:]
        m.down_rows[144 * i : 144 * i + 144, :] = m.narrow_wide[0:144, :].astype(BF)
    for copy in grads_passed:
        copy.wait_recv()
    loads["cotangent"].wait()
    fed.finish()
    feed = m.feed.reshape(D, 2 * SLICE)

    def settle(step):
        gives[step].wait_recv()
        accumulate(m.part.at[step, core], m.part.at[step, core], m.landing.at[step])
        if step == 1:
            reduce.first_above()
        if step == 2:
            reduce.first_below()
        if step == 3:
            reduce.first_far()

    def output_part(step):
        lines = pl.ds(pl.multiple_of(visit(z, step) * PAIR, PAIR), PAIR)
        m.part_out.at[step].reshape(PAIR, D)[...] = dot(m.active[lines, :], m.down_rows[...]).astype(BF)
        gives_left[step].start()
        gives_right[step].start()

    @pl.loop(0, SIDE)
    def _(k):
        @pl.when(k == 0)
        def _():
            passed[0].wait_recv()

        @pl.when(k == 1)
        def _():
            around.second()
            around.wait_above()
            passed[1].start()
            around.wait_below()
            passed[2].start()
            passed[1].wait_recv()

        @pl.when(k == 2)
        def _():
            passed[2].wait_recv()
            around.wait_far()
            passed[3].start()

        @pl.when(k == 3)
        def _():
            passed[3].wait_recv()

        chip = visit(z, k)
        m.value[...] = dot(m.tokens.at[chip].reshape(PAIR, D)[...], feed[...])
        m.grad_active[...] = dot(m.grads.at[chip].reshape(PAIR, D)[...], m.down_rows[...], NT)
        for step in range(SIDE - 1):
            @pl.when(k == step + 1)
            def _(step=step):
                settle(step)

        base = chip * PAIR

        @pl.loop(0, PAIR // 64)
        def _(r):
            line = pl.ds(pl.multiple_of(r * 64, 64), 64)
            target = pl.ds(pl.multiple_of(base + r * 64, 64), 64)
            tail = m.value[line, 1024:1152]
            ends = []
            for gate, up, back, where in (
                (m.value[line, :WIDE], m.value[line, WIDE:1024], m.grad_active[line, :WIDE], slice(0, WIDE)),
                (tail[:, :64], tail[:, 64:], m.grad_active[line, WIDE:], slice(WIDE, SLICE)),
            ):
                sigmoid = jax.nn.sigmoid(gate)
                soft = gate * sigmoid
                m.active[target, where] = (soft * up).astype(BF)
                grad_up = (back * soft).astype(BF)
                grad_gate = (back * up * (sigmoid * (1.0 + gate * (1.0 - sigmoid)))).astype(BF)
                ends.append((grad_gate, grad_up))
            m.grad_value[target, :WIDE] = ends[0][0]
            m.grad_value[target, WIDE:1024] = ends[0][1]
            m.grad_value[target, 1024:1088] = ends[1][0]
            m.grad_value[target, 1088:1152] = ends[1][1]

        lines = pl.ds(pl.multiple_of(base, PAIR), PAIR)
        m.part.at[k].reshape(PAIR, D)[...] = dot(m.grad_value[lines, :], feed[...], NT).astype(BF)
        for step in range(SIDE):
            @pl.when(k == step)
            def _(step=step):
                gives[step].start()

    output_part(0)
    output_part(1)
    settle(3)
    copies.drain(fed.copies())
    copies.drain(downs.copies())
    every_grad, every_token = m.grads.reshape(2048, D), m.tokens.reshape(2048, D)

    @pl.loop(0, 4)
    def _(n):
        columns = pl.ds(pl.multiple_of(n * 256, 256), 256)
        feed[columns, :] = dot(every_token[:, columns], m.grad_value[...], TN).astype(BF)

    plane_neighbours = [at(wrap(x + 1), y, z, core), at(wrap(x - 1), y, z, core)]
    plane_neighbours += [at(x, wrap(y + 1), z, core), at(x, wrap(y - 1), z, core)]
    for device in plane_neighbours:
        pl.semaphore_signal(ready.at[0], inc=1, device_id=device, device_id_type=MESH)
    reduce.second()

    def down_columns(n):
        columns = slice(256 * n, 256 * n + 256)
        m.down_part[...] = dot(m.active[...], every_grad[:, columns], TN)
        for d in range(16):
            block = m.down.at[d // 4, d % 4]
            block[:, columns] = m.down_part[OWN * d : OWN * d + 16, :].astype(BF)
            block[:, 1024 + 256 * n : 1280 + 256 * n] = m.down_part[OWN * d + 16 : OWN * d + 32, :].astype(BF)
            m.down_tail[d, 4 * n : 4 * n + 4, :] = m.down_part[OWN * d + 32 : OWN * d + 36, :]

    fed_landings, down_landings = plane_landings(m.grad_value)
    fed = PlaneReduce(copies, spot, lambda i, j: m.feed.at[i, j], by_rows, halver(-2, 16), fed_landings)
    downs = PlaneReduce(copies, spot, lambda i, j: m.down.at[i, j], by_columns, halver(-1, 640), down_landings)
    down_columns(0)
    pl.semaphore_wait(ready.at[0], len(plane_neighbours))
    fed.one()
    output_part(2)
    output_part(3)
    for n in range(1, 4):
        down_columns(n)
    for d in range(16):
        m.down[d // 4, d % 4, :, 2048:PACKED] = m.down_tail[d].astype(BF)
    downs.one()
    for k in range(SIDE):
        gives_left[k].wait_recv()
        gives_right[k].wait_recv()
        ours = m.part_out.at[k, core]
        accumulate(ours.at[:, 0:HALF], ours.at[:, 0:HALF], m.landing_left.at[k])
        accumulate(ours.at[:, HALF:D], ours.at[:, HALF:D], m.landing_right.at[k])
    ring = RingReduce(
        copies, z, to_z,
        lambda i: m.part_out.at[turn_of(z, i), core],
        halver(0, 128),
        (m.low_out, m.high_out, m.plus_out, m.minus_out),
    )
    ring.first()
    grad_hidden = m.value.at[0:ROWS, 0:D]
    grad_mixer = m.value.at[ROWS : 2 * ROWS, 0:D]
    reduce.finish(grad_hidden)

    copies.drain(gives + gives_left + gives_right + reduce.copies_made() + around.copies_made() + passed)
    copies.drain(grads_passed)
    copies.drain(cotangent_ring.copies_made())
    neighbours = plane_neighbours + [at(x, y, wrap(z + 1), core), at(x, y, wrap(z - 1), core), partner]
    for device in neighbours:
        pl.semaphore_signal(ready.at[1], inc=1, device_id=device, device_id_type=MESH)

    sum_blocks = m.grads.reshape(2, 4, 4, 4, 16, D)

    def flat_views(ref):
        return [ref.reshape(2, D, D).at[group, :, lanes] for group, lanes, _, _ in PARTS]

    sum_flat, give_flat, got_flat = flat_views(m.grads), flat_views(m.tokens), flat_views(m.part)
    cubes = []
    buffers = (m.landing, m.landing, m.landing_left, m.landing_right)
    for (group, lanes, _, order), buffer in zip(PARTS, buffers):
        room = lanes if buffer is m.landing else pl.ds(0, lanes.size)
        lands = iter(cube_landings(buffer, room, order))

        def make(me, to, block, split, fine, lands=lands):
            return RingReduce(copies, me, to, block, split, next(lands), fine)

        cubes.append(cube_rings(spot, order, sum_blocks.at[group, :, :, :, :, lanes], make))
    save = local_copies(save_sem)
    saves = []

    m.sums[...] = jnp.zeros_like(m.sums)
    narrow = m.normed_two

    @pl.loop(0, 8)
    def _(n):
        line = pl.ds(pl.multiple_of(n * 32, 32), 32)
        tokens = m.hidden[line, :]
        inverse = lax.rsqrt(jnp.mean(tokens * tokens, axis=-1, keepdims=True) + epsilon_norm)
        scaled = tokens * inverse
        upstream = grad_hidden[line, :]
        m.sums[1:2, :] += jnp.sum(upstream * scaled, axis=0, keepdims=True)
        weighted = upstream * m.rows[1:2, :]
        total = m.grads[z, core, line, :].astype(F32) + inverse * (
            weighted - scaled * jnp.mean(weighted * scaled, axis=-1, keepdims=True)
        )
        grad_hidden[line, :] = total
        narrow[line, :] = total.astype(BF)

    before = m.normed.at[0:ROWS]
    grad_bc = m.grad_value.reshape(8, ROWS, 2 * SLICE)
    given_parts = {}

    def gradient(part, give):
        half = 1 - core if give else core
        target = (give_flat if give else sum_flat)[part]
        left = m.mixer_in if part == 0 else before
        right = (
            lambda: narrow[:, half_lanes(half)],
            lambda: grad_bc[6 + half, :, 0:HALF],
            lambda: grad_bc[6 + half, :, HALF:D],
            lambda: m.grad_x[half],
        )[part]

        @pl.loop(0, 4)
        def _(n):
            columns = pl.ds(pl.multiple_of(n * 256, 256), 256)
            target[columns, :] = dot(left[:, columns], right(), TN).astype(BF)

        if give:
            given_parts[part] = copies.start(target, got_flat[part], partner)

    def pass_to_cube(part):
        given_parts[part].wait_recv()
        accumulate(sum_flat[part], sum_flat[part], got_flat[part])
        cubes[part][2].first()

    pl.semaphore_wait(ready.at[1], len(neighbours))
    gradient(0, True)
    grad_mixer[...] = dot(narrow[:, :HALF], weights[0][:, :HALF], NT) + dot(narrow[:, HALF:], weights[1][:, :HALF], NT)
    for q in range(2):
        for half in range(2):
            lanes = slice(HALF * half, HALF * half + HALF)
            start = slice(128 * q, 128 * q + 8)
            m.edge_send[q, :, lanes] = grad_mixer[start, lanes] * m.projected[half, start, HALF:1024]
    edge_copy = copies.start(m.edge_send, m.edge_got, (y * SIDE + x, wrap(seq - 1, PEERS)))
    gradient(0, False)
    fed.two()
    for half in range(2):
        lanes = slice(HALF * half, HALF * half + HALF)
        for q in range(2):
            main = slice(128 * q, 128 * q + 128)
            extend(m.extended, m.projected, half, q)
            upstream = grad_mixer[main, lanes]
            grad_bc[6 + half, main, HALF:D] = (upstream * convolve(m.extended, m.rows[2:5, lanes])).astype(BF)
            m.grad_conv[q, 0:128, lanes] = upstream * m.projected[half, main, HALF:1024]
    gradient(2, True)
    pass_to_cube(0)
    edge_copy.wait_recv()
    inside = (seq < PEERS - 1).astype(F32)
    for q in range(2):
        m.grad_conv[q, 128:136, :] = m.edge_got[q] * inside
        main = slice(128 * q, 128 * q + 128)
        for half in range(2):
            lanes = slice(HALF * half, HALF * half + HALF)
            taps = m.rows[2:5, lanes]
            gated = (
                taps[2:3] * m.grad_conv[q, 0:128, lanes]
                + taps[1:2] * m.grad_conv[q, 1:129, lanes]
                + taps[0:1] * m.grad_conv[q, 2:130, lanes]
            )
            grad_bc[6 + half, main, 0:HALF] = (gated * m.projected[half, main, 1024:]).astype(BF)
            m.grad_x[half, main, :] = (gated * m.projected[half, main, :HALF]).astype(BF)
    gradient(1, True)
    gradient(3, True)
    gradient(2, False)
    pass_to_cube(2)
    downs.two()
    ring.second()
    gradient(1, False)
    pass_to_cube(1)
    gradient(3, False)
    pass_to_cube(3)
    for half in range(2):
        lanes = slice(HALF * half, HALF * half + HALF)
        for q in range(2):
            extend(m.extended, m.projected, half, q)
            back = m.grad_conv[q, 0:128, lanes]
            for k in range(3):
                m.sums[2 + k : 3 + k, lanes] += jnp.sum(back * m.extended[6 + k : 134 + k, :], axis=0, keepdims=True)
    fed.three()
    downs.three()

    grad_mixer[...] = dot(grad_bc[6, :, 0:D], weights[0][:, HALF:1536], NT)
    grad_mixer[...] += dot(grad_bc[7, :, 0:D], weights[1][:, HALF:1536], NT)
    grad_mixer[...] += dot(m.grad_x[0], weights[0][:, 1536:], NT) + dot(m.grad_x[1], weights[1][:, 1536:], NT)

    @pl.loop(0, 8)
    def _(n):
        line = pl.ds(pl.multiple_of(n * 32, 32), 32)
        tokens = m.inputs.reshape(ROWS, D)[line, :].astype(F32)
        inverse = lax.rsqrt(jnp.mean(tokens * tokens, axis=-1, keepdims=True) + epsilon_norm)
        scaled = tokens * inverse
        upstream = grad_mixer[line, :]
        m.sums[0:1, :] += jnp.sum(upstream * scaled, axis=0, keepdims=True)
        weighted = upstream * m.rows[0:1, :]
        grad_mixer[line, :] = grad_hidden[line, :] + inverse * (
            weighted - scaled * jnp.mean(weighted * scaled, axis=-1, keepdims=True)
        )

    for q in range(2):
        saves.append(save(grad_mixer.at[128 * q : 128 * q + 128], result.input_grad.at[q]))

    for part in (0, 2, 1, 3):
        cubes[part][2].second()
    fed.four()
    downs.four()

    for d in range(16):
        tile = jnp.concatenate([m.sums[:, 64 * d : 64 * d + 64], jnp.zeros((8, 64), F32)], axis=1)
        m.small[d // 4, d % 4] = tile
    sent_y = [
        copies.start(m.small.at[wrap(y + k)], m.small_y.at[k], device) for k, device in zip(range(1, SIDE), along)
    ]
    for copy in sent_y:
        copy.wait_recv()
    for i in range(SIDE):
        total = m.small[y, i]
        for k in range(1, SIDE):
            total = total + m.small_y[k, i]
        m.small_one[i] = total
    sent_x = [
        copies.start(m.small_one.at[wrap(x + k)], m.small_x.at[k], device)
        for k, device in zip(range(1, SIDE), across)
    ]
    for part in (0, 2, 1, 3):
        cubes[part][2].finish()
        cubes[part][1].first()
    fed.finish(m.feed_wide)
    sent_feed = []
    for k, peer in enumerate(peers):
        line = pl.ds(pl.multiple_of(wrap(seq + k + 1, PEERS) * 8, 8), 8)
        sent_feed.append(copies.start(m.feed_wide.at[line], m.feed_land.at[seq], peer))
    m.feed_land[seq] = m.feed_wide[pl.ds(pl.multiple_of(seq * 8, 8), 8), :]
    downs.finish(m.down_wide)
    m.w_down[0:16, :] = m.down_wide[:, 0:1024]
    m.w_down[16:32, :] = m.down_wide[:, 1024:2048]
    for i in range(4):
        m.w_down[32:36, 256 * i : 256 * i + 256] = m.down_wide[4 * i : 4 * i + 4, 2048:PACKED]
    saves.append(save(m.w_down, result.g_down))
    for copy in sent_x:
        copy.wait_recv()
    total = m.small_one[x]
    for k in range(1, SIDE):
        total = total + m.small_x[k]
    m.small_two[...] = total
    sent_z = [copies.start(m.small_two, m.small_z.at[seq], peer) for peer in peers]
    m.small_z[seq] = total
    for part in (0, 2, 1, 3):
        cubes[part][1].second()
    for copy in sent_z:
        copy.wait_recv()
    m.g_small[...] = functools.reduce(lambda a, b: a + b, [m.small_z[s] for s in range(PEERS)])
    saves.append(save(m.g_small, result.g_small))
    for copy in sent_feed:
        copy.wait_recv()
    def spread(main, tail, target, output):
        for d in range(16):
            pieces = []
            for s in range(PEERS):
                line = m.feed_land[s]
                whole = jnp.concatenate([line[:, main : main + WIDE], line[:, tail : tail + 64]], axis=1)
                pieces.append(whole[:, OWN * d : OWN * d + OWN])
            target[:, 288 * d : 288 * d + 288] = jnp.concatenate(pieces, axis=1)
        saves.append(save(target, output))

    for part in (0, 2, 1, 3):
        cubes[part][1].finish()
        cubes[part][0].first()
    spread(0, 1024, m.w_gate, result.g_gate)
    for part in (0, 2, 1, 3):
        cubes[part][0].second()
    spread(WIDE, 1088, m.w_up, result.g_up)
    for part, (_, lanes, start, _) in enumerate(PARTS):
        cubes[part][0].finish(m.mix_wide.at[:, pl.ds(start, lanes.size)])
    theirs = pl.ds(pl.multiple_of((1 - core) * 8, 8), 8)
    mix_copy = copies.start(m.mix_wide.at[theirs], m.mix_land.at[core], partner)
    m.mix_land[core] = m.mix_wide[pl.ds(pl.multiple_of(core * 8, 8), 8), :]
    ring.finish(grad_hidden)
    m.mixer_in[...] = (m.hidden[...] + grad_hidden[...]).astype(BF)
    for q in range(2):
        saves.append(save(m.mixer_in.at[128 * q : 128 * q + 128], result.output.at[q]))
    mix_copy.wait_recv()
    for half in range(2):
        for k in range(3):
            m.w_in[:, 1024 * k + 512 * half : 1024 * k + 512 * half + 512] = m.mix_land[
                half, :, 512 * k + 512 : 512 * k + 1024
            ]
        m.w_out[:, 512 * half : 512 * half + 512] = m.mix_land[half, :, 0:512]
    saves.append(save(m.w_in, result.g_in))
    saves.append(save(m.w_out, result.g_out))
    for copy in saves:
        copy.wait()
    copies.drain()


def step(*operands):
    hbm, vmem = pl.BlockSpec(memory_space=pl.ANY), pl.BlockSpec(memory_space=pltpu.VMEM)
    return pl.pallas_call(
        step_kernel,
        out_shape=tuple(jax.ShapeDtypeStruct(*shape) for shape in RESULTS.values()),
        in_specs=[vmem if name in ("gains", "taps") else hbm for name in OPERANDS],
        out_specs=(hbm,) * len(RESULTS),
        scratch_shapes=[pltpu.VMEM(*shape) for shape in SCRATCH.values()]
        + [
            pltpu.SemaphoreType.REGULAR((2,)),
            pltpu.SemaphoreType.DMA((7,)),
            pltpu.SemaphoreType.DMA((10,)),
            pltpu.SemaphoreType.DMA((COPIES,)),
            pltpu.SemaphoreType.DMA((COPIES,)),
        ],
        compiler_params=pltpu.CompilerParams(
            collective_id=0, has_side_effects=True, vmem_limit_bytes=VMEM_BYTES
        ),
        name="step",
    )(*operands)


SHAPES = ((2, 8), (3, 8), (8, 3072), (8, 1024), (8, 4608), (8, 4608), (OWN, D))
RATES = ((rate_small, 0.0),) * 2 + ((rate_matrix, weight_decay),) * 5
TILED = 5


def adamw(weight, grad, first, second, rate, decay):
    first_new = beta_one * first + (1.0 - beta_one) * grad
    second_new = beta_two * second + (1.0 - beta_two) * grad * grad
    first_hat = first_new / (1.0 - beta_one**STEP)
    second_hat = second_new / (1.0 - beta_two**STEP)
    weight_new = weight - rate * (
        first_hat / (jnp.sqrt(second_hat) + epsilon_adam) + decay * weight
    )
    return (weight_new, first_new, second_new)


def adamw_kernel(*refs):
    weights, firsts, seconds, refs = refs[:7], refs[7:14], refs[14:21], refs[21:]
    small_grad, grads, finished, refs = refs[0], refs[1:6], refs[6:8], refs[8:]
    outs, final, refs = (refs[:7], refs[7:14], refs[14:21]), refs[21:23], refs[23:]
    held = [refs[5 * k : 5 * k + 5] for k in range(4)]
    through, (load_sem, save_sem) = refs[20:22], refs[22:]
    load, save = local_copies(load_sem), local_copies(save_sem)
    passing = [load(source, kept) for source, kept in zip(finished, through)]
    loads = []
    for index in range(TILED):
        sources = (grads[index], weights[index + 2], firsts[index + 2], seconds[index + 2])
        loads.append([load(source, kept[index]) for source, kept in zip(sources, held)])
    seq = lax.axis_index("seq")
    tile = pltpu.roll(small_grad[...], lax.rem(128 - seq * 8, 128), 1)
    for index, (start, count) in enumerate(((0, 2), (2, 3))):
        grad = tile[start : start + count, 0:8]
        new = adamw(weights[index][...], grad, firsts[index][...], seconds[index][...], *RATES[index])
        for out, value in zip(outs, new):
            out[index][...] = value
    saves = []
    for copy, kept, target in zip(passing, through, final):
        copy.wait()
        saves.append(save(kept, target))
    for index in range(TILED):
        for copy in loads[index]:
            copy.wait()
        grad, weight, first, second = (kept[index] for kept in held)
        rows, columns = weight.shape
        for start in range(0, columns, 512):
            lanes = slice(start, min(start + 512, columns))
            new = adamw(weight[:, lanes], grad[:, lanes], first[:, lanes], second[:, lanes], *RATES[index + 2])
            weight[:, lanes], first[:, lanes], second[:, lanes] = new
        for out, kept in zip(outs, (weight, first, second)):
            saves.append(save(kept, out[index + 2]))
    for copy in saves:
        copy.wait()


def adamw_all(weights, firsts, seconds, small_grad, grads, finished):
    hbm, vmem = pl.BlockSpec(memory_space=pl.ANY), pl.BlockSpec(memory_space=pltpu.VMEM)
    group = [vmem] * 2 + [hbm] * TILED
    return pl.pallas_call(
        adamw_kernel,
        out_shape=[jax.ShapeDtypeStruct(shape, F32) for shape in SHAPES] * 3
        + [jax.ShapeDtypeStruct(array.shape, array.dtype) for array in finished],
        in_specs=group * 3 + [vmem] + [hbm] * (TILED + 2),
        out_specs=group * 3 + [hbm] * 2,
        scratch_shapes=[pltpu.VMEM(shape, F32) for shape in SHAPES[2:]] * 4
        + [pltpu.VMEM(array.shape, array.dtype) for array in finished]
        + [pltpu.SemaphoreType.DMA((4 * TILED + 2,)), pltpu.SemaphoreType.DMA((3 * TILED + 2,))],
        compiler_params=pltpu.CompilerParams(vmem_limit_bytes=VMEM_BYTES),
        name="adamw",
    )(*weights, *firsts, *seconds, small_grad, *grads, *finished)


def shards(
    inputs, cotangent, norm_gains, conv_taps, w_in, w_out, w_gate, w_up, w_down,
    first_gains, first_taps, first_in, first_out, first_gate, first_up, first_down,
    second_gains, second_taps, second_in, second_out, second_gate, second_up, second_down,
):
    output, input_grad, red_in, red_out, red_gate, red_up, red_down, red_small = step(
        w_in, w_out, w_gate, w_up, w_down, norm_gains, conv_taps, inputs, cotangent.reshape(ROWS, D)
    )
    *new, output, input_grad = adamw_all(
        (norm_gains, conv_taps, w_in, w_out, w_gate, w_up, w_down),
        (first_gains, first_taps, first_in, first_out, first_gate, first_up, first_down),
        (second_gains, second_taps, second_in, second_out, second_gate, second_up, second_down),
        red_small,
        (red_in, red_out, red_gate, red_up, red_down),
        (output, input_grad),
    )
    return (output, input_grad, *new)


def solution(mesh):
    tokens, columns, rows = P("dp", "seq", None), P(None, ("dp", "seq")), P(("dp", "seq"), None)
    weights = (columns, columns, rows, rows, rows, rows, rows)
    return jax.shard_map(
        shards,
        mesh=mesh,
        in_specs=(tokens, tokens) + weights * 3,
        out_specs=(tokens, tokens) + weights * 3,
        check_vma=False,
    )
```

```python
import functools
import types

import jax
import jax.numpy as jnp
from jax import lax
from jax.experimental import pallas as pl
from jax.experimental.pallas import tpu as pltpu
from jax.sharding import PartitionSpec as P

D = 1024
STEP = 5

epsilon_norm = 1e-05
beta_one = 0.9
beta_two = 0.95
epsilon_adam = 1e-08
rate_matrix = 0.02
rate_small = 0.3
weight_decay = 0.1

MESH = pl.DeviceIdType.MESH
BF = jnp.bfloat16
F32 = jnp.float32
SIDE = 4
PEERS = 8
OWN = 36
PACKED = 2304
SLICE = 576
WIDE = 512
VMEM_BYTES = 62 * 2**20


def place():
    dp, seq = lax.axis_index("dp"), lax.axis_index("seq")
    return lax.rem(dp, SIDE), lax.div(dp, SIDE), lax.div(seq, 2), lax.rem(seq, 2)


def wrap(value, size=SIDE):
    return lax.rem(value + size, size)


def at(x, y, z, core):
    return (y * SIDE + x, z * 2 + core)


class Copies:
    def __init__(self, send, recv):
        self.send, self.recv, self.started, self.sent = send, recv, [], set()

    def plan(self, source, target, device):
        index = len(self.started)
        assert index < self.send.shape[0]
        copy = pltpu.make_async_remote_copy(
            src_ref=source,
            dst_ref=target,
            send_sem=self.send.at[index],
            recv_sem=self.recv.at[index],
            device_id=device,
            device_id_type=MESH,
        )
        self.started.append(copy)
        return copy

    def start(self, source, target, device):
        copy = self.plan(source, target, device)
        copy.start()
        return copy

    def drain(self, some=None):
        for copy in self.started if some is None else some:
            if id(copy) not in self.sent:
                self.sent.add(id(copy))
                copy.wait_send()


def seq_peers(x, y, z, core):
    seq = z * 2 + core
    return [(y * SIDE + x, wrap(seq + k, PEERS)) for k in range(1, PEERS)]


def halver(dim, low):
    def split(ref, part):
        size = ref.shape[dim]
        places = [slice(None)] * len(ref.shape)
        places[dim] = pl.ds(0, low) if part == 0 else pl.ds(low, size - low)
        return ref.at[tuple(places)]

    return split


class RingGather:
    def __init__(self, copies, me, to, block, split, fine=True):
        self.copies, self.me, self.to, self.block, self.split, self.fine = copies, me, to, block, split, fine

    def plan(self, source=None):
        source = self.block(self.me) if source is None else source
        below, above = wrap(self.me - 1), wrap(self.me + 1)

        def move(start, target, part, place):
            return self.copies.plan(self.split(start, part), self.split(target, part), self.to(place))

        mine, before, after = self.block(self.me), self.block(below), self.block(above)
        if self.fine:
            self.up = [move(source, mine, part, above) for part in range(2)]
            self.down = [move(source, mine, part, below) for part in range(2)]
        else:
            self.up = [self.copies.plan(source, mine, self.to(above))]
            self.down = [self.copies.plan(source, mine, self.to(below))]
        self.pass_up = move(before, before, 0, above)
        self.pass_down = move(after, after, 1, below)

    def first(self, source=None):
        if not hasattr(self, "up"):
            self.plan(source)
        self.up[0].start()
        self.down[-1].start()
        if self.fine:
            self.up[1].start()
            self.down[0].start()

    def second(self):
        self.up[0].wait_recv()
        self.pass_up.start()
        self.down[-1].wait_recv()
        self.pass_down.start()

    def wait_below(self):
        if self.fine:
            self.up[1].wait_recv()

    def wait_above(self):
        if self.fine:
            self.down[0].wait_recv()

    def wait_far(self):
        self.pass_up.wait_recv()
        self.pass_down.wait_recv()

    def finish(self):
        self.wait_below()
        self.wait_above()
        self.wait_far()

    def copies_made(self):
        return [*self.up, *self.down, self.pass_up, self.pass_down]


class RingReduce:
    def __init__(self, copies, me, to, block, split, landing, fine=True):
        self.copies, self.me, self.to, self.block, self.split, self.fine = copies, me, to, block, split, fine
        self.low_in, self.high_in, self.plus_in, self.minus_in = landing

    def plan(self):
        far, below, above = wrap(self.me + 2), wrap(self.me - 1), wrap(self.me + 1)
        plan, split = self.copies.plan, self.split
        self.far_up = plan(split(self.block(far), 0), self.low_in, self.to(above))
        self.far_down = plan(split(self.block(far), 1), self.high_in, self.to(below))
        if self.fine:
            self.up = [plan(split(self.block(above), k), split(self.plus_in, k), self.to(above)) for k in range(2)]
            self.down = [plan(split(self.block(below), k), split(self.minus_in, k), self.to(below)) for k in range(2)]
        else:
            self.up = [plan(self.block(above), self.plus_in, self.to(above))]
            self.down = [plan(self.block(below), self.minus_in, self.to(below))]

    def first_far(self):
        self.far_up.start()
        self.far_down.start()

    def first_above(self):
        self.up[1].start()

    def first_below(self):
        self.down[0].start()

    def first(self):
        if not hasattr(self, "up"):
            self.plan()
        self.first_far()
        if self.fine:
            self.first_above()
            self.first_below()

    def second(self):
        below, above = self.block(wrap(self.me - 1)), self.block(wrap(self.me + 1))
        self.far_up.wait_recv()
        accumulate(self.split(above, 0), self.split(above, 0), self.low_in)
        self.up[0].start()
        self.far_down.wait_recv()
        accumulate(self.split(below, 1), self.split(below, 1), self.high_in)
        self.down[-1].start()

    def copies_made(self):
        return [self.far_up, self.far_down, *self.up, *self.down]

    def finish(self, target=None):
        own = self.block(self.me)
        for copy in (*self.up, *self.down):
            copy.wait_recv()
        accumulate(own if target is None else target, own, self.plus_in, self.minus_in)


def accumulate(target, *sources):
    shape = target.shape
    if len(shape) > 2:
        for index in range(shape[0]):
            accumulate(target.at[index], *[source.at[index] for source in sources])
        return
    step = 16

    @pl.loop(0, shape[0] // step)
    def _(i):
        rows = pl.ds(pl.multiple_of(i * step, step), step)
        total = sources[0][rows, :].astype(F32)
        for source in sources[1:]:
            total = total + source[rows, :].astype(F32)
        target[rows, :] = total.astype(target.dtype)


def columns_of(seq, dp_count=16):
    return [(288 * d + OWN * seq, 36 * d) for d in range(dp_count)]


def dot(a, b, dims=((1,), (0,))):
    return lax.dot_general(a, b, (dims, ((), ())), preferred_element_type=F32)


NT = ((1,), (1,))
TN = ((0,), (0,))
ROWS = 256
PAIR = 512
EVERY = 272
HALF = 512


def by_rows(ref, which, part):
    start, size = (32 * which, 32) if part is None else (32 * which + 16 * part, 16)
    lead = [slice(None)] * (len(ref.shape) - 2)
    return ref.at[(*lead, pl.ds(start, size), slice(None))]


def rows_of(lanes):
    def halves(ref, which, part):
        rows = by_rows(ref, which, part)
        return rows.at[(*[slice(None)] * (len(rows.shape) - 1), lanes)]

    return halves


def by_columns(ref, which, part):
    first, size = ((0, 1152), (0, 640), (640, 512))[0 if part is None else part + 1]
    lead = [slice(None)] * (len(ref.shape) - 2)
    return ref.at[(*lead, slice(None), pl.ds(1152 * which + first, size))]


def visit(z, k):
    return wrap(z + k + lax.div(k, 2) * (5 - 2 * k))


def turn_of(z, chip):
    ahead = wrap(chip - z)
    return ahead + lax.div(ahead, 2) * (5 - 2 * ahead)


class PlaneGather:
    def __init__(self, copies, spot, view, halves, block, split, fine=True):
        x, y, z, core = spot
        to_x, to_y = (lambda i: at(i, y, z, core)), (lambda i: at(x, i, z, core))
        everything, fours = slice(None), halver(0, 2)
        self.x, self.y, self.view, self.halves = x, y, view, halves
        self.row_x = RingGather(copies, x, to_x, lambda i: halves(view(y, i), 0, None), split, False)
        self.row_y = RingGather(copies, y, to_y, lambda i: halves(view(i, x), 1, None), split, False)
        self.all_y = RingGather(copies, y, to_y, lambda i: halves(view(i, everything), 0, None), fours, fine)
        self.all_x = RingGather(copies, x, to_x, lambda i: halves(view(everything, i), 1, None), fours, fine)
        self.row_x.plan(halves(block, 0, None))
        self.row_y.plan(halves(block, 1, None))
        self.all_y.plan()
        self.all_x.plan()

    def one(self):
        self.row_x.first()
        self.row_y.first()

    def two(self):
        self.row_x.second()
        self.row_y.second()

    def three(self):
        self.row_x.finish()
        self.all_y.first()
        self.row_y.finish()
        self.all_x.first()

    def four(self):
        self.all_y.second()
        self.all_x.second()

    def finish(self):
        self.all_y.finish()
        self.all_x.finish()

    def wait_near(self, then):
        self.all_y.wait_below()
        self.all_x.wait_below()
        then(self, -1)
        self.all_y.wait_above()
        self.all_x.wait_above()
        then(self, 1)

    def copies(self):
        return [copy for ring in (self.row_x, self.row_y, self.all_y, self.all_x) for copy in ring.copies_made()]

    def group(self, which, step):
        everything = slice(None)
        if which == 0:
            return self.halves(self.view(wrap(self.y + step), everything), 0, None)
        return self.halves(self.view(everything, wrap(self.x + step)), 1, None)


PARTS = (
    (0, pl.ds(0, 512), 0, ("y", "z", "x")),
    (0, pl.ds(512, 512), 512, ("x", "y", "z")),
    (1, pl.ds(0, 512), 1024, ("z", "x", "y")),
    (1, pl.ds(512, 512), 1536, ("y", "z", "x")),
)


def first_half(width):
    return (width + 255) // 256 * 128


def cube_spots(spot, order):
    x, y, z, core = spot
    own = {"x": x, "y": y, "z": z}
    to = {
        "x": lambda i: at(i, y, z, core),
        "y": lambda i: at(x, i, z, core),
        "z": lambda i: at(x, y, i, core),
    }

    def view(ref, **places):
        return ref.at[tuple(places.get(axis, own[axis]) for axis in ("y", "x", "z"))]

    return [own[axis] for axis in order], [to[axis] for axis in order], view


def cube_rings(spot, order, ref, make):
    (a, b, c), (to_a, to_b, to_c), view = cube_spots(spot, order)
    one, two, three = order
    everything = slice(None)
    place_of = {"y": 0, "x": 1, "z": 2}
    first = make(a, to_a, lambda i: view(ref, **{one: i}), halver(-1, first_half(ref.shape[-1])), False)
    second = make(b, to_b, lambda i: view(ref, **{one: everything, two: i}), halver(0, 2), False)
    third = make(
        c, to_c,
        lambda i: view(ref, **{one: everything, two: everything, three: i}),
        halver(0 if place_of[two] < place_of[one] else 1, 2),
        True,
    )
    return first, second, third


def small_rows(small_all):
    pieces = [small_all[d // 4, d % 4][:, :64] for d in range(16)]
    return jnp.concatenate(pieces, axis=1)


def normalize(rows, gain):
    inverse = lax.rsqrt(jnp.mean(rows * rows, axis=-1, keepdims=True) + epsilon_norm)
    return rows * inverse * gain


def extend(extended, projected, half, sequence):
    first = pl.ds(ROWS + 8 * sequence, 8)
    main = pl.ds(128 * sequence, 128)
    extended[0:8, :] = projected[half, first, :HALF] * projected[half, first, 1024:]
    extended[8:136, :] = projected[half, main, :HALF] * projected[half, main, 1024:]


def convolve(extended, taps):
    return taps[0:1] * extended[6:134, :] + taps[1:2] * extended[7:135, :] + taps[2:3] * extended[8:136, :]


def half_lanes(half):
    return pl.ds(pl.multiple_of(half * HALF, HALF), HALF)


class PlaneReduce:
    def __init__(self, copies, spot, view, halves, split, landings):
        x, y, z, core = spot
        to_x, to_y = (lambda i: at(i, y, z, core)), (lambda i: at(x, i, z, core))
        everything, fours = slice(None), halver(0, 2)
        self.halves = halves
        self.all_y = RingReduce(copies, y, to_y, lambda i: halves(view(i, everything), 0, None), fours, landings[0:4])
        self.all_x = RingReduce(copies, x, to_x, lambda i: halves(view(everything, i), 1, None), fours, landings[4:8])
        self.row_x = RingReduce(copies, x, to_x, lambda i: halves(view(y, i), 0, None), split, landings[8:12], False)
        self.row_y = RingReduce(copies, y, to_y, lambda i: halves(view(i, x), 1, None), split, landings[12:16], False)

    def one(self):
        self.all_y.first()
        self.all_x.first()

    def two(self):
        self.all_y.second()
        self.all_x.second()

    def three(self):
        self.all_y.finish()
        self.row_x.first()
        self.all_x.finish()
        self.row_y.first()

    def four(self):
        self.row_x.second()
        self.row_y.second()

    def finish(self, target):
        self.row_x.finish(self.halves(target, 0, None))
        self.row_y.finish(self.halves(target, 1, None))


def plane_landings(ref):
    wide = lambda count, blocks, rows: ref.reshape(count, blocks, rows, 1152)
    single = lambda rows: ref.reshape(2048 // rows, rows, 1152)
    fed, downs = [], []
    for k in range(2):
        fed += [wide(32, 2, 32).at[8 + 2 * k], wide(32, 2, 32).at[9 + 2 * k]]
        fed += [wide(16, 4, 32).at[2 * k], wide(16, 4, 32).at[2 * k + 1]]
        downs += [wide(64, 2, 16).at[38 + 2 * k], wide(64, 2, 16).at[39 + 2 * k]]
        downs += [wide(32, 4, 16).at[15 + 2 * k], wide(32, 4, 16).at[16 + 2 * k]]
    for k in range(2):
        fed += [single(16).at[56 + 2 * k], single(16).at[57 + 2 * k], single(32).at[24 + 2 * k], single(32).at[25 + 2 * k]]
        downs += [single(16).at[88 + 2 * k, :, pl.ds(0, 640)], single(16).at[89 + 2 * k, :, pl.ds(0, 512)]]
        downs += [single(16).at[84 + 2 * k], single(16).at[85 + 2 * k]]
    return fed, downs


def cube_landings(ref, lanes, order):
    width, total = lanes.size, ref.shape[-1]
    place_of = {"y": 0, "x": 1, "z": 2}
    halved = (2, 4) if place_of[order[1]] < place_of[order[0]] else (4, 2)

    def take(count, lead, index, part=None):
        window = lanes
        if part is not None:
            low = first_half(width)
            window = pl.ds(lanes.start, low) if part == 0 else pl.ds(lanes.start, width - low)
        places = (slice(None),) * (len(lead) + 1)
        return ref.reshape(count, *lead, 16, total).at[(index, *places, window)]

    first = [take(64, (), 60, 0), take(64, (), 61, 1), take(64, (), 62), take(64, (), 63)]
    second = [take(32, (2,), 24), take(32, (2,), 25), take(16, (4,), 13), take(16, (4,), 14)]
    third = [take(8, halved, 4), take(8, halved, 5), take(4, (4, 4), 0), take(4, (4, 4), 1)]
    return first, second, third


def local_copies(semaphores):
    count = iter(range(semaphores.shape[0]))

    def start(source, target):
        copy = pltpu.make_async_copy(source, target, semaphores.at[next(count)])
        copy.start()
        return copy

    return start


OPERANDS = ("w_in", "w_out", "w_gate", "w_up", "w_down", "gains", "taps", "inputs", "cotangent")
RESULTS = {
    "output": ((2, 128, D), BF),
    "input_grad": ((2, 128, D), F32),
    "g_in": ((8, 3072), F32),
    "g_out": ((8, 1024), F32),
    "g_gate": ((8, 4608), F32),
    "g_up": ((8, 4608), F32),
    "g_down": ((OWN, D), F32),
    "g_small": ((8, 128), F32),
}
SCRATCH = {
    "w_in": ((8, 3072), F32),
    "w_out": ((8, 1024), F32),
    "w_gate": ((8, 4608), F32),
    "w_up": ((8, 4608), F32),
    "w_down": ((OWN, D), F32),
    "tile": ((8, 128), F32),
    "inputs": ((2, 128, D), BF),
    "mix": ((2, 4, 4, 64, 2048), BF),
    "feed": ((4, 4, 64, 2 * SLICE), BF),
    "down": ((4, 4, 16, PACKED), BF),
    "small_all": ((4, 4, 8, 128), F32),
    "edge_in": ((2, 16, D), BF),
    "tokens": ((SIDE, 2, ROWS, D), BF),
    "grads": ((SIDE, 2, ROWS, D), BF),
    "mix_send": ((2, 16, D), BF),
    "feed_send": ((PEERS, 16, 640), BF),
    "mix_got": ((PEERS, 16, D), BF),
    "feed_got": ((PEERS, 16, 640), BF),
    "small_got": ((PEERS, 8, 128), F32),
    "mix_block": ((64, 2048), BF),
    "feed_block": ((64, 2 * SLICE), BF),
    "down_block": ((16, PACKED), BF),
    "small_send": ((8, 128), F32),
    "rows": ((8, D), F32),
    "normed": ((EVERY, D), BF),
    "projected": ((2, EVERY, 1536), F32),
    "extended": ((136, HALF), F32),
    "mixer_in": ((ROWS, D), BF),
    "hidden": ((ROWS, D), F32),
    "normed_two": ((ROWS, D), BF),
    "down_rows": ((SLICE, D), BF),
    "narrow_wide": ((160, D), F32),
    "value": ((PAIR, 2 * SLICE), F32),
    "grad_active": ((PAIR, SLICE), F32),
    "active": ((2048, SLICE), BF),
    "grad_value": ((2048, 2 * SLICE), BF),
    "part": ((SIDE, 2, ROWS, D), BF),
    "part_out": ((SIDE, 2, ROWS, D), BF),
    "landing": ((SIDE, ROWS, D), BF),
    "landing_left": ((SIDE, ROWS, HALF), BF),
    "landing_right": ((SIDE, ROWS, HALF), BF),
    "low_in": ((128, D), BF),
    "high_in": ((128, D), BF),
    "plus_in": ((ROWS, D), BF),
    "minus_in": ((ROWS, D), BF),
    "low_out": ((128, D), BF),
    "high_out": ((128, D), BF),
    "plus_out": ((ROWS, D), BF),
    "minus_out": ((ROWS, D), BF),
    "down_part": ((SLICE, 256), F32),
    "down_tail": ((16, 16, 256), F32),
    "grad_conv": ((2, 136, D), F32),
    "grad_x": ((2, ROWS, HALF), BF),
    "edge_send": ((2, 8, D), F32),
    "edge_got": ((2, 8, D), F32),
    "sums": ((8, D), F32),
    "mix_wide": ((16, 2048), F32),
    "feed_wide": ((64, 2 * SLICE), F32),
    "down_wide": ((16, PACKED), F32),
    "mix_land": ((2, 8, 2048), F32),
    "feed_land": ((PEERS, 8, 2 * SLICE), F32),
    "small": ((4, 4, 8, 128), F32),
    "small_y": ((4, 4, 8, 128), F32),
    "small_x": ((4, 8, 128), F32),
    "small_z": ((PEERS, 8, 128), F32),
    "small_one": ((4, 8, 128), F32),
    "small_two": ((8, 128), F32),
    "g_small": ((8, 128), F32),
}
COPIES = 448


def step_kernel(*refs):
    count = len(OPERANDS)
    given = types.SimpleNamespace(**dict(zip(OPERANDS, refs)))
    result = types.SimpleNamespace(**dict(zip(RESULTS, refs[count:])))
    count += len(RESULTS)
    m = types.SimpleNamespace(**dict(zip(SCRATCH, refs[count:])))
    ready, load_sem, save_sem, send, recv = refs[count + len(SCRATCH) :]

    spot = x, y, z, core = place()
    seq = z * 2 + core
    copies = Copies(send, recv)
    peers = seq_peers(x, y, z, core)
    across = [at(wrap(x + k), y, z, core) for k in range(1, SIDE)]
    along = [at(x, wrap(y + k), z, core) for k in range(1, SIDE)]
    partner = at(x, y, z, 1 - core)
    load = local_copies(load_sem)
    loads = {
        "w_in": load(given.w_in, m.w_in),
        "w_out": load(given.w_out, m.w_out),
        "w_gate": load(given.w_gate, m.w_gate),
        "w_up": load(given.w_up, m.w_up),
        "w_down": load(given.w_down, m.w_down),
        "inputs": load(given.inputs, m.inputs),
        "cotangent": load(given.cotangent, m.grads.at[z, core]),
    }
    barrier = pltpu.get_barrier_semaphore()
    for device in peers + across + along:
        pl.semaphore_signal(barrier, inc=1, device_id=device, device_id_type=MESH)

    def to_z(i):
        return at(x, y, i, core)

    loads["w_in"].wait()
    loads["w_out"].wait()
    for half in range(2):
        parts = [m.w_out[:, 512 * half : 512 * half + 512]]
        parts += [m.w_in[:, 1024 * k + 512 * half : 1024 * k + 512 * half + 512] for k in range(3)]
        upper = jnp.concatenate(parts[:2], axis=1)
        lower = jnp.concatenate(parts[2:], axis=1)
        m.mix_send[half] = jnp.concatenate([upper, lower], axis=0).astype(BF)
    pl.semaphore_wait(barrier, len(peers + across + along))
    mix_copies = []
    for k, peer in enumerate(peers):
        other = wrap(seq + k + 1, PEERS)
        mix_copies.append(copies.start(m.mix_send.at[lax.rem(other, 2)], m.mix_got.at[seq], peer))
    m.mix_got[seq] = m.mix_send[core]
    mixed, mixed_out = (
        PlaneGather(copies, spot, lambda i, j: m.mix.at[core, i, j], rows_of(lanes), m.mix_block, halver(-2, 16))
        for lanes in (pl.ds(HALF, 1536), pl.ds(0, HALF))
    )
    fed = PlaneGather(copies, spot, lambda i, j: m.feed.at[i, j], by_rows, m.feed_block, halver(-2, 16))
    downs = PlaneGather(copies, spot, lambda i, j: m.down.at[i, j], by_columns, m.down_block, halver(-1, 640), False)
    loads["w_down"].wait()
    for i in range(4):
        m.narrow_wide[4 * i : 4 * i + 4, 0:256] = m.w_down[32:36, 256 * i : 256 * i + 256]
    m.down_block[:, 0:1024] = m.w_down[0:16, :].astype(BF)
    m.down_block[:, 1024:2048] = m.w_down[16:32, :].astype(BF)
    m.down_block[:, 2048:PACKED] = m.narrow_wide[0:16, 0:256].astype(BF)
    m.down[y, x] = m.down_block[...]
    downs.one()
    m.tile[...] = jnp.zeros_like(m.tile)
    m.tile[0:2, 0:8] = given.gains[...].astype(BF).astype(F32)
    m.tile[2:5, 0:8] = given.taps[...].astype(BF).astype(F32)
    m.small_got[seq] = pltpu.roll(m.tile[...], seq * 8, 1)
    small_copies = [copies.start(m.small_got.at[seq], m.small_got.at[seq], peer) for peer in peers]
    edge_copy = copies.start(
        given.inputs.at[:, pl.ds(112, 16)], m.edge_in, (y * SIDE + x, wrap(seq + 1, PEERS))
    )
    ring = RingGather(
        copies, z, to_z,
        lambda i: m.grads.at[i, core],
        halver(0, 128),
    )
    ring.plan(given.cotangent)

    def slices(which):
        for s in which:
            gate = jnp.concatenate([m.w_gate[:, a : a + OWN] for a, _ in columns_of(s)], axis=1)
            up = jnp.concatenate([m.w_up[:, a : a + OWN] for a, _ in columns_of(s)], axis=1)
            tail = jnp.concatenate([gate[:, WIDE:], up[:, WIDE:]], axis=1)
            upper = jnp.concatenate([gate[:, :WIDE], up[:, :128]], axis=1)
            lower = jnp.concatenate([up[:, 128:WIDE], tail, jnp.zeros((8, 128), F32)], axis=1)
            m.feed_send[s] = jnp.concatenate([upper, lower], axis=0).astype(BF)

    loads["w_gate"].wait()
    loads["w_up"].wait()
    slices(range(PEERS))
    feed_copies = []
    for k, peer in enumerate(peers):
        other = wrap(seq + k + 1, PEERS)
        feed_copies.append(copies.start(m.feed_send.at[other], m.feed_got.at[seq], peer))
    m.feed_got[seq] = m.feed_send[seq]
    downs.two()
    for copy in mix_copies:
        copy.wait_recv()
    for k in range(4):
        a, b = m.mix_got[2 * k].astype(F32), m.mix_got[2 * k + 1].astype(F32)
        line = slice(16 * k, 16 * k + 16)
        m.mix_block[line, :1024] = jnp.concatenate([a[:8], b[:8]], axis=0).astype(BF)
        m.mix_block[line, 1024:] = jnp.concatenate([a[8:], b[8:]], axis=0).astype(BF)
    mixed.one()
    mixed_out.one()
    downs.three()
    m.mix[core, y, x] = m.mix_block[...]
    mixed.two()
    mixed_out.two()

    for copy in feed_copies:
        copy.wait_recv()
    for k in range(4):
        a, b = m.feed_got[2 * k].astype(F32), m.feed_got[2 * k + 1].astype(F32)
        line = slice(16 * k, 16 * k + 16)
        m.feed_block[line, :640] = jnp.concatenate([a[:8], b[:8]], axis=0).astype(BF)
        m.feed_block[line, 640:] = jnp.concatenate([a[8:, :512], b[8:, :512]], axis=0).astype(BF)
    m.feed[y, x] = m.feed_block[...]
    fed.one()
    ring.first()
    cotangent_ring = ring
    grads_passed = [copies.start(given.cotangent, m.grads.at[z, core], partner)]
    mixed.three()
    mix_passed = []

    def pass_on(gather, step):
        for which in range(2):
            part = gather.group(which, step)
            mix_passed.append(copies.start(part, part, partner))

    pass_on(mixed, 0)
    for copy in small_copies:
        copy.wait_recv()
    m.small_send[...] = functools.reduce(lambda a, b: a + b, [m.small_got[s] for s in range(PEERS)])
    small_x = [copies.start(m.small_send, m.small_all.at[y, x], device) for device in across]
    m.small_all[y, x] = m.small_send[...]
    fed.two()
    downs.four()
    for copy in small_x:
        copy.wait_recv()
    small_y = [copies.start(m.small_all.at[y], m.small_all.at[y], device) for device in along]
    for copy in small_y:
        copy.wait_recv()
    m.rows[...] = small_rows(m.small_all)
    loads["inputs"].wait()
    for q in range(2):
        m.normed[128 * q : 128 * q + 128, :] = normalize(m.inputs[q].astype(F32), m.rows[0:1, :]).astype(BF)
    edge_copy.wait_recv()
    inside = (seq > 0).astype(F32)
    earlier = [normalize(m.edge_in[q].astype(F32)[8:], m.rows[0:1, :]) * inside for q in range(2)]
    m.normed[ROWS:EVERY, :] = jnp.concatenate(earlier, axis=0).astype(BF)
    ring.second()
    mixed.four()
    mixed_out.three()
    mixed.wait_near(pass_on)
    mixed.all_y.wait_far()
    mixed.all_x.wait_far()
    pass_on(mixed, 2)
    mixed_out.four()
    fed.three()
    for turn in range(2):
        if turn == 1:
            for copy in mix_passed[:8]:
                copy.wait_recv()
        half = core if turn == 0 else 1 - core
        m.projected[half] = dot(m.normed[...], m.mix.at[half].reshape(D, 2048)[:, HALF:])
        lanes = half_lanes(half)
        for q in range(2):
            main = slice(128 * q, 128 * q + 128)
            extend(m.extended, m.projected, half, q)
            convolved = convolve(m.extended, m.rows[2:5, lanes])
            m.mixer_in[main, lanes] = (m.projected[half, main, HALF:1024] * convolved).astype(BF)
    pass_on(mixed_out, 0)
    mixed_out.wait_near(pass_on)
    mixed_out.all_y.wait_far()
    mixed_out.all_x.wait_far()
    pass_on(mixed_out, 2)
    for copy in mix_passed[8:]:
        copy.wait_recv()
    weights = [m.mix.at[half].reshape(D, 2048) for half in range(2)]
    for half in range(2):
        lanes = slice(HALF * half, HALF * half + HALF)
        mixed_out = dot(m.mixer_in[...], weights[half][:, :HALF])
        for q in range(2):
            main = slice(128 * q, 128 * q + 128)
            m.hidden[main, lanes] = m.inputs[q, :, lanes].astype(F32) + mixed_out[main]
    m.normed_two[...] = normalize(m.hidden[...], m.rows[1:2, :]).astype(BF)

    around = RingGather(
        copies, z, to_z,
        lambda i: m.tokens.at[i, core],
        halver(0, 128),
    )
    around.plan(m.normed_two)
    passed = [copies.plan(m.normed_two, m.tokens.at[z, core], partner)]
    for step in (1, 3, 2):
        chunk = m.tokens.at[wrap(z + step), core]
        passed.append(copies.plan(chunk, chunk, partner))
    around.first()
    passed[0].start()
    m.tokens[z, core] = m.normed_two[...]
    fed.four()
    ring.finish()
    for step in (1, 3, 2):
        chunk = m.grads.at[wrap(z + step), core]
        grads_passed.append(copies.start(chunk, chunk, partner))
    gives, gives_left, gives_right = [], [], []
    for k in range(SIDE):
        theirs = m.part_out.at[k, 1 - core]
        gives.append(copies.plan(m.part.at[k, 1 - core], m.landing.at[k], partner))
        gives_left.append(copies.plan(theirs.at[:, 0:HALF], m.landing_left.at[k], partner))
        gives_right.append(copies.plan(theirs.at[:, HALF:D], m.landing_right.at[k], partner))
    reduce = RingReduce(
        copies, z, to_z,
        lambda i: m.part.at[turn_of(z, i), core],
        halver(0, 128),
        (m.low_in, m.high_in, m.plus_in, m.minus_in),
    )
    reduce.plan()
    downs.finish()
    for i in range(SIDE):
        for d in range(SIDE):
            packed = m.down[i, d].astype(F32)
            m.narrow_wide[OWN * d : OWN * d + 16, :] = packed[:, 0:1024]
            m.narrow_wide[OWN * d + 16 : OWN * d + 32, :] = packed[:, 1024:2048]
            for k in range(4):
                m.narrow_wide[OWN * d + 32 : OWN * d + 36, 256 * k : 256 * k + 256] = packed[4 * k : 4 * k + 4, 2048:]
        m.down_rows[144 * i : 144 * i + 144, :] = m.narrow_wide[0:144, :].astype(BF)
    for copy in grads_passed:
        copy.wait_recv()
    loads["cotangent"].wait()
    fed.finish()
    feed = m.feed.reshape(D, 2 * SLICE)

    def settle(step):
        gives[step].wait_recv()
        accumulate(m.part.at[step, core], m.part.at[step, core], m.landing.at[step])
        if step == 1:
            reduce.first_above()
        if step == 2:
            reduce.first_below()
        if step == 3:
            reduce.first_far()

    def output_part(step):
        lines = pl.ds(pl.multiple_of(visit(z, step) * PAIR, PAIR), PAIR)
        m.part_out.at[step].reshape(PAIR, D)[...] = dot(m.active[lines, :], m.down_rows[...]).astype(BF)
        gives_left[step].start()
        gives_right[step].start()

    @pl.loop(0, SIDE)
    def _(k):
        @pl.when(k == 0)
        def _():
            passed[0].wait_recv()

        @pl.when(k == 1)
        def _():
            around.second()
            around.wait_above()
            passed[1].start()
            around.wait_below()
            passed[2].start()
            passed[1].wait_recv()

        @pl.when(k == 2)
        def _():
            passed[2].wait_recv()
            around.wait_far()
            passed[3].start()

        @pl.when(k == 3)
        def _():
            passed[3].wait_recv()

        chip = visit(z, k)
        m.value[...] = dot(m.tokens.at[chip].reshape(PAIR, D)[...], feed[...])
        m.grad_active[...] = dot(m.grads.at[chip].reshape(PAIR, D)[...], m.down_rows[...], NT)
        for step in range(SIDE - 1):
            @pl.when(k == step + 1)
            def _(step=step):
                settle(step)

        base = chip * PAIR

        @pl.loop(0, PAIR // 64)
        def _(r):
            line = pl.ds(pl.multiple_of(r * 64, 64), 64)
            target = pl.ds(pl.multiple_of(base + r * 64, 64), 64)
            tail = m.value[line, 1024:1152]
            ends = []
            for gate, up, back, where in (
                (m.value[line, :WIDE], m.value[line, WIDE:1024], m.grad_active[line, :WIDE], slice(0, WIDE)),
                (tail[:, :64], tail[:, 64:], m.grad_active[line, WIDE:], slice(WIDE, SLICE)),
            ):
                sigmoid = jax.nn.sigmoid(gate)
                soft = gate * sigmoid
                m.active[target, where] = (soft * up).astype(BF)
                grad_up = (back * soft).astype(BF)
                grad_gate = (back * up * (sigmoid * (1.0 + gate * (1.0 - sigmoid)))).astype(BF)
                ends.append((grad_gate, grad_up))
            m.grad_value[target, :WIDE] = ends[0][0]
            m.grad_value[target, WIDE:1024] = ends[0][1]
            m.grad_value[target, 1024:1088] = ends[1][0]
            m.grad_value[target, 1088:1152] = ends[1][1]

        lines = pl.ds(pl.multiple_of(base, PAIR), PAIR)
        m.part.at[k].reshape(PAIR, D)[...] = dot(m.grad_value[lines, :], feed[...], NT).astype(BF)
        for step in range(SIDE):
            @pl.when(k == step)
            def _(step=step):
                gives[step].start()

    output_part(0)
    output_part(1)
    settle(3)
    copies.drain(fed.copies())
    copies.drain(downs.copies())
    every_grad, every_token = m.grads.reshape(2048, D), m.tokens.reshape(2048, D)

    @pl.loop(0, 4)
    def _(n):
        columns = pl.ds(pl.multiple_of(n * 256, 256), 256)
        feed[columns, :] = dot(every_token[:, columns], m.grad_value[...], TN).astype(BF)

    plane_neighbours = [at(wrap(x + 1), y, z, core), at(wrap(x - 1), y, z, core)]
    plane_neighbours += [at(x, wrap(y + 1), z, core), at(x, wrap(y - 1), z, core)]
    for device in plane_neighbours:
        pl.semaphore_signal(ready.at[0], inc=1, device_id=device, device_id_type=MESH)
    reduce.second()

    def down_columns(n):
        columns = slice(256 * n, 256 * n + 256)
        m.down_part[...] = dot(m.active[...], every_grad[:, columns], TN)
        for d in range(16):
            block = m.down.at[d // 4, d % 4]
            block[:, columns] = m.down_part[OWN * d : OWN * d + 16, :].astype(BF)
            block[:, 1024 + 256 * n : 1280 + 256 * n] = m.down_part[OWN * d + 16 : OWN * d + 32, :].astype(BF)
            m.down_tail[d, 4 * n : 4 * n + 4, :] = m.down_part[OWN * d + 32 : OWN * d + 36, :]

    fed_landings, down_landings = plane_landings(m.grad_value)
    fed = PlaneReduce(copies, spot, lambda i, j: m.feed.at[i, j], by_rows, halver(-2, 16), fed_landings)
    downs = PlaneReduce(copies, spot, lambda i, j: m.down.at[i, j], by_columns, halver(-1, 640), down_landings)
    down_columns(0)
    pl.semaphore_wait(ready.at[0], len(plane_neighbours))
    fed.one()
    output_part(2)
    output_part(3)
    for n in range(1, 4):
        down_columns(n)
    for d in range(16):
        m.down[d // 4, d % 4, :, 2048:PACKED] = m.down_tail[d].astype(BF)
    downs.one()
    for k in range(SIDE):
        gives_left[k].wait_recv()
        gives_right[k].wait_recv()
        ours = m.part_out.at[k, core]
        accumulate(ours.at[:, 0:HALF], ours.at[:, 0:HALF], m.landing_left.at[k])
        accumulate(ours.at[:, HALF:D], ours.at[:, HALF:D], m.landing_right.at[k])
    ring = RingReduce(
        copies, z, to_z,
        lambda i: m.part_out.at[turn_of(z, i), core],
        halver(0, 128),
        (m.low_out, m.high_out, m.plus_out, m.minus_out),
    )
    ring.first()
    grad_hidden = m.value.at[0:ROWS, 0:D]
    grad_mixer = m.value.at[ROWS : 2 * ROWS, 0:D]
    reduce.finish(grad_hidden)

    copies.drain(gives + gives_left + gives_right + reduce.copies_made() + around.copies_made() + passed)
    copies.drain(grads_passed)
    copies.drain(cotangent_ring.copies_made())
    neighbours = plane_neighbours + [at(x, y, wrap(z + 1), core), at(x, y, wrap(z - 1), core), partner]
    for device in neighbours:
        pl.semaphore_signal(ready.at[1], inc=1, device_id=device, device_id_type=MESH)

    sum_blocks = m.grads.reshape(2, 4, 4, 4, 16, D)

    def flat_views(ref):
        return [ref.reshape(2, D, D).at[group, :, lanes] for group, lanes, _, _ in PARTS]

    sum_flat, give_flat, got_flat = flat_views(m.grads), flat_views(m.tokens), flat_views(m.part)
    cubes = []
    buffers = (m.landing, m.landing, m.landing_left, m.landing_right)
    for (group, lanes, _, order), buffer in zip(PARTS, buffers):
        room = lanes if buffer is m.landing else pl.ds(0, lanes.size)
        lands = iter(cube_landings(buffer, room, order))

        def make(me, to, block, split, fine, lands=lands):
            return RingReduce(copies, me, to, block, split, next(lands), fine)

        cubes.append(cube_rings(spot, order, sum_blocks.at[group, :, :, :, :, lanes], make))
    save = local_copies(save_sem)
    saves = []

    m.sums[...] = jnp.zeros_like(m.sums)
    narrow = m.normed_two

    @pl.loop(0, 8)
    def _(n):
        line = pl.ds(pl.multiple_of(n * 32, 32), 32)
        tokens = m.hidden[line, :]
        inverse = lax.rsqrt(jnp.mean(tokens * tokens, axis=-1, keepdims=True) + epsilon_norm)
        scaled = tokens * inverse
        upstream = grad_hidden[line, :]
        m.sums[1:2, :] += jnp.sum(upstream * scaled, axis=0, keepdims=True)
        weighted = upstream * m.rows[1:2, :]
        total = m.grads[z, core, line, :].astype(F32) + inverse * (
            weighted - scaled * jnp.mean(weighted * scaled, axis=-1, keepdims=True)
        )
        grad_hidden[line, :] = total
        narrow[line, :] = total.astype(BF)

    before = m.normed.at[0:ROWS]
    grad_bc = m.grad_value.reshape(8, ROWS, 2 * SLICE)
    given_parts = {}

    def gradient(part, give):
        half = 1 - core if give else core
        target = (give_flat if give else sum_flat)[part]
        left = m.mixer_in if part == 0 else before
        right = (
            lambda: narrow[:, half_lanes(half)],
            lambda: grad_bc[6 + half, :, 0:HALF],
            lambda: grad_bc[6 + half, :, HALF:D],
            lambda: m.grad_x[half],
        )[part]

        @pl.loop(0, 4)
        def _(n):
            columns = pl.ds(pl.multiple_of(n * 256, 256), 256)
            target[columns, :] = dot(left[:, columns], right(), TN).astype(BF)

        if give:
            given_parts[part] = copies.start(target, got_flat[part], partner)

    def pass_to_cube(part):
        given_parts[part].wait_recv()
        accumulate(sum_flat[part], sum_flat[part], got_flat[part])
        cubes[part][2].first()

    pl.semaphore_wait(ready.at[1], len(neighbours))
    gradient(0, True)
    grad_mixer[...] = dot(narrow[:, :HALF], weights[0][:, :HALF], NT) + dot(narrow[:, HALF:], weights[1][:, :HALF], NT)
    for q in range(2):
        for half in range(2):
            lanes = slice(HALF * half, HALF * half + HALF)
            start = slice(128 * q, 128 * q + 8)
            m.edge_send[q, :, lanes] = grad_mixer[start, lanes] * m.projected[half, start, HALF:1024]
    edge_copy = copies.start(m.edge_send, m.edge_got, (y * SIDE + x, wrap(seq - 1, PEERS)))
    gradient(0, False)
    fed.two()
    for half in range(2):
        lanes = slice(HALF * half, HALF * half + HALF)
        for q in range(2):
            main = slice(128 * q, 128 * q + 128)
            extend(m.extended, m.projected, half, q)
            upstream = grad_mixer[main, lanes]
            grad_bc[6 + half, main, HALF:D] = (upstream * convolve(m.extended, m.rows[2:5, lanes])).astype(BF)
            m.grad_conv[q, 0:128, lanes] = upstream * m.projected[half, main, HALF:1024]
    gradient(2, True)
    pass_to_cube(0)
    edge_copy.wait_recv()
    inside = (seq < PEERS - 1).astype(F32)
    for q in range(2):
        m.grad_conv[q, 128:136, :] = m.edge_got[q] * inside
        main = slice(128 * q, 128 * q + 128)
        for half in range(2):
            lanes = slice(HALF * half, HALF * half + HALF)
            taps = m.rows[2:5, lanes]
            gated = (
                taps[2:3] * m.grad_conv[q, 0:128, lanes]
                + taps[1:2] * m.grad_conv[q, 1:129, lanes]
                + taps[0:1] * m.grad_conv[q, 2:130, lanes]
            )
            grad_bc[6 + half, main, 0:HALF] = (gated * m.projected[half, main, 1024:]).astype(BF)
            m.grad_x[half, main, :] = (gated * m.projected[half, main, :HALF]).astype(BF)
    gradient(1, True)
    gradient(3, True)
    gradient(2, False)
    pass_to_cube(2)
    downs.two()
    ring.second()
    gradient(1, False)
    pass_to_cube(1)
    gradient(3, False)
    pass_to_cube(3)
    for half in range(2):
        lanes = slice(HALF * half, HALF * half + HALF)
        for q in range(2):
            extend(m.extended, m.projected, half, q)
            back = m.grad_conv[q, 0:128, lanes]
            for k in range(3):
                m.sums[2 + k : 3 + k, lanes] += jnp.sum(back * m.extended[6 + k : 134 + k, :], axis=0, keepdims=True)
    fed.three()
    downs.three()

    grad_mixer[...] = dot(grad_bc[6, :, 0:D], weights[0][:, HALF:1536], NT)
    grad_mixer[...] += dot(grad_bc[7, :, 0:D], weights[1][:, HALF:1536], NT)
    grad_mixer[...] += dot(m.grad_x[0], weights[0][:, 1536:], NT) + dot(m.grad_x[1], weights[1][:, 1536:], NT)

    @pl.loop(0, 8)
    def _(n):
        line = pl.ds(pl.multiple_of(n * 32, 32), 32)
        tokens = m.inputs.reshape(ROWS, D)[line, :].astype(F32)
        inverse = lax.rsqrt(jnp.mean(tokens * tokens, axis=-1, keepdims=True) + epsilon_norm)
        scaled = tokens * inverse
        upstream = grad_mixer[line, :]
        m.sums[0:1, :] += jnp.sum(upstream * scaled, axis=0, keepdims=True)
        weighted = upstream * m.rows[0:1, :]
        grad_mixer[line, :] = grad_hidden[line, :] + inverse * (
            weighted - scaled * jnp.mean(weighted * scaled, axis=-1, keepdims=True)
        )

    for q in range(2):
        saves.append(save(grad_mixer.at[128 * q : 128 * q + 128], result.input_grad.at[q]))

    for part in (0, 2, 1, 3):
        cubes[part][2].second()
    fed.four()
    downs.four()

    for d in range(16):
        tile = jnp.concatenate([m.sums[:, 64 * d : 64 * d + 64], jnp.zeros((8, 64), F32)], axis=1)
        m.small[d // 4, d % 4] = tile
    sent_y = [
        copies.start(m.small.at[wrap(y + k)], m.small_y.at[k], device) for k, device in zip(range(1, SIDE), along)
    ]
    for copy in sent_y:
        copy.wait_recv()
    for i in range(SIDE):
        total = m.small[y, i]
        for k in range(1, SIDE):
            total = total + m.small_y[k, i]
        m.small_one[i] = total
    sent_x = [
        copies.start(m.small_one.at[wrap(x + k)], m.small_x.at[k], device)
        for k, device in zip(range(1, SIDE), across)
    ]
    for part in (0, 2, 1, 3):
        cubes[part][2].finish()
        cubes[part][1].first()
    fed.finish(m.feed_wide)
    sent_feed = []
    for k, peer in enumerate(peers):
        line = pl.ds(pl.multiple_of(wrap(seq + k + 1, PEERS) * 8, 8), 8)
        sent_feed.append(copies.start(m.feed_wide.at[line], m.feed_land.at[seq], peer))
    m.feed_land[seq] = m.feed_wide[pl.ds(pl.multiple_of(seq * 8, 8), 8), :]
    downs.finish(m.down_wide)
    m.w_down[0:16, :] = m.down_wide[:, 0:1024]
    m.w_down[16:32, :] = m.down_wide[:, 1024:2048]
    for i in range(4):
        m.w_down[32:36, 256 * i : 256 * i + 256] = m.down_wide[4 * i : 4 * i + 4, 2048:PACKED]
    saves.append(save(m.w_down, result.g_down))
    for copy in sent_x:
        copy.wait_recv()
    total = m.small_one[x]
    for k in range(1, SIDE):
        total = total + m.small_x[k]
    m.small_two[...] = total
    sent_z = [copies.start(m.small_two, m.small_z.at[seq], peer) for peer in peers]
    m.small_z[seq] = total
    for part in (0, 2, 1, 3):
        cubes[part][1].second()
    for copy in sent_z:
        copy.wait_recv()
    m.g_small[...] = functools.reduce(lambda a, b: a + b, [m.small_z[s] for s in range(PEERS)])
    saves.append(save(m.g_small, result.g_small))
    for copy in sent_feed:
        copy.wait_recv()
    def spread(main, tail, target, output):
        for d in range(16):
            pieces = []
            for s in range(PEERS):
                line = m.feed_land[s]
                whole = jnp.concatenate([line[:, main : main + WIDE], line[:, tail : tail + 64]], axis=1)
                pieces.append(whole[:, OWN * d : OWN * d + OWN])
            target[:, 288 * d : 288 * d + 288] = jnp.concatenate(pieces, axis=1)
        saves.append(save(target, output))

    for part in (0, 2, 1, 3):
        cubes[part][1].finish()
        cubes[part][0].first()
    spread(0, 1024, m.w_gate, result.g_gate)
    for part in (0, 2, 1, 3):
        cubes[part][0].second()
    spread(WIDE, 1088, m.w_up, result.g_up)
    for part, (_, lanes, start, _) in enumerate(PARTS):
        cubes[part][0].finish(m.mix_wide.at[:, pl.ds(start, lanes.size)])
    theirs = pl.ds(pl.multiple_of((1 - core) * 8, 8), 8)
    mix_copy = copies.start(m.mix_wide.at[theirs], m.mix_land.at[core], partner)
    m.mix_land[core] = m.mix_wide[pl.ds(pl.multiple_of(core * 8, 8), 8), :]
    ring.finish(grad_hidden)
    m.mixer_in[...] = (m.hidden[...] + grad_hidden[...]).astype(BF)
    for q in range(2):
        saves.append(save(m.mixer_in.at[128 * q : 128 * q + 128], result.output.at[q]))
    mix_copy.wait_recv()
    for half in range(2):
        for k in range(3):
            m.w_in[:, 1024 * k + 512 * half : 1024 * k + 512 * half + 512] = m.mix_land[
                half, :, 512 * k + 512 : 512 * k + 1024
            ]
        m.w_out[:, 512 * half : 512 * half + 512] = m.mix_land[half, :, 0:512]
    saves.append(save(m.w_in, result.g_in))
    saves.append(save(m.w_out, result.g_out))
    for copy in saves:
        copy.wait()
    copies.drain()


def step(*operands):
    hbm, vmem = pl.BlockSpec(memory_space=pl.ANY), pl.BlockSpec(memory_space=pltpu.VMEM)
    return pl.pallas_call(
        step_kernel,
        out_shape=tuple(jax.ShapeDtypeStruct(*shape) for shape in RESULTS.values()),
        in_specs=[vmem if name in ("gains", "taps") else hbm for name in OPERANDS],
        out_specs=(hbm,) * len(RESULTS),
        scratch_shapes=[pltpu.VMEM(*shape) for shape in SCRATCH.values()]
        + [
            pltpu.SemaphoreType.REGULAR((2,)),
            pltpu.SemaphoreType.DMA((7,)),
            pltpu.SemaphoreType.DMA((10,)),
            pltpu.SemaphoreType.DMA((COPIES,)),
            pltpu.SemaphoreType.DMA((COPIES,)),
        ],
        compiler_params=pltpu.CompilerParams(
            collective_id=0, has_side_effects=True, vmem_limit_bytes=VMEM_BYTES
        ),
        name="step",
    )(*operands)


SHAPES = ((2, 8), (3, 8), (8, 3072), (8, 1024), (8, 4608), (8, 4608), (OWN, D))
RATES = ((rate_small, 0.0),) * 2 + ((rate_matrix, weight_decay),) * 5
TILED = 5


def adamw(weight, grad, first, second, rate, decay):
    first_new = beta_one * first + (1.0 - beta_one) * grad
    second_new = beta_two * second + (1.0 - beta_two) * grad * grad
    first_hat = first_new / (1.0 - beta_one**STEP)
    second_hat = second_new / (1.0 - beta_two**STEP)
    weight_new = weight - rate * (
        first_hat / (jnp.sqrt(second_hat) + epsilon_adam) + decay * weight
    )
    return (weight_new, first_new, second_new)


def adamw_kernel(*refs):
    weights, firsts, seconds, refs = refs[:7], refs[7:14], refs[14:21], refs[21:]
    small_grad, grads, finished, refs = refs[0], refs[1:6], refs[6:8], refs[8:]
    outs, final, refs = (refs[:7], refs[7:14], refs[14:21]), refs[21:23], refs[23:]
    held = [refs[5 * k : 5 * k + 5] for k in range(4)]
    through, (load_sem, save_sem) = refs[20:22], refs[22:]
    load, save = local_copies(load_sem), local_copies(save_sem)
    passing = [load(source, kept) for source, kept in zip(finished, through)]
    loads = []
    for index in range(TILED):
        sources = (grads[index], weights[index + 2], firsts[index + 2], seconds[index + 2])
        loads.append([load(source, kept[index]) for source, kept in zip(sources, held)])
    seq = lax.axis_index("seq")
    tile = pltpu.roll(small_grad[...], lax.rem(128 - seq * 8, 128), 1)
    for index, (start, count) in enumerate(((0, 2), (2, 3))):
        grad = tile[start : start + count, 0:8]
        new = adamw(weights[index][...], grad, firsts[index][...], seconds[index][...], *RATES[index])
        for out, value in zip(outs, new):
            out[index][...] = value
    saves = []
    for copy, kept, target in zip(passing, through, final):
        copy.wait()
        saves.append(save(kept, target))
    for index in range(TILED):
        for copy in loads[index]:
            copy.wait()
        grad, weight, first, second = (kept[index] for kept in held)
        rows, columns = weight.shape
        for start in range(0, columns, 512):
            lanes = slice(start, min(start + 512, columns))
            new = adamw(weight[:, lanes], grad[:, lanes], first[:, lanes], second[:, lanes], *RATES[index + 2])
            weight[:, lanes], first[:, lanes], second[:, lanes] = new
        for out, kept in zip(outs, (weight, first, second)):
            saves.append(save(kept, out[index + 2]))
    for copy in saves:
        copy.wait()


def adamw_all(weights, firsts, seconds, small_grad, grads, finished):
    hbm, vmem = pl.BlockSpec(memory_space=pl.ANY), pl.BlockSpec(memory_space=pltpu.VMEM)
    group = [vmem] * 2 + [hbm] * TILED
    return pl.pallas_call(
        adamw_kernel,
        out_shape=[jax.ShapeDtypeStruct(shape, F32) for shape in SHAPES] * 3
        + [jax.ShapeDtypeStruct(array.shape, array.dtype) for array in finished],
        in_specs=group * 3 + [vmem] + [hbm] * (TILED + 2),
        out_specs=group * 3 + [hbm] * 2,
        scratch_shapes=[pltpu.VMEM(shape, F32) for shape in SHAPES[2:]] * 4
        + [pltpu.VMEM(array.shape, array.dtype) for array in finished]
        + [pltpu.SemaphoreType.DMA((4 * TILED + 2,)), pltpu.SemaphoreType.DMA((3 * TILED + 2,))],
        compiler_params=pltpu.CompilerParams(vmem_limit_bytes=VMEM_BYTES),
        name="adamw",
    )(*weights, *firsts, *seconds, small_grad, *grads, *finished)


def shards(
    inputs, cotangent, norm_gains, conv_taps, w_in, w_out, w_gate, w_up, w_down,
    first_gains, first_taps, first_in, first_out, first_gate, first_up, first_down,
    second_gains, second_taps, second_in, second_out, second_gate, second_up, second_down,
):
    output, input_grad, red_in, red_out, red_gate, red_up, red_down, red_small = step(
        w_in, w_out, w_gate, w_up, w_down, norm_gains, conv_taps, inputs, cotangent.reshape(ROWS, D)
    )
    *new, output, input_grad = adamw_all(
        (norm_gains, conv_taps, w_in, w_out, w_gate, w_up, w_down),
        (first_gains, first_taps, first_in, first_out, first_gate, first_up, first_down),
        (second_gains, second_taps, second_in, second_out, second_gate, second_up, second_down),
        red_small,
        (red_in, red_out, red_gate, red_up, red_down),
        (output, input_grad),
    )
    return (output, input_grad, *new)


def solution(mesh):
    tokens, columns, rows = P("dp", "seq", None), P(None, ("dp", "seq")), P(("dp", "seq"), None)
    weights = (columns, columns, rows, rows, rows, rows, rows)
    return jax.shard_map(
        shards,
        mesh=mesh,
        in_specs=(tokens, tokens) + weights * 3,
        out_specs=(tokens, tokens) + weights * 3,
        check_vma=False,
    )
```
